128 devices in a mesh: gx: 8 (over x, core), gy: 16 (over y, z).
Axes of the slice: x: 4, y: 4, z: 4, core: 2. Of those that a mesh axis runs over, the one named last changes fastest.
Arguments:
- right_side: float32 [216, 65536], P(None, ('gx', 'gy')), may hold values from -15 to 15
- stiffness: float32 [3, 216, 216], replicated, may hold values from -6.5 to 8, as said below
- metric: float32 [3, 65536], P(None, ('gx', 'gy')), may hold values from 0.2 to 2
- levels: int32 [65536], P(('gx', 'gy')), may hold values from 0 to 2
- projection: float32 [4, 36, 36], replicated, may hold values from -1 to 1
- mortar_fine: int32 [65536], P(('gx', 'gy')), may hold values from 0 to 511, as said below
- mortar_face: int32 [65536], P(('gx', 'gy')), may hold values from 0 to 5
- mortar_owner: int32 [65536, 1], P(('gx', 'gy')), may hold values from 0 to 127, as said below
- mortar_subface: int32 [65536], P(('gx', 'gy')), may hold values from 0 to 3
- mortar_coarse: int32 [65536], P(('gx', 'gy')), may hold values from 0 to 511, as said below
- mortar_cface: int32 [65536], P(('gx', 'gy')), may hold values from 0 to 5
Outputs:
- solution_field: float32 [216, 65536], P(None, ('gx', 'gy'))
- residual: float32 [216, 65536], P(None, ('gx', 'gy'))
The draws below stay inside these ranges and needn't reach their ends.
Inputs may be any that keep to these rules, and one draw needn't show every extreme that they name: `stiffness`: symmetric; positive definite. `mortar_owner`: A device index in mesh order: the device that holds the fine element or one of its neighbours in the grid of devices, diagonal ones included. Exactly 128 of one device's 512 faces name that device itself, at most 128 name any one neighbour, and each neighbour of a corner device is named exactly 128 times by it. `mortar_fine`: where the owner is another device, an element on the edge of the block that faces the owner: a = 0 or 3 toward a neighbour along the first direction, b = 0 or 127 along the second. `mortar_coarse`: where the owner is another device, the owner's element across that edge or corner from the fine element; where the owner is the device itself, any element.
All inputs are finite; a program needn't handle non-finite values.
Results may differ from the reference program's by a relative error of at most 0.0003.
Values sent between devices are 32-bit elements; how exact they have to be, the bound alone decides.
A program may use at most 64 MiB of HBM per device.

```python
import math
import jax
import jax.numpy as jnp
import numpy as np
from jax import lax

NP = 6
EA = 4
EB = 128
MORT_DEV = 512
ITERS = 2
ELEM_DEV = 512
ELEMS = 65536
MORTS = 65536
CAP = 128
N_GX = 8
N_GY = 16


def draw_right_side(key, part):
    key = jax.random.fold_in(key, 11)
    columns = jnp.arange(ELEMS, dtype=jnp.float32)
    scale = 1.0 + 2.0 * columns / ELEMS
    rough = jnp.clip(jax.random.normal(key, (NP * NP * NP, ELEMS), jnp.float32), -5.0, 5.0)
    return rough * scale[None, :]


def gll_tables():
    order = 5
    seven_root = math.sqrt(7.0)
    outer_node = math.sqrt((7.0 + 2.0 * seven_root) / 21.0)
    inner_node = math.sqrt((7.0 - 2.0 * seven_root) / 21.0)
    points = np.array([-1.0, -outer_node, -inner_node, inner_node, outer_node, 1.0])
    legendre = (63.0 * points ** 5 - 70.0 * points ** 3 + 15.0 * points) / 8.0
    weights = 2.0 / (order * (order + 1) * legendre ** 2)
    derivative = np.zeros((6, 6))
    for row_index in range(6):
        for col_index in range(6):
            if row_index != col_index:
                derivative[row_index, col_index] = legendre[row_index] / legendre[col_index] / (points[row_index] - points[col_index])
    derivative[0, 0] = -order * (order + 1) / 4.0
    derivative[5, 5] = order * (order + 1) / 4.0
    line_matrix = derivative.T * weights[None, :] @ derivative
    line_matrix = line_matrix * (2.5 / np.max(np.abs(line_matrix)))
    identity_six = np.eye(6)
    tables = np.stack([np.kron(line_matrix, np.eye(36)), np.kron(np.kron(identity_six, line_matrix), identity_six), np.kron(np.eye(36), line_matrix)])
    return jnp.asarray(tables, jnp.float32)


def draw_stiffness(key, part):
    key = jax.random.fold_in(key, 23)
    nodes = NP * NP * NP
    first, second, third = jax.random.split(key, 3)
    tables = gll_tables()
    gains = jnp.exp(jax.random.uniform(first, (3, nodes), jnp.float32, math.log(0.6), math.log(1.6)))
    spread = 0.004 * jnp.clip(0.5 * jax.random.normal(second, (3, nodes, nodes), jnp.float32), -1.0, 1.0)
    mirrored = 0.5 * (spread + jnp.swapaxes(spread, 1, 2))
    shifts = jax.random.uniform(third, (3, nodes), jnp.float32, 0.9, 1.4)
    identity = (jnp.arange(nodes)[:, None] == jnp.arange(nodes)[None, :]).astype(jnp.float32)
    return gains[:, :, None] * tables * gains[:, None, :] + mirrored + identity[None] * shifts[:, :, None]


def mortar_layout(key):
    devices = N_GX * N_GY
    codes = jnp.array([0, 1, 2, 3, 5, 6, 7, 8], jnp.int32)
    slots = 8 * CAP
    slot_code = jnp.arange(slots, dtype=jnp.int32) // CAP

    def one_device(device):
        device_key = jax.random.fold_in(jax.random.fold_in(key, 101), device)
        first, second, third, fourth = jax.random.split(device_key, 4)
        target_x = device // N_GY + codes // 3 - 1
        target_y = device % N_GY + codes % 3 - 1
        usable = (target_x >= 0) & (target_x < N_GX) & (target_y >= 0) & (target_y < N_GY)
        ranks = jax.random.permutation(first, slots).astype(jnp.int32)
        score = ranks + jnp.where(usable[slot_code], 0, slots).astype(jnp.int32)
        order = jnp.argsort(score)
        picked = codes[slot_code[order[:3 * CAP]]]
        directions = jnp.concatenate([jnp.full((CAP,), 4, jnp.int32), picked])
        directions = jax.random.permutation(second, directions)
        spot_a = jax.random.randint(third, (MORT_DEV,), 0, EA)
        spot_b = jax.random.randint(fourth, (MORT_DEV,), 0, EB)
        return (directions, spot_a, spot_b)
    return jax.vmap(one_device)(jnp.arange(devices, dtype=jnp.int32))


def draw_mortar_owner(key, part):
    directions, spot_a, spot_b = mortar_layout(key)
    devices = jnp.arange(N_GX * N_GY, dtype=jnp.int32)[:, None]
    owner = (devices // N_GY + directions // 3 - 1) * N_GY + devices % N_GY + directions % 3 - 1
    return owner.reshape(MORTS, 1)


def draw_mortar_fine(key, part):
    directions, spot_a, spot_b = mortar_layout(key)
    step_x = directions // 3 - 1
    step_y = directions % 3 - 1
    place_a = jnp.where(step_x < 0, 0, jnp.where(step_x > 0, EA - 1, spot_a))
    place_b = jnp.where(step_y < 0, 0, jnp.where(step_y > 0, EB - 1, spot_b))
    return (place_a * EB + place_b).reshape(MORTS)


def draw_mortar_coarse(key, part):
    directions, spot_a, spot_b = mortar_layout(key)
    key = jax.random.fold_in(key, 37)
    anywhere = jax.random.randint(key, (N_GX * N_GY, MORT_DEV), 0, ELEM_DEV)
    step_x = directions // 3 - 1
    step_y = directions % 3 - 1
    place_a = jnp.where(step_x < 0, EA - 1, jnp.where(step_x > 0, 0, spot_a))
    place_b = jnp.where(step_y < 0, EB - 1, jnp.where(step_y > 0, 0, spot_b))
    return jnp.where(directions == 4, anywhere, place_a * EB + place_b).reshape(MORTS)


def place_ends(entries, key, least, top_value):
    longest = entries.shape.index(max(entries.shape))
    spots = []
    for shift in (0, 1):
        where = [jax.random.randint(jax.random.fold_in(key, axis), (), 0, length) for axis, length in enumerate(entries.shape)]
        where[longest] = (where[longest] + shift) % entries.shape[longest]
        spots.append(tuple(where))
    return entries.at[spots[0]].set(least).at[spots[1]].set(top_value)


def block_levels(own_key, dims, pieces, low, high):
    def one(position, blocks):
        draws = jax.random.uniform(jax.random.fold_in(jax.random.fold_in(own_key, 6), position), (blocks,), jnp.float32, low / len(pieces), high / len(pieces))
        return jnp.repeat(jnp.exp(draws), dims[position] // blocks).reshape((-1,) + (1,) * (len(dims) - position - 1))

    loudness = one(*pieces[0])
    for cut in pieces[1:]:
        loudness = loudness * one(*cut)
    return loudness


def centred(rng, dims, width, limit, held_as=jnp.bfloat16):
    entries = width * jax.random.normal(rng, dims, jnp.float32)
    return jnp.clip(entries, min=-limit, max=limit).astype(held_as)


def setup_inputs(seed: int = 0) -> dict:
    key_list = jax.random.split(jax.random.key(seed), 12)
    right_side = draw_right_side(jax.random.fold_in(key_list[11], 71), 0)
    stiffness = draw_stiffness(jax.random.fold_in(key_list[11], 71), 0)
    metric = jnp.clip(jnp.exp(math.log(2.0) - 2.3025851 * jax.random.uniform(key_list[2], (3, ELEMS), jnp.float32) ** block_levels(key_list[2], (3, ELEMS), ((1, 128),), -0.2, 0.2)), 0.2, 2.0)
    levels = place_ends(jax.random.randint(key_list[3], (ELEMS,), 0, 3), jax.random.fold_in(key_list[3], 1), 0, 2).astype(jnp.int32)
    projection = centred(key_list[4], (4, NP * NP, NP * NP), (NP * NP) ** -0.5, 1.0, jnp.float32)
    mortar_fine = draw_mortar_fine(jax.random.fold_in(key_list[11], 71), 0)
    mortar_face = place_ends(jax.random.randint(key_list[6], (MORTS,), 0, 6), jax.random.fold_in(key_list[6], 1), 0, 5).astype(jnp.int32)
    mortar_owner = draw_mortar_owner(jax.random.fold_in(key_list[11], 71), 0)
    mortar_subface = place_ends(jax.random.randint(key_list[8], (MORTS,), 0, 4), jax.random.fold_in(key_list[8], 1), 0, 3).astype(jnp.int32)
    mortar_coarse = draw_mortar_coarse(jax.random.fold_in(key_list[11], 71), 0)
    mortar_cface = place_ends(jax.random.randint(key_list[10], (MORTS,), 0, 6), jax.random.fold_in(key_list[10], 1), 0, 5).astype(jnp.int32)
    return {"right_side": right_side, "stiffness": stiffness, "metric": metric, "levels": levels, "projection": projection, "mortar_fine": mortar_fine, "mortar_face": mortar_face, "mortar_owner": mortar_owner, "mortar_subface": mortar_subface, "mortar_coarse": mortar_coarse, "mortar_cface": mortar_cface}


PENALTY = 1.0
HIGH = lax.Precision.HIGHEST


def face_values(columns, face):
    count = columns.shape[1]
    cube = columns.reshape(NP, NP, NP, count)
    sides = jnp.stack([cube[0], cube[NP - 1], cube[:, 0], cube[:, NP - 1], cube[:, :, 0], cube[:, :, NP - 1]])
    sides = sides.reshape(6, NP * NP, count)
    choose = (face[None, :] == jnp.arange(6, dtype=jnp.int32)[:, None]).astype(columns.dtype)
    return jnp.sum(sides * choose[:, None, :], axis=0)


def face_spread(values, face):
    count = values.shape[1]
    choose = (face[None, :] == jnp.arange(6, dtype=jnp.int32)[:, None]).astype(values.dtype)
    parts = (values[None] * choose[:, None, :]).reshape(6, NP, NP, count)
    cube = jnp.zeros((NP, NP, NP, count), values.dtype)
    cube = cube.at[0].add(parts[0]).at[NP - 1].add(parts[1])
    cube = cube.at[:, 0].add(parts[2]).at[:, NP - 1].add(parts[3])
    cube = cube.at[:, :, 0].add(parts[4]).at[:, :, NP - 1].add(parts[5])
    return cube.reshape(NP * NP * NP, count)


def mortar_terms(coarse, fine, subface, projection):
    choose = (subface[None, :] == jnp.arange(4, dtype=jnp.int32)[:, None]).astype(coarse.dtype)
    images = jnp.einsum("sij,jn->sin", projection, coarse, precision=HIGH)
    jump = jnp.sum(images * choose[:, None, :], axis=0) - fine
    backs = jnp.einsum("sji,jn->sin", projection, jump, precision=HIGH)
    return jump, jnp.sum(backs * choose[:, None, :], axis=0)


def element_apply(field, stiffness, metric, levels):
    nodes = NP * NP * NP
    stacked = jnp.dot(stiffness.reshape(3 * nodes, nodes), field, precision=HIGH).reshape(3, nodes, field.shape[1])
    total = field + metric[0] * stacked[0] + metric[1] * stacked[1] + metric[2] * stacked[2]
    return (0.5 ** levels.astype(jnp.float32)) * total


def conforming(field):
    nodes = NP * NP * NP
    grid = field.reshape(nodes, N_GX, N_GY, EA, EB).transpose(0, 1, 3, 2, 4)
    grid = grid.reshape(NP, NP, NP, N_GX * EA, N_GY * EB)
    x_low = grid[0]
    x_high = grid[NP - 1]
    y_low = grid[:, 0]
    y_high = grid[:, NP - 1]
    zero_x = jnp.zeros_like(x_low[:, :, :1])
    zero_y = jnp.zeros_like(y_low[:, :, :, :1])
    left = jnp.concatenate([zero_x, x_high[:, :, :-1]], axis=2)
    right = jnp.concatenate([x_low[:, :, 1:], zero_x], axis=2)
    below = jnp.concatenate([zero_y, y_high[:, :, :, :-1]], axis=3)
    above = jnp.concatenate([y_low[:, :, :, 1:], zero_y], axis=3)
    result = jnp.zeros_like(grid)
    result = result.at[0].add(PENALTY * (x_low - left)).at[NP - 1].add(PENALTY * (x_high - right))
    result = result.at[:, 0].add(PENALTY * (y_low - below)).at[:, NP - 1].add(PENALTY * (y_high - above))
    result = result.reshape(nodes, N_GX, EA, N_GY, EB).transpose(0, 1, 3, 2, 4)
    return result.reshape(nodes, ELEMS)


def reference(right_side, stiffness, metric, levels, projection, mortar_fine, mortar_face, mortar_owner, mortar_subface, mortar_coarse, mortar_cface):
    nodes = NP * NP * NP
    blocks_total = N_GX * N_GY
    slot_device = jnp.arange(MORTS, dtype=jnp.int32) // MORT_DEV
    fine_global = slot_device * ELEM_DEV + mortar_fine
    coarse_global = mortar_owner[:, 0] * ELEM_DEV + mortar_coarse
    metric_blocks = metric.reshape(3, blocks_total, ELEM_DEV).transpose(1, 0, 2)
    level_blocks = levels.reshape(blocks_total, ELEM_DEV)

    def operate(field):
        field_blocks = field.reshape(nodes, blocks_total, ELEM_DEV).transpose(1, 0, 2)
        local = lax.map(lambda item: element_apply(item[0], stiffness, item[1], item[2]), (field_blocks, metric_blocks, level_blocks))
        image = local.transpose(1, 0, 2).reshape(nodes, ELEMS) + conforming(field)
        fine = face_values(field[:, fine_global], mortar_face)
        coarse = face_values(field[:, coarse_global], mortar_cface)
        jump, back = mortar_terms(coarse, fine, mortar_subface, projection)
        image = image.at[:, coarse_global].add(face_spread(PENALTY * back, mortar_cface))
        return image.at[:, fine_global].add(face_spread(-PENALTY * jump, mortar_face))

    solution_field = jnp.zeros_like(right_side)
    residual, direction = right_side, right_side
    norm_now = jnp.sum(residual * residual)
    for step in range(ITERS):
        image = operate(direction)
        alpha = norm_now / jnp.sum(direction * image)
        solution_field = solution_field + alpha * direction
        residual = residual - alpha * image
        norm_next = jnp.sum(residual * residual)
        direction = residual + (norm_next / norm_now) * direction
        norm_now = norm_next
    return solution_field, residual
```

```python
import functools

import jax
import jax.numpy as jnp
import numpy as np
from jax import lax
from jax.experimental import pallas as pl
from jax.experimental.pallas import tpu as pltpu
from jax.sharding import PartitionSpec as P

NP = 6
NODES = NP * NP * NP
SIDE = NP * NP
EA = 4
EB = 128
ELEMS = EA * EB
FR = 40
FACES = 6 * FR
PENALTY = 1.0

F32 = jnp.float32
BF16 = jnp.bfloat16
MESH = pl.DeviceIdType.MESH

DIRS = {d: (d // 3 - 1, d % 3 - 1) for d in range(9) if d != 4}
EDGE_DIRS = (3, 5, 0, 2, 6, 8)
EDGE_BASE = {3: 0, 5: 4, 0: 8, 2: 9, 6: 10, 8: 11}


def face_nodes(face):
    ids = np.arange(NODES).reshape(NP, NP, NP)
    return [ids[0], ids[5], ids[:, 0], ids[:, 5], ids[:, :, 0], ids[:, :, 5]][face].reshape(-1)


def constant_tables():
    pick = np.zeros((FACES, NODES), np.float32)
    for face in range(6):
        pick[face * FR + np.arange(SIDE), face_nodes(face)] = 1.0
    edge = np.zeros((ELEMS, 128), np.float32)
    columns = [a * EB for a in range(EA)] + [a * EB + EB - 1 for a in range(EA)]
    columns += [0, EB - 1, (EA - 1) * EB, ELEMS - 1]
    for face in range(6):
        for pair, column in enumerate(columns):
            edge[column, face * 16 + pair] = 1.0
    return pick, pick.T.copy(), edge


def dot(a, b):
    return lax.dot_general(a, b, (((1,), (0,)), ((), ())), preferred_element_type=F32)


def dot_nt(a, b):
    return lax.dot_general(a, b, (((1,), (1,)), ((), ())), preferred_element_type=F32)


def split(value):
    high = value.astype(BF16)
    return high, (value - high.astype(F32)).astype(BF16)


def iota(shape, dim):
    return lax.broadcasted_iota(jnp.int32, shape, dim)


def one_hot(rows, code):
    return jnp.where(iota((rows, code.shape[1]), 0).astype(F32) == code, 1.0, 0.0).astype(BF16)


def pick_face(sides, face):
    out = None
    for f in range(6):
        part = jnp.where(face == float(f), sides[f * FR : (f + 1) * FR], 0.0)
        out = part if out is None else out + part
    return out


def spread_face(values, face):
    return jnp.concatenate([jnp.where(face == float(f), values, 0.0) for f in range(6)], axis=0)


def spread_split(values, face):
    high = values.astype(BF16).astype(F32)
    return spread_face(high, face).astype(BF16), spread_face(values - high, face).astype(BF16)


def by_subface(values, sub):
    return jnp.concatenate([jnp.where(sub == float(s), values, 0.0) for s in range(4)], axis=0).astype(BF16)


def column_sums(a, b):
    prod = a * b
    rows = jnp.sum(prod, axis=0, keepdims=True)
    return sum(rows[:, t * EB : (t + 1) * EB] for t in range(EA))


def kernel(
    n_gx,
    n_gy,
    b_ref,
    stiff_ref,
    metric_ref,
    ints_ref,
    proj_ref,
    pick_ref,
    place_ref,
    edge_ref,
    x_ref,
    r_ref,
    fld,
    halo_x,
    halo_y,
    halo_m,
    own_m,
    own_y,
    stiff_h,
    stiff_l,
    oh_self,
    oh_x,
    n_out,
    n_in,
    proj_s,
    proj_c,
    proj_t,
    red1,
    red2,
    mine1,
    mine2,
    sx_send,
    sx_recv,
    sy_send,
    sy_recv,
    sm_send,
    sm_recv,
    s1_send,
    s1_recv,
    s2_send,
    s2_recv,
):
    gx = lax.axis_index("gx")
    gy = lax.axis_index("gy")

    def there(d):
        dx, dy = DIRS[d]
        ok = (gx + dx >= 0) & (gx + dx < n_gx) & (gy + dy >= 0) & (gy + dy < n_gy)
        return ok, {"gx": gx + dx, "gy": gy + dy}

    halo_x[...] = jnp.zeros_like(halo_x)
    halo_y[...] = jnp.zeros_like(halo_y)
    halo_m[...] = jnp.zeros_like(halo_m)

    barrier = pltpu.get_barrier_semaphore()
    for k in range(1, n_gx):
        pl.semaphore_signal(barrier, inc=1, device_id={"gx": lax.rem(gx + k, n_gx), "gy": gy}, device_id_type=MESH)
    for k in range(1, n_gy):
        pl.semaphore_signal(barrier, inc=1, device_id={"gx": gx, "gy": lax.rem(gy + k, n_gy)}, device_id_type=MESH)
    expected = jnp.int32(n_gx + n_gy - 2)
    for d in (0, 2, 6, 8):
        ok, where = there(d)

        @pl.when(ok)
        def _():
            pl.semaphore_signal(barrier, inc=1, device_id=where, device_id_type=MESH)

        expected = expected + ok.astype(jnp.int32)
    pl.semaphore_wait(barrier, expected)

    def x_copy(t, side, arriving):
        d = (1, 7)[side]
        tile = (0, EA - 1)[side]
        slot = side if arriving else 1 - side
        return pltpu.make_async_remote_copy(
            src_ref=fld.at[t, :, pl.ds(tile * EB, EB)],
            dst_ref=halo_x.at[t, slot],
            send_sem=sx_send.at[t, side],
            recv_sem=sx_recv.at[t, slot],
            device_id=there(d)[1],
            device_id_type=MESH,
        )

    def y_copy(t, index, arriving):
        d = EDGE_DIRS[index]
        slot = index if arriving else EDGE_DIRS.index(8 - d)
        return pltpu.make_async_remote_copy(
            src_ref=own_y.at[t],
            dst_ref=halo_y.at[t, slot],
            send_sem=sy_send.at[t, index],
            recv_sem=sy_recv.at[t, slot],
            device_id=there(d)[1],
            device_id_type=MESH,
        )

    def m_copy(d, arriving):
        slot = d if arriving else 8 - d
        return pltpu.make_async_remote_copy(
            src_ref=own_m.at[d],
            dst_ref=halo_m.at[slot],
            send_sem=sm_send.at[d],
            recv_sem=sm_recv.at[slot],
            device_id=there(d)[1],
            device_id_type=MESH,
        )

    def if_there(d, act):
        pl.when(there(d)[0])(act)

    def send_x(t):
        for side in range(2):
            if_there((1, 7)[side], lambda: x_copy(t, side, False).start())

    fld[0] = b_ref[...]
    send_x(0)

    fine = ints_ref[0:1, :]
    face = ints_ref[1:2, :]
    owner = ints_ref[2:3, :]
    sub = ints_ref[3:4, :]
    coarse = ints_ref[4:5, :]
    cface = ints_ref[5:6, :]
    level = ints_ref[6:7, :]
    shift = n_gy.bit_length() - 1
    slot = ((owner >> shift) - gx + 1) * 3 + (owner & (n_gy - 1)) - gy + 1
    count = fine.shape[1]
    hits = jnp.where(iota((16, count), 0) == slot, 1.0, 0.0)
    before = jnp.where(iota((count, count), 0) < iota((count, count), 1), 1.0, 0.0).astype(BF16)
    position = jnp.sum(hits * dot(hits.astype(BF16), before), axis=0, keepdims=True)
    row = iota((8, count), 0)
    facts = jnp.ones((8, count), jnp.int32)
    for index, entry in enumerate((fine >> 7, fine & 127, face, coarse >> 7, coarse & 127, cface, sub)):
        facts = jnp.where(row == index, entry, facts)
    facts = facts.astype(F32)
    stacked = jnp.concatenate([facts * hits[k : k + 1] for k in range(9)], axis=0).astype(BF16)
    packed = dot_nt(stacked, one_hot(EB, position))
    for k in range(9):
        own_m[k] = packed[8 * k : 8 * k + 8]
    for d in DIRS:
        if_there(d, lambda: m_copy(d, False).start())

    for d in range(3):
        high, low = split(stiff_ref[d])
        stiff_h[d] = high
        stiff_l[d] = low
    proj_s[...] = jnp.zeros_like(proj_s)
    for s in range(4):
        proj_s[s * FR : s * FR + SIDE, 0:SIDE] = proj_ref[s]
    stack = proj_s[...]
    flipped = stack.T
    proj_t[...] = flipped[0:FR]
    proj_c[...] = jnp.zeros_like(proj_c)
    for s in range(4):
        proj_c[0:SIDE, s * FR : s * FR + SIDE] = proj_ref[s]
    scale = jnp.where(level == 0, 1.0, jnp.where(level == 1, 0.5, 0.25))

    def code(entry, active):
        return jnp.where(active > 0.0, entry, -1.0)

    me = own_m[4]
    self_fine = code(me[0:1] * float(EB) + me[1:2], me[7:8])
    self_coarse = code(me[3:4] * float(EB) + me[4:5], me[7:8])
    oh_self[...] = one_hot(ELEMS, jnp.concatenate([self_fine, self_coarse], axis=1))

    def edge_codes(held):
        parts_f, parts_c = [], []
        for d in EDGE_DIRS:
            facts_d = held[d]
            pair = facts_d[0:1] + float(EDGE_BASE[d]) if d in (3, 5) else float(EDGE_BASE[d])
            parts_f.append(code(facts_d[2:3] * 16.0 + pair, facts_d[7:8]))
            parts_c.append(code(facts_d[6:7] * 128.0 + facts_d[5:6] * 16.0 + pair, facts_d[7:8]))
        return (
            one_hot(128, jnp.concatenate(parts_f, axis=1)),
            one_hot(512, jnp.concatenate(parts_c, axis=1)),
        )

    ones = jnp.ones((16, 6 * EB), BF16)
    edge_f, edge_c = edge_codes(own_m)
    n_out[...] = dot_nt(edge_f, edge_c).astype(BF16)
    sum_out = dot_nt(ones, edge_f)[0:1]

    lane = iota((1, 128), 1)
    lane_face = lane >> 4
    lane_pair = lane & 15

    proj_s_h, proj_s_l = split(proj_s[0 : 4 * FR, 0:FR])
    proj_c_h, proj_c_l = split(proj_c[:, 0 : 4 * FR])
    proj_t_h, proj_t_l = split(proj_t[:, 0 : 4 * FR])

    def by_table(high, low, value_h, value_l):
        return dot(high, value_h) + dot(low, value_h) + dot(high, value_l)

    state = {}

    def first_lists():
        for d in DIRS:
            if_there(d, lambda: m_copy(d, True).wait_recv())
        for side in range(2):
            d = (1, 7)[side]
            both = jnp.concatenate([own_m[d], halo_m[d]], axis=1)
            oh_x[side] = one_hot(EB, code(both[1:2], both[7:8]))
        edge_f_in, edge_c_in = edge_codes(halo_m)
        n_in[...] = dot_nt(edge_f_in, edge_c_in).astype(BF16)
        state["sum_in"] = dot_nt(ones, edge_c_in)[0:1]

    def apply(t):
        pick = pick_ref[...]
        field = fld[t]
        field_h, field_l = split(field)
        f_h = dot(pick, field_h)
        f_l = dot(pick, field_l)
        faces = f_h + f_l
        f_h = f_h.astype(BF16)
        f_l = f_l.astype(BF16)
        edges = dot(f_h, edge_ref[...]) + dot(f_l, edge_ref[...])
        own = None
        for f in range(6):
            part = jnp.where(lane_face == f, edges[f * FR : (f + 1) * FR], 0.0)
            own = part if own is None else own + part
        own_y[t] = own
        for index in range(6):
            if_there(EDGE_DIRS[index], lambda: y_copy(t, index, False).start())

        total = field
        for d in range(3):
            total = total + metric_ref[d : d + 1, :] * by_table(stiff_h[d], stiff_l[d], field_h, field_l)
        total = scale * total

        got = dot(f_h, oh_self[...]) + dot(f_l, oh_self[...])
        fines = [pick_face(got[:, 0:EB], me[2:3])]
        coarses = [pick_face(got[:, EB:], me[5:6])]

        for side in range(2):
            if_there((1, 7)[side], lambda: x_copy(t, side, True).wait_recv())
        for index in range(6):
            if_there(EDGE_DIRS[index], lambda: y_copy(t, index, True).wait_recv())
        if t == 0:
            first_lists()

        halo_faces = []
        for side in range(2):
            tile = (0, EA - 1)[side]
            d = (1, 7)[side]
            h_h, h_l = split(halo_x[t, side])
            h_h = dot(pick, h_h)
            h_l = dot(pick, h_l)
            halo_faces.append(h_h + h_l)
            here = slice(tile * EB, (tile + 1) * EB)
            rows = jnp.concatenate([f_h[:, here], h_h.astype(BF16)], axis=0)
            rows_l = jnp.concatenate([f_l[:, here], h_l.astype(BF16)], axis=0)
            got = dot(rows, oh_x[side]) + dot(rows_l, oh_x[side])
            ours, theirs = got[0:FACES], got[FACES:]
            fines.append(pick_face(ours[:, 0:EB], own_m[d][2:3]))
            coarses.append(pick_face(theirs[:, 0:EB], own_m[d][5:6]))
            fines.append(pick_face(theirs[:, EB:], halo_m[d][2:3]))
            coarses.append(pick_face(ours[:, EB:], halo_m[d][5:6]))
        subs = jnp.concatenate(
            [me[6:7], own_m[1][6:7], halo_m[1][6:7], own_m[7][6:7], halo_m[7][6:7]], axis=1
        )
        fines = jnp.concatenate(fines, axis=1)
        coarses = jnp.concatenate(coarses, axis=1)
        c_high = coarses.astype(BF16).astype(F32)
        jump = by_table(proj_c_h, proj_c_l, by_subface(c_high, subs), by_subface(coarses - c_high, subs)) - fines

        def block(k):
            return jump[:, k * EB : (k + 1) * EB]

        returned = jnp.concatenate([block(0), block(2), block(4)], axis=1)
        back_subs = jnp.concatenate([me[6:7], halo_m[1][6:7], halo_m[7][6:7]], axis=1)
        j_high = returned.astype(BF16).astype(F32)
        back = by_table(proj_t_h, proj_t_l, by_subface(j_high, back_subs), by_subface(returned - j_high, back_subs))

        own_terms = jnp.concatenate([-PENALTY * block(0), PENALTY * back[:, 0:EB]], axis=1)
        s_h, s_l = spread_split(own_terms, jnp.concatenate([me[2:3], me[5:6]], axis=1))
        gathered = dot_nt(s_h, oh_self[...]) + dot_nt(s_l, oh_self[...])

        side_terms = []
        for side in range(2):
            d = (1, 7)[side]
            terms = jnp.concatenate(
                [-PENALTY * block(1 + 2 * side), PENALTY * back[:, (1 + side) * EB : (2 + side) * EB]], axis=1
            )
            s_h, s_l = spread_split(terms, jnp.concatenate([own_m[d][2:3], halo_m[d][5:6]], axis=1))
            side_terms.append(dot_nt(s_h, oh_x[side]) + dot_nt(s_l, oh_x[side]))

        across = jnp.zeros((FR, 128), F32)
        for index, (d, turn, low, high) in enumerate(
            ((3, -4, 0, 4), (5, 4, 4, 8), (0, -3, 8, 9), (2, -1, 9, 10), (6, 1, 10, 11), (8, 3, 11, 12))
        ):
            moved = pltpu.roll(halo_y[t, index], turn % 128, 1)
            across = jnp.where((lane_pair >= low) & (lane_pair < high), moved, across)
        pairs = jnp.concatenate([own, across], axis=1)
        pairs_h, pairs_l = split(pairs)
        images = by_table(proj_s_h, proj_s_l, pairs_h, pairs_l)
        image_own = jnp.concatenate([images[s * FR : (s + 1) * FR, 0:128] for s in range(4)], axis=1)
        image_far = jnp.concatenate([images[s * FR : (s + 1) * FR, 128:] for s in range(4)], axis=1)
        far_h, far_l = split(image_far)
        on_fine = own * sum_out - dot_nt(far_h, n_out[...]) - dot_nt(far_l, n_out[...])
        jumps = image_own * state["sum_in"] - dot(pairs_h[:, 128:], n_in[...]) - dot(pairs_l[:, 128:], n_in[...])
        jumps = jnp.concatenate([jumps[:, s * 128 : (s + 1) * 128] for s in range(4)], axis=0)
        jumps_h, jumps_l = split(jumps)
        on_edge = PENALTY * (on_fine + by_table(proj_t_h, proj_t_l, jumps_h, jumps_l))
        from_low = pltpu.roll(across, 128 - 16, 1)
        from_high = pltpu.roll(across, 16, 1)
        on_edge = on_edge - PENALTY * jnp.where(
            (lane_face == 2) & (lane_pair < 4),
            from_low,
            jnp.where((lane_face == 3) & (lane_pair >= 4) & (lane_pair < 8), from_high, 0.0),
        )
        e_high = on_edge.astype(BF16).astype(F32)
        e_low = on_edge - e_high
        e_h = jnp.concatenate([jnp.where(lane_face == f, e_high, 0.0) for f in range(6)], axis=0).astype(BF16)
        e_l = jnp.concatenate([jnp.where(lane_face == f, e_low, 0.0) for f in range(6)], axis=0).astype(BF16)
        gathered = gathered + dot_nt(e_h, edge_ref[...]) + dot_nt(e_l, edge_ref[...])

        blocks = []
        for a in range(EA):
            here = slice(a * EB, (a + 1) * EB)
            x_low, x_high = faces[0:FR, here], faces[FR : 2 * FR, here]
            y_low, y_high = faces[2 * FR : 3 * FR, here], faces[3 * FR : 4 * FR, here]
            if a == 0:
                left = halo_faces[0][FR : 2 * FR]
            else:
                left = faces[FR : 2 * FR, (a - 1) * EB : a * EB]
            if a == EA - 1:
                right = halo_faces[1][0:FR]
            else:
                right = faces[0:FR, (a + 1) * EB : (a + 2) * EB]
            below = jnp.where(lane == 0, 0.0, pltpu.roll(y_high, 1, 1))
            above = jnp.where(lane == EB - 1, 0.0, pltpu.roll(y_low, EB - 1, 1))
            lateral = jnp.concatenate([x_low - left, x_high - right, y_low - below, y_high - above], axis=0)
            lateral = jnp.concatenate([PENALTY * lateral, jnp.zeros((2 * FR, EB), F32)], axis=0)
            lateral = lateral + gathered[:, here]
            if a == 0:
                lateral = lateral + side_terms[0]
            if a == EA - 1:
                lateral = lateral + side_terms[1]
            blocks.append(lateral)
        g_h, g_l = split(jnp.concatenate(blocks, axis=1))
        place = place_ref[...]
        return total + dot(place, g_h) + dot(place, g_l)

    b = b_ref[...]
    q = apply(0)
    fld[1] = q
    send_x(1)
    w = apply(1)
    q = fld[1]
    b = b_ref[...]

    row = iota((8, 128), 0)
    sums = jnp.zeros((8, 128), F32)
    for index, (left, right) in enumerate(((b, b), (b, q), (q, q), (b, w), (q, w))):
        sums = jnp.where(row == index, column_sums(left, right), sums)

    mine1[...] = sums

    def one_copy(k):
        return pltpu.make_async_remote_copy(
            src_ref=mine1,
            dst_ref=red1.at[k],
            send_sem=s1_send.at[k],
            recv_sem=s1_recv.at[k],
            device_id={"gx": lax.rem(gx + k, n_gx), "gy": gy},
            device_id_type=MESH,
        )

    def two_copy(k):
        return pltpu.make_async_remote_copy(
            src_ref=mine2,
            dst_ref=red2.at[k],
            send_sem=s2_send.at[k],
            recv_sem=s2_recv.at[k],
            device_id={"gx": gx, "gy": lax.rem(gy + k, n_gy)},
            device_id_type=MESH,
        )

    for k in range(1, n_gx):
        one_copy(k).start()
    total = mine1[...]
    for k in range(1, n_gx):
        one_copy(k).wait_recv()
        total = total + red1[k]
    mine2[...] = total
    for k in range(1, n_gy):
        two_copy(k).start()
    for k in range(1, n_gy):
        two_copy(k).wait_recv()
        total = total + red2[k]

    sums = jnp.sum(total, axis=1, keepdims=True)
    bb, bq, qq, bw, qw = (sums[i : i + 1] for i in range(5))
    alpha = bb / bq
    new = bb - 2.0 * alpha * bq + alpha * alpha * qq
    grow = 1.0 + new / bb
    alpha_next = new / (grow * grow * bq - grow * alpha * (bw + qq) + alpha * alpha * qw)
    first = alpha + alpha_next * grow
    second = alpha * alpha_next
    x_ref[...] = first * b - second * q
    r_ref[...] = b - first * q + second * w

    for t in range(2):
        for side in range(2):
            if_there((1, 7)[side], lambda: x_copy(t, side, False).wait_send())
        for index in range(6):
            if_there(EDGE_DIRS[index], lambda: y_copy(t, index, False).wait_send())
    for d in DIRS:
        if_there(d, lambda: m_copy(d, False).wait_send())
    for k in range(1, n_gx):
        one_copy(k).wait_send()
    for k in range(1, n_gy):
        two_copy(k).wait_send()


def body(
    n_gx,
    n_gy,
    right_side,
    stiffness,
    metric,
    levels,
    projection,
    mortar_fine,
    mortar_face,
    mortar_owner,
    mortar_subface,
    mortar_coarse,
    mortar_cface,
):
    ints = jnp.stack(
        [
            mortar_fine,
            mortar_face,
            mortar_owner[:, 0],
            mortar_subface,
            mortar_coarse,
            mortar_cface,
            levels,
            jnp.zeros_like(levels),
        ]
    )
    pick, place, edge = constant_tables()
    field = jax.ShapeDtypeStruct(right_side.shape, F32)
    vmem = pl.BlockSpec(memory_space=pltpu.VMEM)
    dma = pltpu.SemaphoreType.DMA
    return pl.pallas_call(
        functools.partial(kernel, n_gx, n_gy),
        out_shape=(field, field),
        in_specs=[vmem] * 8,
        out_specs=(vmem, vmem),
        scratch_shapes=[
            pltpu.VMEM((2, NODES, ELEMS), F32),
            pltpu.VMEM((2, 2, NODES, EB), F32),
            pltpu.VMEM((2, 6, FR, 128), F32),
            pltpu.VMEM((9, 8, 128), F32),
            pltpu.VMEM((9, 8, 128), F32),
            pltpu.VMEM((2, FR, 128), F32),
            pltpu.VMEM((3, NODES, NODES), BF16),
            pltpu.VMEM((3, NODES, NODES), BF16),
            pltpu.VMEM((ELEMS, 2 * EB), BF16),
            pltpu.VMEM((2, EB, 2 * EB), BF16),
            pltpu.VMEM((128, 512), BF16),
            pltpu.VMEM((128, 512), BF16),
            pltpu.VMEM((256, 128), F32),
            pltpu.VMEM((FR, 256), F32),
            pltpu.VMEM((FR, 256), F32),
            pltpu.VMEM((n_gx, 8, 128), F32),
            pltpu.VMEM((n_gy, 8, 128), F32),
            pltpu.VMEM((8, 128), F32),
            pltpu.VMEM((8, 128), F32),
            dma((2, 2)),
            dma((2, 2)),
            dma((2, 6)),
            dma((2, 6)),
            dma((9,)),
            dma((9,)),
            dma((n_gx,)),
            dma((n_gx,)),
            dma((n_gy,)),
            dma((n_gy,)),
        ],
        compiler_params=pltpu.CompilerParams(
            collective_id=0, has_side_effects=True, vmem_limit_bytes=48 * 1024 * 1024
        ),
    )(
        right_side,
        stiffness,
        metric,
        ints,
        projection,
        jnp.asarray(pick, BF16),
        jnp.asarray(place, BF16),
        jnp.asarray(edge, BF16),
    )


def solution(mesh):
    columns = P(None, ("gx", "gy"))
    faces = P(("gx", "gy"))
    in_specs = (columns, P(), columns, faces, P(), faces, faces, P(("gx", "gy"), None), faces, faces, faces)
    run = functools.partial(body, mesh.shape["gx"], mesh.shape["gy"])
    return jax.shard_map(run, mesh=mesh, in_specs=in_specs, out_specs=(columns, columns), check_vma=False)
```

```python
import functools

import jax
import jax.numpy as jnp
import numpy as np
from jax import lax
from jax.experimental import pallas as pl
from jax.experimental.pallas import tpu as pltpu
from jax.sharding import PartitionSpec as P

NP = 6
NODES = NP * NP * NP
SIDE = NP * NP
EA = 4
EB = 128
ELEMS = EA * EB
FR = 40
FACES = 6 * FR
PENALTY = 1.0

F32 = jnp.float32
BF16 = jnp.bfloat16
MESH = pl.DeviceIdType.MESH

DIRS = {d: (d // 3 - 1, d % 3 - 1) for d in range(9) if d != 4}
EDGE_DIRS = (3, 5, 0, 2, 6, 8)
EDGE_BASE = {3: 0, 5: 4, 0: 8, 2: 9, 6: 10, 8: 11}


def face_nodes(face):
    ids = np.arange(NODES).reshape(NP, NP, NP)
    return [ids[0], ids[5], ids[:, 0], ids[:, 5], ids[:, :, 0], ids[:, :, 5]][face].reshape(-1)


def constant_tables():
    pick = np.zeros((FACES, NODES), np.float32)
    for face in range(6):
        pick[face * FR + np.arange(SIDE), face_nodes(face)] = 1.0
    edge = np.zeros((ELEMS, 128), np.float32)
    columns = [a * EB for a in range(EA)] + [a * EB + EB - 1 for a in range(EA)]
    columns += [0, EB - 1, (EA - 1) * EB, ELEMS - 1]
    for face in range(6):
        for pair, column in enumerate(columns):
            edge[column, face * 16 + pair] = 1.0
    return pick, pick.T.copy(), edge


def dot(a, b):
    return lax.dot_general(a, b, (((1,), (0,)), ((), ())), preferred_element_type=F32)


def dot_nt(a, b):
    return lax.dot_general(a, b, (((1,), (1,)), ((), ())), preferred_element_type=F32)


def split(value):
    high = value.astype(BF16)
    return high, (value - high.astype(F32)).astype(BF16)


def iota(shape, dim):
    return lax.broadcasted_iota(jnp.int32, shape, dim)


def one_hot(rows, code):
    return jnp.where(iota((rows, code.shape[1]), 0).astype(F32) == code, 1.0, 0.0).astype(BF16)


def pick_face(sides, face):
    out = None
    for f in range(6):
        part = jnp.where(face == float(f), sides[f * FR : (f + 1) * FR], 0.0)
        out = part if out is None else out + part
    return out


def spread_face(values, face):
    return jnp.concatenate([jnp.where(face == float(f), values, 0.0) for f in range(6)], axis=0)


def spread_split(values, face):
    high = values.astype(BF16).astype(F32)
    return spread_face(high, face).astype(BF16), spread_face(values - high, face).astype(BF16)


def by_subface(values, sub):
    return jnp.concatenate([jnp.where(sub == float(s), values, 0.0) for s in range(4)], axis=0).astype(BF16)


def column_sums(a, b):
    prod = a * b
    rows = jnp.sum(prod, axis=0, keepdims=True)
    return sum(rows[:, t * EB : (t + 1) * EB] for t in range(EA))


def kernel(
    n_gx,
    n_gy,
    b_hbm,
    stiff_hbm,
    metric_hbm,
    fine_hbm,
    face_hbm,
    owner_hbm,
    sub_hbm,
    coarse_hbm,
    cface_hbm,
    level_hbm,
    proj_hbm,
    pick_hbm,
    place_hbm,
    edge_hbm,
    q_ref,
    w_ref,
    coef_ref,
    b_ref,
    stiff_ref,
    metric_ref,
    ints_ref,
    proj_ref,
    pick_ref,
    place_ref,
    edge_ref,
    halo_x,
    halo_y,
    halo_m,
    own_m,
    own_x,
    own_y,
    stiff_h,
    stiff_l,
    oh_self,
    oh_x,
    n_out,
    n_in,
    proj_s,
    proj_c,
    proj_t,
    red0,
    red1,
    mine0,
    mine1,
    in_sem,
    sx_send,
    sx_recv,
    sy_send,
    sy_recv,
    sm_send,
    sm_recv,
    s0_send,
    s0_recv,
    s1_send,
    s1_recv,
):
    gx = lax.axis_index("gx")
    gy = lax.axis_index("gy")

    def there(d):
        dx, dy = DIRS[d]
        ok = (gx + dx >= 0) & (gx + dx < n_gx) & (gy + dy >= 0) & (gy + dy < n_gy)
        return ok, {"gx": gx + dx, "gy": gy + dy}

    def if_there(d, act):
        pl.when(there(d)[0])(act)

    size_x, size_y, size_z = n_gx // 2, n_gy // 4, 4
    chips = [(i, j, k) for i in range(size_x) for j in range(size_y) for k in range(size_z)][1:]
    chips.sort(key=lambda c: -sum(min(v, n - v) for v, n in zip(c, (size_x, size_y, size_z))))

    def chip(offset):
        y, z = gy // size_z, lax.rem(gy, size_z)
        return {
            "gx": lax.rem(gx + 2 * offset[0], n_gx),
            "gy": lax.rem(y + offset[1], size_y) * size_z + lax.rem(z + offset[2], size_z),
        }

    halo_x[...] = jnp.zeros_like(halo_x)
    halo_y[...] = jnp.zeros_like(halo_y)
    halo_m[...] = jnp.zeros_like(halo_m)

    barrier = pltpu.get_barrier_semaphore()
    expected = jnp.int32(len(chips))
    for offset in chips:
        pl.semaphore_signal(barrier, inc=1, device_id=chip(offset), device_id_type=MESH)
    for d in (0, 2, 6, 8, 1, 7):
        ok, where = there(d)

        @pl.when(ok)
        def _():
            pl.semaphore_signal(barrier, inc=1, device_id=where, device_id_type=MESH)

        expected = expected + ok.astype(jnp.int32)

    int_names = (fine_hbm, face_hbm, owner_hbm, sub_hbm, coarse_hbm, cface_hbm, level_hbm)
    loads = [(source, ints_ref.at[k]) for k, source in enumerate(int_names)]
    loads += [(b_hbm, b_ref), (pick_hbm, pick_ref), (edge_hbm, edge_ref), (proj_hbm, proj_ref)]
    loads += [(stiff_hbm, stiff_ref), (metric_hbm, metric_ref), (place_hbm, place_ref)]
    loads = [pltpu.make_async_copy(source, target, in_sem.at[k]) for k, (source, target) in enumerate(loads)]
    for load in loads:
        load.start()

    def x_copy(t, side, arriving):
        slot = side if arriving else 1 - side
        return pltpu.make_async_remote_copy(
            src_ref=own_x.at[t, side],
            dst_ref=halo_x.at[t, slot],
            send_sem=sx_send.at[t, side],
            recv_sem=sx_recv.at[t, slot],
            device_id=there((1, 7)[side])[1],
            device_id_type=MESH,
        )

    def y_copy(t, index, arriving):
        d = EDGE_DIRS[index]
        slot = index if arriving else EDGE_DIRS.index(8 - d)
        return pltpu.make_async_remote_copy(
            src_ref=own_y.at[t],
            dst_ref=halo_y.at[t, slot],
            send_sem=sy_send.at[t, index],
            recv_sem=sy_recv.at[t, slot],
            device_id=there(d)[1],
            device_id_type=MESH,
        )

    def m_copy(d, arriving):
        slot = d if arriving else 8 - d
        return pltpu.make_async_remote_copy(
            src_ref=own_m.at[d],
            dst_ref=halo_m.at[slot],
            send_sem=sm_send.at[d],
            recv_sem=sm_recv.at[slot],
            device_id=there(d)[1],
            device_id_type=MESH,
        )

    lane = iota((1, 128), 1)
    lane_face = lane >> 4
    lane_pair = lane & 15

    def by_table(high, low, value_h, value_l):
        return dot(high, value_h) + dot(low, value_h) + dot(high, value_l)

    def code(entry, active):
        return jnp.where(active > 0.0, entry, -1.0)

    for load in loads[:7]:
        load.wait()
    fine, face, owner, sub, coarse, cface, level = (ints_ref[k] for k in range(7))
    shift = n_gy.bit_length() - 1
    slot = ((owner >> shift) - gx + 1) * 3 + (owner & (n_gy - 1)) - gy + 1
    count = fine.shape[1]
    hits = jnp.where(iota((16, count), 0) == slot, 1.0, 0.0)
    before = jnp.where(iota((count, count), 0) < iota((count, count), 1), 1.0, 0.0).astype(BF16)
    position = jnp.sum(hits * dot(hits.astype(BF16), before), axis=0, keepdims=True)
    row = iota((8, count), 0)
    facts = jnp.ones((8, count), jnp.int32)
    for index, entry in enumerate((fine >> 7, fine & 127, face, coarse >> 7, coarse & 127, cface, sub)):
        facts = jnp.where(row == index, entry, facts)
    facts = facts.astype(F32)
    stacked = jnp.concatenate([facts * hits[k : k + 1] for k in range(9)], axis=0).astype(BF16)
    packed = dot_nt(stacked, one_hot(EB, position))
    for k in range(9):
        own_m[k] = packed[8 * k : 8 * k + 8]
    scale = jnp.where(level == 0, 1.0, jnp.where(level == 1, 0.5, 0.25))

    def faces_of(t, field):
        pick = pick_ref[...]
        field_h, field_l = split(field)
        f_h = dot(pick, field_h)
        f_l = dot(pick, field_l)
        faces = f_h + f_l
        own_x[t, 0] = faces[:, 0:EB]
        own_x[t, 1] = faces[:, (EA - 1) * EB :]
        f_h = f_h.astype(BF16)
        f_l = f_l.astype(BF16)
        edges = dot(f_h, edge_ref[...]) + dot(f_l, edge_ref[...])
        own = None
        for f in range(6):
            part = jnp.where(lane_face == f, edges[f * FR : (f + 1) * FR], 0.0)
            own = part if own is None else own + part
        own_y[t] = own
        return field_h, field_l, f_h, f_l, faces, own

    def send(t):
        for index in (2, 3, 4, 5, 0, 1):
            if_there(EDGE_DIRS[index], lambda: y_copy(t, index, False).start())
        for side in range(2):
            if_there((1, 7)[side], lambda: x_copy(t, side, False).start())

    for load in loads[7:10]:
        load.wait()
    views = faces_of(0, b_ref[...])

    pl.semaphore_wait(barrier, expected)
    send(0)
    for d in (0, 2, 6, 8, 3, 5, 1, 7):
        if_there(d, lambda: m_copy(d, False).start())

    for load in loads[10:]:
        load.wait()
    for d in range(3):
        high, low = split(stiff_ref[d])
        stiff_h[d] = high
        stiff_l[d] = low
    proj_s[...] = jnp.zeros_like(proj_s)
    proj_c[...] = jnp.zeros_like(proj_c)
    for s in range(4):
        table = proj_ref[:, s, :]
        proj_s[s * FR : s * FR + SIDE, 0:SIDE] = table
        proj_c[0:SIDE, s * FR : s * FR + SIDE] = table
    proj_t[...] = proj_s[...].T[0:FR]
    proj_s_h, proj_s_l = split(proj_s[0 : 4 * FR, 0:FR])
    proj_c_h, proj_c_l = split(proj_c[:, 0 : 4 * FR])
    proj_t_h, proj_t_l = split(proj_t[:, 0 : 4 * FR])

    me = own_m[4]
    self_fine = code(me[0:1] * float(EB) + me[1:2], me[7:8])
    self_coarse = code(me[3:4] * float(EB) + me[4:5], me[7:8])
    oh_self[...] = one_hot(ELEMS, jnp.concatenate([self_fine, self_coarse], axis=1))

    def edge_codes(held):
        parts_f, parts_c = [], []
        for d in EDGE_DIRS:
            facts_d = held[d]
            pair = facts_d[0:1] + float(EDGE_BASE[d]) if d in (3, 5) else float(EDGE_BASE[d])
            parts_f.append(code(facts_d[2:3] * 16.0 + pair, facts_d[7:8]))
            parts_c.append(code(facts_d[6:7] * 128.0 + facts_d[5:6] * 16.0 + pair, facts_d[7:8]))
        return (
            one_hot(128, jnp.concatenate(parts_f, axis=1)),
            one_hot(512, jnp.concatenate(parts_c, axis=1)),
        )

    ones = jnp.ones((16, 6 * EB), BF16)
    edge_f, edge_c = edge_codes(own_m)
    n_out[...] = dot_nt(edge_f, edge_c).astype(BF16)
    sum_out = dot_nt(ones, edge_f)[0:1]

    def mortar_jump(coarses, fines, subs):
        high = coarses.astype(BF16).astype(F32)
        return by_table(proj_c_h, proj_c_l, by_subface(high, subs), by_subface(coarses - high, subs)) - fines

    def mortar_back(jump, subs):
        high = jump.astype(BF16).astype(F32)
        return by_table(proj_t_h, proj_t_l, by_subface(high, subs), by_subface(jump - high, subs))

    def local_part(field, views):
        field_h, field_l, f_h, f_l, faces, own = views
        got = dot(f_h, oh_self[...]) + dot(f_l, oh_self[...])
        jump = mortar_jump(pick_face(got[:, EB:], me[5:6]), pick_face(got[:, 0:EB], me[2:3]), me[6:7])
        back = mortar_back(jump, me[6:7])
        terms = jnp.concatenate([-PENALTY * jump, PENALTY * back], axis=1)
        s_h, s_l = spread_split(terms, jnp.concatenate([me[2:3], me[5:6]], axis=1))
        gathered = dot_nt(s_h, oh_self[...]) + dot_nt(s_l, oh_self[...])

        blocks = []
        for a in range(EA):
            here = slice(a * EB, (a + 1) * EB)
            x_low, x_high = faces[0:FR, here], faces[FR : 2 * FR, here]
            y_low, y_high = faces[2 * FR : 3 * FR, here], faces[3 * FR : 4 * FR, here]
            left = x_low if a == 0 else x_low - faces[FR : 2 * FR, (a - 1) * EB : a * EB]
            right = x_high if a == EA - 1 else x_high - faces[0:FR, (a + 1) * EB : (a + 2) * EB]
            below = jnp.where(lane == 0, 0.0, pltpu.roll(y_high, 1, 1))
            above = jnp.where(lane == EB - 1, 0.0, pltpu.roll(y_low, EB - 1, 1))
            lateral = jnp.concatenate([left, right, y_low - below, y_high - above], axis=0)
            blocks.append(jnp.concatenate([PENALTY * lateral, jnp.zeros((2 * FR, EB), F32)], axis=0))
        gathered = gathered + jnp.concatenate(blocks, axis=1)

        total = field
        for d in range(3):
            total = total + metric_ref[d : d + 1, :] * by_table(stiff_h[d], stiff_l[d], field_h, field_l)
        return scale * total, gathered

    def remote_part(t, views, gathered, sum_in):
        field_h, field_l, f_h, f_l, faces, own = views
        fines, coarses, subs = [], [], []
        for side in range(2):
            d = (1, 7)[side]
            here = slice(0, EB) if side == 0 else slice((EA - 1) * EB, EA * EB)
            h_h, h_l = split(halo_x[t, side])
            got = dot(jnp.concatenate([f_h[:, here], h_h], axis=0), oh_x[side])
            got = got + dot(jnp.concatenate([f_l[:, here], h_l], axis=0), oh_x[side])
            ours, theirs = got[0:FACES], got[FACES:]
            fines += [pick_face(ours[:, 0:EB], own_m[d][2:3]), pick_face(theirs[:, EB:], halo_m[d][2:3])]
            coarses += [pick_face(theirs[:, 0:EB], own_m[d][5:6]), pick_face(ours[:, EB:], halo_m[d][5:6])]
            subs += [own_m[d][6:7], halo_m[d][6:7]]
        jump = mortar_jump(*(jnp.concatenate(parts, axis=1) for parts in (coarses, fines, subs)))
        jump = [jump[:, k * EB : (k + 1) * EB] for k in range(4)]
        back = mortar_back(jnp.concatenate([jump[1], jump[3]], axis=1), jnp.concatenate([subs[1], subs[3]], axis=1))
        side_terms = []
        for side in range(2):
            d = (1, 7)[side]
            terms = jnp.concatenate(
                [-PENALTY * jump[2 * side], PENALTY * back[:, side * EB : (side + 1) * EB]], axis=1
            )
            s_h, s_l = spread_split(terms, jnp.concatenate([own_m[d][2:3], halo_m[d][5:6]], axis=1))
            side_term = dot_nt(s_h, oh_x[side]) + dot_nt(s_l, oh_x[side])
            if side == 0:
                beside = [-PENALTY * halo_x[t, 0, FR : 2 * FR, :], jnp.zeros((5 * FR, EB), F32)]
            else:
                beside = [jnp.zeros((FR, EB), F32), -PENALTY * halo_x[t, 1, 0:FR, :], jnp.zeros((4 * FR, EB), F32)]
            side_terms.append(side_term + jnp.concatenate(beside, axis=0))

        across = jnp.zeros((FR, 128), F32)
        for index, (d, turn, low, high) in enumerate(
            ((3, -4, 0, 4), (5, 4, 4, 8), (0, -3, 8, 9), (2, -1, 9, 10), (6, 1, 10, 11), (8, 3, 11, 12))
        ):
            moved = pltpu.roll(halo_y[t, index], turn % 128, 1)
            across = jnp.where((lane_pair >= low) & (lane_pair < high), moved, across)
        pairs = jnp.concatenate([own, across], axis=1)
        pairs_h, pairs_l = split(pairs)
        images = by_table(proj_s_h, proj_s_l, pairs_h, pairs_l)
        image_own = jnp.concatenate([images[s * FR : (s + 1) * FR, 0:128] for s in range(4)], axis=1)
        image_far = jnp.concatenate([images[s * FR : (s + 1) * FR, 128:] for s in range(4)], axis=1)
        far_h, far_l = split(image_far)
        on_fine = own * sum_out - dot_nt(far_h, n_out[...]) - dot_nt(far_l, n_out[...])
        jumps = image_own * sum_in - dot(pairs_h[:, 128:], n_in[...]) - dot(pairs_l[:, 128:], n_in[...])
        jumps = jnp.concatenate([jumps[:, s * 128 : (s + 1) * 128] for s in range(4)], axis=0)
        jumps_h, jumps_l = split(jumps)
        on_edge = PENALTY * (on_fine + by_table(proj_t_h, proj_t_l, jumps_h, jumps_l))
        from_low = pltpu.roll(across, 128 - 16, 1)
        from_high = pltpu.roll(across, 16, 1)
        on_edge = on_edge - PENALTY * jnp.where(
            (lane_face == 2) & (lane_pair < 4),
            from_low,
            jnp.where((lane_face == 3) & (lane_pair >= 4) & (lane_pair < 8), from_high, 0.0),
        )
        e_high = on_edge.astype(BF16).astype(F32)
        e_low = on_edge - e_high
        e_h = jnp.concatenate([jnp.where(lane_face == f, e_high, 0.0) for f in range(6)], axis=0).astype(BF16)
        e_l = jnp.concatenate([jnp.where(lane_face == f, e_low, 0.0) for f in range(6)], axis=0).astype(BF16)
        gathered = gathered + dot_nt(e_h, edge_ref[...]) + dot_nt(e_l, edge_ref[...])

        middle = jnp.zeros((FACES, (EA - 2) * EB), F32)
        gathered = gathered + jnp.concatenate([side_terms[0], middle, side_terms[1]], axis=1)
        g_h, g_l = split(gathered)
        place = place_ref[...]
        return dot(place, g_h) + dot(place, g_l)

    def arrive(t):
        for side in range(2):
            if_there((1, 7)[side], lambda: x_copy(t, side, True).wait_recv())
        for index in range(6):
            if_there(EDGE_DIRS[index], lambda: y_copy(t, index, True).wait_recv())

    b = b_ref[...]
    total, gathered = local_part(b, views)
    for d in DIRS:
        if_there(d, lambda: m_copy(d, True).wait_recv())
    for side in range(2):
        d = (1, 7)[side]
        both = jnp.concatenate([own_m[d], halo_m[d]], axis=1)
        oh_x[side] = one_hot(EB, code(both[1:2], both[7:8]))
    edge_f, edge_c = edge_codes(halo_m)
    n_in[...] = dot_nt(edge_f, edge_c).astype(BF16)
    sum_in = dot_nt(ones, edge_c)[0:1]
    arrive(0)
    q = total + remote_part(0, views, gathered, sum_in)

    views = faces_of(1, q)
    send(1)
    q_ref[...] = q
    total, gathered = local_part(q, views)
    b = b_ref[...]
    q = q_ref[...]
    early = [column_sums(b, b), column_sums(b, q), column_sums(q, q)]
    arrive(1)
    w = total + remote_part(1, views, gathered, sum_in)
    w_ref[...] = w
    early += [column_sums(b_ref[...], w), column_sums(q_ref[...], w)]

    lanes = jnp.zeros((1, 128), F32)
    for index, sums in enumerate(early):
        lanes = jnp.where(lane == index, jnp.sum(sums, axis=1, keepdims=True), lanes)
    mine0[...] = lanes
    core = pltpu.make_async_remote_copy(
        src_ref=mine0,
        dst_ref=red0,
        send_sem=s0_send,
        recv_sem=s0_recv,
        device_id={"gx": gx + 1 - 2 * lax.rem(gx, 2), "gy": gy},
        device_id_type=MESH,
    )
    core.start()
    core.wait_recv()
    lanes = mine0[...] + red0[...]
    mine1[...] = lanes
    for k, offset in enumerate(chips):
        pltpu.make_async_remote_copy(
            src_ref=mine1,
            dst_ref=red1.at[k],
            send_sem=s1_send,
            recv_sem=s1_recv,
            device_id=chip(offset),
            device_id_type=MESH,
        ).start()
    pltpu.make_async_copy(red1, red1, s1_recv).wait()
    lanes = lanes + jnp.sum(red1[...], axis=0)

    bb, bq, qq, bw, qw = (lanes[:, i : i + 1] for i in range(5))
    alpha = bb / bq
    new = bb - 2.0 * alpha * bq + alpha * alpha * qq
    grow = 1.0 + new / bb
    alpha_next = new / (grow * grow * bq - grow * alpha * (bw + qq) + alpha * alpha * qw)
    row = iota((8, ELEMS), 0)
    coef_ref[...] = jnp.where(row == 0, alpha + alpha_next * grow, alpha * alpha_next)

    for t in range(2):
        for side in range(2):
            if_there((1, 7)[side], lambda: x_copy(t, side, False).wait_send())
        for index in range(6):
            if_there(EDGE_DIRS[index], lambda: y_copy(t, index, False).wait_send())
    for d in DIRS:
        if_there(d, lambda: m_copy(d, False).wait_send())
    core.wait_send()
    pltpu.make_async_copy(red1, red1, s1_send).wait()


def body(
    n_gx,
    n_gy,
    right_side,
    stiffness,
    metric,
    levels,
    projection,
    mortar_fine,
    mortar_face,
    mortar_owner,
    mortar_subface,
    mortar_coarse,
    mortar_cface,
):
    pick, place, edge = (jnp.asarray(table, BF16) for table in constant_tables())
    field = jax.ShapeDtypeStruct(right_side.shape, F32)
    count = mortar_fine.shape[0]
    others = n_gx // 2 * n_gy - 1
    hbm = pl.BlockSpec(memory_space=pltpu.HBM)
    vmem = pl.BlockSpec(memory_space=pltpu.VMEM)
    dma = pltpu.SemaphoreType.DMA
    line = [
        entry.reshape(1, count)
        for entry in (
            mortar_fine,
            mortar_face,
            mortar_owner,
            mortar_subface,
            mortar_coarse,
            mortar_cface,
            levels,
        )
    ]
    q, w, coef = pl.pallas_call(
        functools.partial(kernel, n_gx, n_gy),
        out_shape=(field, field, jax.ShapeDtypeStruct((8, ELEMS), F32)),
        in_specs=[hbm] * 14,
        out_specs=(vmem, vmem, vmem),
        scratch_shapes=[
            pltpu.VMEM((NODES, ELEMS), F32),
            pltpu.VMEM((3, NODES, NODES), F32),
            pltpu.VMEM((3, ELEMS), F32),
            pltpu.VMEM((7, 1, ELEMS), jnp.int32),
            pltpu.VMEM((SIDE, 4, SIDE), F32),
            pltpu.VMEM((FACES, NODES), BF16),
            pltpu.VMEM((NODES, FACES), BF16),
            pltpu.VMEM((ELEMS, 128), BF16),
            pltpu.VMEM((2, 2, FACES, EB), F32),
            pltpu.VMEM((2, 6, FR, 128), F32),
            pltpu.VMEM((9, 8, 128), F32),
            pltpu.VMEM((9, 8, 128), F32),
            pltpu.VMEM((2, 2, FACES, EB), F32),
            pltpu.VMEM((2, FR, 128), F32),
            pltpu.VMEM((3, NODES, NODES), BF16),
            pltpu.VMEM((3, NODES, NODES), BF16),
            pltpu.VMEM((ELEMS, 2 * EB), BF16),
            pltpu.VMEM((2, EB, 2 * EB), BF16),
            pltpu.VMEM((128, 512), BF16),
            pltpu.VMEM((128, 512), BF16),
            pltpu.VMEM((256, 128), F32),
            pltpu.VMEM((FR, 256), F32),
            pltpu.VMEM((FR, 256), F32),
            pltpu.VMEM((1, 128), F32),
            pltpu.VMEM((others, 1, 128), F32),
            pltpu.VMEM((1, 128), F32),
            pltpu.VMEM((1, 128), F32),
            dma((14,)),
            dma((2, 2)),
            dma((2, 2)),
            dma((2, 6)),
            dma((2, 6)),
            dma((9,)),
            dma((9,)),
            dma,
            dma,
            dma,
            dma,
        ],
        compiler_params=pltpu.CompilerParams(
            collective_id=0, has_side_effects=True, vmem_limit_bytes=48 * 1024 * 1024
        ),
    )(right_side, stiffness, metric, *line, projection.transpose(1, 0, 2), pick, place, edge)
    first, second = coef[0:1], coef[1:2]
    return first * right_side - second * q, right_side - first * q + second * w


def solution(mesh):
    columns = P(None, ("gx", "gy"))
    faces = P(("gx", "gy"))
    in_specs = (columns, P(), columns, faces, P(), faces, faces, P(("gx", "gy"), None), faces, faces, faces)
    run = functools.partial(body, mesh.shape["gx"], mesh.shape["gy"])
    return jax.shard_map(run, mesh=mesh, in_specs=in_specs, out_specs=(columns, columns), check_vma=False)
```

```python
import functools

import jax
import jax.numpy as jnp
import numpy as np
from jax import lax
from jax.experimental import pallas as pl
from jax.experimental.pallas import tpu as pltpu
from jax.sharding import PartitionSpec as P

NP = 6
NODES = NP * NP * NP
SIDE = NP * NP
EA = 4
EB = 128
ELEMS = EA * EB
FR = 40
FACES = 6 * FR
PENALTY = 1.0

F32 = jnp.float32
BF16 = jnp.bfloat16
MESH = pl.DeviceIdType.MESH

DIRS = {d: (d // 3 - 1, d % 3 - 1) for d in range(9) if d != 4}
EDGE_DIRS = (3, 5, 0, 2, 6, 8)
EDGE_BASE = {3: 0, 5: 4, 0: 8, 2: 9, 6: 10, 8: 11}


def face_nodes(face):
    ids = np.arange(NODES).reshape(NP, NP, NP)
    return [ids[0], ids[5], ids[:, 0], ids[:, 5], ids[:, :, 0], ids[:, :, 5]][face].reshape(-1)


def constant_tables():
    pick = np.zeros((FACES, NODES), np.float32)
    for face in range(6):
        pick[face * FR + np.arange(SIDE), face_nodes(face)] = 1.0
    edge = np.zeros((ELEMS, 128), np.float32)
    columns = [a * EB for a in range(EA)] + [a * EB + EB - 1 for a in range(EA)]
    columns += [0, EB - 1, (EA - 1) * EB, ELEMS - 1]
    for face in range(6):
        for pair, column in enumerate(columns):
            edge[column, face * 16 + pair] = 1.0
    return pick, pick.T.copy(), edge


def dot(a, b):
    return lax.dot_general(a, b, (((1,), (0,)), ((), ())), preferred_element_type=F32)


def dot_nt(a, b):
    return lax.dot_general(a, b, (((1,), (1,)), ((), ())), preferred_element_type=F32)


def split(value):
    high = value.astype(BF16)
    return high, (value - high.astype(F32)).astype(BF16)


def iota(shape, dim):
    return lax.broadcasted_iota(jnp.int32, shape, dim)


def one_hot(rows, code):
    return jnp.where(iota((rows, code.shape[1]), 0).astype(F32) == code, 1.0, 0.0).astype(BF16)


def pick_face(sides, face):
    out = None
    for f in range(6):
        part = jnp.where(face == float(f), sides[f * FR : (f + 1) * FR], 0.0)
        out = part if out is None else out + part
    return out


def spread_face(values, face):
    return jnp.concatenate([jnp.where(face == float(f), values, 0.0) for f in range(6)], axis=0)


def spread_split(values, face):
    high = values.astype(BF16).astype(F32)
    return spread_face(high, face).astype(BF16), spread_face(values - high, face).astype(BF16)


def by_subface(values, sub):
    return jnp.concatenate([jnp.where(sub == float(s), values, 0.0) for s in range(4)], axis=0).astype(BF16)


def column_sums(a, b):
    prod = a * b
    rows = jnp.sum(prod, axis=0, keepdims=True)
    return sum(rows[:, t * EB : (t + 1) * EB] for t in range(EA))


def kernel(
    n_gx,
    n_gy,
    b_hbm,
    stiff_hbm,
    metric_hbm,
    fine_hbm,
    face_hbm,
    owner_hbm,
    sub_hbm,
    coarse_hbm,
    cface_hbm,
    level_hbm,
    proj_hbm,
    pick_hbm,
    place_hbm,
    edge_hbm,
    q_ref,
    w_ref,
    coef_ref,
    b_ref,
    stiff_ref,
    metric_ref,
    ints_ref,
    proj_ref,
    pick_ref,
    place_ref,
    edge_ref,
    halo_x,
    halo_y,
    halo_m,
    own_m,
    own_x,
    own_y,
    stiff_h,
    stiff_l,
    oh_self,
    oh_x,
    n_out,
    n_in,
    proj_s,
    proj_c,
    proj_t,
    red0,
    red1,
    mine0,
    mine1,
    in_sem,
    sx_send,
    sx_recv,
    sy_send,
    sy_recv,
    sm_send,
    sm_recv,
    s0_send,
    s0_recv,
    s1_send,
    s1_recv,
):
    gx = lax.axis_index("gx")
    gy = lax.axis_index("gy")

    def there(d):
        dx, dy = DIRS[d]
        ok = (gx + dx >= 0) & (gx + dx < n_gx) & (gy + dy >= 0) & (gy + dy < n_gy)
        return ok, {"gx": gx + dx, "gy": gy + dy}

    def if_there(d, act):
        pl.when(there(d)[0])(act)

    size_x, size_y, size_z = n_gx // 2, n_gy // 4, 4
    chips = [(i, j, k) for i in range(size_x) for j in range(size_y) for k in range(size_z)][1:]
    chips.sort(key=lambda c: sum((v - 1) % n for v, n in zip(c, (size_x, size_y, size_z))))

    def chip(offset):
        y, z = gy // size_z, lax.rem(gy, size_z)
        return {
            "gx": lax.rem(gx + 2 * offset[0], n_gx),
            "gy": lax.rem(y + offset[1], size_y) * size_z + lax.rem(z + offset[2], size_z),
        }

    halo_x[...] = jnp.zeros_like(halo_x)
    halo_y[...] = jnp.zeros_like(halo_y)
    halo_m[...] = jnp.zeros_like(halo_m)

    barrier = pltpu.get_barrier_semaphore()
    expected = jnp.int32(len(chips))
    for offset in chips:
        pl.semaphore_signal(barrier, inc=1, device_id=chip(offset), device_id_type=MESH)
    for d in (0, 2, 6, 8, 1, 7):
        ok, where = there(d)

        @pl.when(ok)
        def _():
            pl.semaphore_signal(barrier, inc=1, device_id=where, device_id_type=MESH)

        expected = expected + ok.astype(jnp.int32)

    int_names = (fine_hbm, face_hbm, owner_hbm, sub_hbm, coarse_hbm, cface_hbm, level_hbm)
    loads = [(source, ints_ref.at[k]) for k, source in enumerate(int_names)]
    loads += [(b_hbm, b_ref), (pick_hbm, pick_ref), (edge_hbm, edge_ref), (proj_hbm, proj_ref)]
    loads += [(stiff_hbm, stiff_ref), (metric_hbm, metric_ref), (place_hbm, place_ref)]
    loads = [pltpu.make_async_copy(source, target, in_sem.at[k]) for k, (source, target) in enumerate(loads)]
    for load in loads:
        load.start()

    def x_copy(t, side, arriving):
        slot = side if arriving else 1 - side
        return pltpu.make_async_remote_copy(
            src_ref=own_x.at[t, side],
            dst_ref=halo_x.at[t, slot],
            send_sem=sx_send.at[t, side],
            recv_sem=sx_recv.at[t, slot],
            device_id=there((1, 7)[side])[1],
            device_id_type=MESH,
        )

    def y_copy(t, index, arriving):
        d = EDGE_DIRS[index]
        slot = index if arriving else EDGE_DIRS.index(8 - d)
        return pltpu.make_async_remote_copy(
            src_ref=own_y.at[t],
            dst_ref=halo_y.at[t, slot],
            send_sem=sy_send.at[t, index],
            recv_sem=sy_recv.at[t, slot],
            device_id=there(d)[1],
            device_id_type=MESH,
        )

    def m_copy(d, arriving):
        slot = d if arriving else 8 - d
        return pltpu.make_async_remote_copy(
            src_ref=own_m.at[d],
            dst_ref=halo_m.at[slot],
            send_sem=sm_send.at[d],
            recv_sem=sm_recv.at[slot],
            device_id=there(d)[1],
            device_id_type=MESH,
        )

    lane = iota((1, 128), 1)
    lane_face = lane >> 4
    lane_pair = lane & 15

    def by_table(high, low, value_h, value_l):
        return dot(high, value_h) + dot(low, value_h) + dot(high, value_l)

    def code(entry, active):
        return jnp.where(active > 0.0, entry, -1.0)

    for load in loads[:7]:
        load.wait()
    fine, face, owner, sub, coarse, cface, level = (ints_ref[k] for k in range(7))
    shift = n_gy.bit_length() - 1
    slot = ((owner >> shift) - gx + 1) * 3 + (owner & (n_gy - 1)) - gy + 1
    count = fine.shape[1]
    hits = jnp.where(iota((16, count), 0) == slot, 1.0, 0.0)
    before = jnp.where(iota((count, count), 0) < iota((count, count), 1), 1.0, 0.0).astype(BF16)
    position = jnp.sum(hits * dot(hits.astype(BF16), before), axis=0, keepdims=True)
    row = iota((8, count), 0)
    facts = jnp.ones((8, count), jnp.int32)
    for index, entry in enumerate((fine >> 7, fine & 127, face, coarse >> 7, coarse & 127, cface, sub)):
        facts = jnp.where(row == index, entry, facts)
    facts = facts.astype(F32)
    stacked = jnp.concatenate([facts * hits[k : k + 1] for k in range(9)], axis=0).astype(BF16)
    packed = dot_nt(stacked, one_hot(EB, position))
    for k in range(9):
        own_m[k] = packed[8 * k : 8 * k + 8]
    scale = jnp.where(level == 0, 1.0, jnp.where(level == 1, 0.5, 0.25))

    def faces_of(t, field):
        pick = pick_ref[...]
        field_h, field_l = split(field)
        f_h = dot(pick, field_h)
        f_l = dot(pick, field_l)
        faces = f_h + f_l
        own_x[t, 0] = faces[:, 0:EB]
        own_x[t, 1] = faces[:, (EA - 1) * EB :]
        f_h = f_h.astype(BF16)
        f_l = f_l.astype(BF16)
        edges = dot(f_h, edge_ref[...]) + dot(f_l, edge_ref[...])
        own = None
        for f in range(6):
            part = jnp.where(lane_face == f, edges[f * FR : (f + 1) * FR], 0.0)
            own = part if own is None else own + part
        own_y[t] = own
        return field_h, field_l, f_h, f_l, faces, own

    def send(t):
        for index in (2, 3, 4, 5, 0, 1):
            if_there(EDGE_DIRS[index], lambda: y_copy(t, index, False).start())
        for side in range(2):
            if_there((1, 7)[side], lambda: x_copy(t, side, False).start())

    for load in loads[7:10]:
        load.wait()
    views = faces_of(0, b_ref[...])

    pl.semaphore_wait(barrier, expected)
    send(0)
    for d in (0, 2, 6, 8, 3, 5, 1, 7):
        if_there(d, lambda: m_copy(d, False).start())

    for load in loads[10:]:
        load.wait()
    for d in range(3):
        high, low = split(stiff_ref[d])
        stiff_h[d] = high
        stiff_l[d] = low
    proj_s[...] = jnp.zeros_like(proj_s)
    proj_c[...] = jnp.zeros_like(proj_c)
    for s in range(4):
        table = proj_ref[:, s, :]
        proj_s[s * FR : s * FR + SIDE, 0:SIDE] = table
        proj_c[0:SIDE, s * FR : s * FR + SIDE] = table
    proj_t[...] = proj_s[...].T[0:FR]
    proj_s_h, proj_s_l = split(proj_s[0 : 4 * FR, 0:FR])
    proj_c_h, proj_c_l = split(proj_c[:, 0 : 4 * FR])
    proj_t_h, proj_t_l = split(proj_t[:, 0 : 4 * FR])

    me = own_m[4]
    self_fine = code(me[0:1] * float(EB) + me[1:2], me[7:8])
    self_coarse = code(me[3:4] * float(EB) + me[4:5], me[7:8])
    oh_self[...] = one_hot(ELEMS, jnp.concatenate([self_fine, self_coarse], axis=1))

    def edge_codes(held):
        parts_f, parts_c = [], []
        for d in EDGE_DIRS:
            facts_d = held[d]
            pair = facts_d[0:1] + float(EDGE_BASE[d]) if d in (3, 5) else float(EDGE_BASE[d])
            parts_f.append(code(facts_d[2:3] * 16.0 + pair, facts_d[7:8]))
            parts_c.append(code(facts_d[6:7] * 128.0 + facts_d[5:6] * 16.0 + pair, facts_d[7:8]))
        return (
            one_hot(128, jnp.concatenate(parts_f, axis=1)),
            one_hot(512, jnp.concatenate(parts_c, axis=1)),
        )

    ones = jnp.ones((16, 6 * EB), BF16)
    edge_f, edge_c = edge_codes(own_m)
    n_out[...] = dot_nt(edge_f, edge_c).astype(BF16)
    sum_out = dot_nt(ones, edge_f)[0:1]

    def mortar_jump(coarses, fines, subs):
        high = coarses.astype(BF16).astype(F32)
        return by_table(proj_c_h, proj_c_l, by_subface(high, subs), by_subface(coarses - high, subs)) - fines

    def mortar_back(jump, subs):
        high = jump.astype(BF16).astype(F32)
        return by_table(proj_t_h, proj_t_l, by_subface(high, subs), by_subface(jump - high, subs))

    def local_part(field, views):
        field_h, field_l, f_h, f_l, faces, own = views
        got = dot(f_h, oh_self[...]) + dot(f_l, oh_self[...])
        jump = mortar_jump(pick_face(got[:, EB:], me[5:6]), pick_face(got[:, 0:EB], me[2:3]), me[6:7])
        back = mortar_back(jump, me[6:7])
        terms = jnp.concatenate([-PENALTY * jump, PENALTY * back], axis=1)
        s_h, s_l = spread_split(terms, jnp.concatenate([me[2:3], me[5:6]], axis=1))
        gathered = dot_nt(s_h, oh_self[...]) + dot_nt(s_l, oh_self[...])

        blocks = []
        for a in range(EA):
            here = slice(a * EB, (a + 1) * EB)
            x_low, x_high = faces[0:FR, here], faces[FR : 2 * FR, here]
            y_low, y_high = faces[2 * FR : 3 * FR, here], faces[3 * FR : 4 * FR, here]
            left = x_low if a == 0 else x_low - faces[FR : 2 * FR, (a - 1) * EB : a * EB]
            right = x_high if a == EA - 1 else x_high - faces[0:FR, (a + 1) * EB : (a + 2) * EB]
            below = jnp.where(lane == 0, 0.0, pltpu.roll(y_high, 1, 1))
            above = jnp.where(lane == EB - 1, 0.0, pltpu.roll(y_low, EB - 1, 1))
            lateral = jnp.concatenate([left, right, y_low - below, y_high - above], axis=0)
            blocks.append(jnp.concatenate([PENALTY * lateral, jnp.zeros((2 * FR, EB), F32)], axis=0))
        gathered = gathered + jnp.concatenate(blocks, axis=1)

        total = field
        for d in range(3):
            total = total + metric_ref[d : d + 1, :] * by_table(stiff_h[d], stiff_l[d], field_h, field_l)
        return scale * total, gathered

    def remote_part(t, views, gathered, sum_in):
        field_h, field_l, f_h, f_l, faces, own = views
        for side in range(2):
            if_there((1, 7)[side], lambda: x_copy(t, side, True).wait_recv())
        fines, coarses, subs = [], [], []
        for side in range(2):
            d = (1, 7)[side]
            here = slice(0, EB) if side == 0 else slice((EA - 1) * EB, EA * EB)
            h_h, h_l = split(halo_x[t, side])
            got = dot(jnp.concatenate([f_h[:, here], h_h], axis=0), oh_x[side])
            got = got + dot(jnp.concatenate([f_l[:, here], h_l], axis=0), oh_x[side])
            ours, theirs = got[0:FACES], got[FACES:]
            fines += [pick_face(ours[:, 0:EB], own_m[d][2:3]), pick_face(theirs[:, EB:], halo_m[d][2:3])]
            coarses += [pick_face(theirs[:, 0:EB], own_m[d][5:6]), pick_face(ours[:, EB:], halo_m[d][5:6])]
            subs += [own_m[d][6:7], halo_m[d][6:7]]
        jump = mortar_jump(*(jnp.concatenate(parts, axis=1) for parts in (coarses, fines, subs)))
        jump = [jump[:, k * EB : (k + 1) * EB] for k in range(4)]
        back = mortar_back(jnp.concatenate([jump[1], jump[3]], axis=1), jnp.concatenate([subs[1], subs[3]], axis=1))
        side_terms = []
        for side in range(2):
            d = (1, 7)[side]
            terms = jnp.concatenate(
                [-PENALTY * jump[2 * side], PENALTY * back[:, side * EB : (side + 1) * EB]], axis=1
            )
            s_h, s_l = spread_split(terms, jnp.concatenate([own_m[d][2:3], halo_m[d][5:6]], axis=1))
            side_term = dot_nt(s_h, oh_x[side]) + dot_nt(s_l, oh_x[side])
            if side == 0:
                beside = [-PENALTY * halo_x[t, 0, FR : 2 * FR, :], jnp.zeros((5 * FR, EB), F32)]
            else:
                beside = [jnp.zeros((FR, EB), F32), -PENALTY * halo_x[t, 1, 0:FR, :], jnp.zeros((4 * FR, EB), F32)]
            side_terms.append(side_term + jnp.concatenate(beside, axis=0))

        for index in range(6):
            if_there(EDGE_DIRS[index], lambda: y_copy(t, index, True).wait_recv())
        across = jnp.zeros((FR, 128), F32)
        for index, (d, turn, low, high) in enumerate(
            ((3, -4, 0, 4), (5, 4, 4, 8), (0, -3, 8, 9), (2, -1, 9, 10), (6, 1, 10, 11), (8, 3, 11, 12))
        ):
            moved = pltpu.roll(halo_y[t, index], turn % 128, 1)
            across = jnp.where((lane_pair >= low) & (lane_pair < high), moved, across)
        pairs = jnp.concatenate([own, across], axis=1)
        pairs_h, pairs_l = split(pairs)
        images = by_table(proj_s_h, proj_s_l, pairs_h, pairs_l)
        image_own = jnp.concatenate([images[s * FR : (s + 1) * FR, 0:128] for s in range(4)], axis=1)
        image_far = jnp.concatenate([images[s * FR : (s + 1) * FR, 128:] for s in range(4)], axis=1)
        far_h, far_l = split(image_far)
        on_fine = own * sum_out - dot_nt(far_h, n_out[...]) - dot_nt(far_l, n_out[...])
        jumps = image_own * sum_in - dot(pairs_h[:, 128:], n_in[...]) - dot(pairs_l[:, 128:], n_in[...])
        jumps = jnp.concatenate([jumps[:, s * 128 : (s + 1) * 128] for s in range(4)], axis=0)
        jumps_h, jumps_l = split(jumps)
        on_edge = PENALTY * (on_fine + by_table(proj_t_h, proj_t_l, jumps_h, jumps_l))
        from_low = pltpu.roll(across, 128 - 16, 1)
        from_high = pltpu.roll(across, 16, 1)
        on_edge = on_edge - PENALTY * jnp.where(
            (lane_face == 2) & (lane_pair < 4),
            from_low,
            jnp.where((lane_face == 3) & (lane_pair >= 4) & (lane_pair < 8), from_high, 0.0),
        )
        e_high = on_edge.astype(BF16).astype(F32)
        e_low = on_edge - e_high
        e_h = jnp.concatenate([jnp.where(lane_face == f, e_high, 0.0) for f in range(6)], axis=0).astype(BF16)
        e_l = jnp.concatenate([jnp.where(lane_face == f, e_low, 0.0) for f in range(6)], axis=0).astype(BF16)
        gathered = gathered + dot_nt(e_h, edge_ref[...]) + dot_nt(e_l, edge_ref[...])

        middle = jnp.zeros((FACES, (EA - 2) * EB), F32)
        gathered = gathered + jnp.concatenate([side_terms[0], middle, side_terms[1]], axis=1)
        g_h, g_l = split(gathered)
        place = place_ref[...]
        return dot(place, g_h) + dot(place, g_l)

    b = b_ref[...]
    total, gathered = local_part(b, views)
    for d in DIRS:
        if_there(d, lambda: m_copy(d, True).wait_recv())
    for side in range(2):
        d = (1, 7)[side]
        both = jnp.concatenate([own_m[d], halo_m[d]], axis=1)
        oh_x[side] = one_hot(EB, code(both[1:2], both[7:8]))
    edge_f, edge_c = edge_codes(halo_m)
    n_in[...] = dot_nt(edge_f, edge_c).astype(BF16)
    sum_in = dot_nt(ones, edge_c)[0:1]
    q = total + remote_part(0, views, gathered, sum_in)

    views = faces_of(1, q)
    send(1)
    q_ref[...] = q
    total, gathered = local_part(q, views)
    b = b_ref[...]
    q = q_ref[...]
    early = [column_sums(b, b), column_sums(b, q), column_sums(q, q)]
    w = total + remote_part(1, views, gathered, sum_in)
    w_ref[...] = w
    early += [column_sums(b_ref[...], w), column_sums(q_ref[...], w)]

    lanes = jnp.zeros((1, 128), F32)
    for index, sums in enumerate(early):
        lanes = jnp.where(lane == index, jnp.sum(sums, axis=1, keepdims=True), lanes)
    mine0[...] = lanes
    core = pltpu.make_async_remote_copy(
        src_ref=mine0,
        dst_ref=red0,
        send_sem=s0_send,
        recv_sem=s0_recv,
        device_id={"gx": gx + 1 - 2 * lax.rem(gx, 2), "gy": gy},
        device_id_type=MESH,
    )
    core.start()
    core.wait_recv()
    lanes = mine0[...] + red0[...]
    mine1[...] = lanes
    for k, offset in enumerate(chips):
        pltpu.make_async_remote_copy(
            src_ref=mine1,
            dst_ref=red1.at[k],
            send_sem=s1_send,
            recv_sem=s1_recv,
            device_id=chip(offset),
            device_id_type=MESH,
        ).start()
    pltpu.make_async_copy(red1, red1, s1_recv).wait()
    lanes = lanes + jnp.sum(red1[...], axis=0)

    bb, bq, qq, bw, qw = (lanes[:, i : i + 1] for i in range(5))
    alpha = bb / bq
    new = bb - 2.0 * alpha * bq + alpha * alpha * qq
    grow = 1.0 + new / bb
    alpha_next = new / (grow * grow * bq - grow * alpha * (bw + qq) + alpha * alpha * qw)
    row = iota((8, 128), 0)
    coef_ref[...] = jnp.where(row == 0, alpha + alpha_next * grow, alpha * alpha_next)

    for t in range(2):
        for side in range(2):
            if_there((1, 7)[side], lambda: x_copy(t, side, False).wait_send())
        for index in range(6):
            if_there(EDGE_DIRS[index], lambda: y_copy(t, index, False).wait_send())
    for d in DIRS:
        if_there(d, lambda: m_copy(d, False).wait_send())
    core.wait_send()
    pltpu.make_async_copy(red1, red1, s1_send).wait()


def finish(coef_ref, b_ref, q_ref, w_ref, x_hbm, r_hbm, made, out_sem):
    first, second = coef_ref[0:1, 0:1], coef_ref[1:2, 0:1]
    stores = []
    for part, (start, size) in enumerate(((0, 104), (104, NODES - 104))):
        rows = pl.ds(start, size)
        b, q, w = b_ref[rows, :], q_ref[rows, :], w_ref[rows, :]
        made[0, rows, :] = first * b - second * q
        made[1, rows, :] = b - first * q + second * w
        for k, target in enumerate((x_hbm, r_hbm)):
            store = pltpu.make_async_copy(made.at[k, rows], target.at[rows], out_sem.at[part, k])
            store.start()
            stores.append(store)
    for store in stores:
        store.wait()


def body(
    n_gx,
    n_gy,
    right_side,
    stiffness,
    metric,
    levels,
    projection,
    mortar_fine,
    mortar_face,
    mortar_owner,
    mortar_subface,
    mortar_coarse,
    mortar_cface,
):
    pick, place, edge = (jnp.asarray(table, BF16) for table in constant_tables())
    field = jax.ShapeDtypeStruct(right_side.shape, F32)
    count = mortar_fine.shape[0]
    others = n_gx // 2 * n_gy - 1
    hbm = pl.BlockSpec(memory_space=pltpu.HBM)
    vmem = pl.BlockSpec(memory_space=pltpu.VMEM)
    dma = pltpu.SemaphoreType.DMA
    line = [
        entry.reshape(1, count)
        for entry in (
            mortar_fine,
            mortar_face,
            mortar_owner,
            mortar_subface,
            mortar_coarse,
            mortar_cface,
            levels,
        )
    ]
    q, w, coef = pl.pallas_call(
        functools.partial(kernel, n_gx, n_gy),
        out_shape=(field, field, jax.ShapeDtypeStruct((8, 128), F32)),
        in_specs=[hbm] * 14,
        out_specs=(vmem, vmem, vmem),
        scratch_shapes=[
            pltpu.VMEM((NODES, ELEMS), F32),
            pltpu.VMEM((3, NODES, NODES), F32),
            pltpu.VMEM((3, ELEMS), F32),
            pltpu.VMEM((7, 1, ELEMS), jnp.int32),
            pltpu.VMEM((SIDE, 4, SIDE), F32),
            pltpu.VMEM((FACES, NODES), BF16),
            pltpu.VMEM((NODES, FACES), BF16),
            pltpu.VMEM((ELEMS, 128), BF16),
            pltpu.VMEM((2, 2, FACES, EB), F32),
            pltpu.VMEM((2, 6, FR, 128), F32),
            pltpu.VMEM((9, 8, 128), F32),
            pltpu.VMEM((9, 8, 128), F32),
            pltpu.VMEM((2, 2, FACES, EB), F32),
            pltpu.VMEM((2, FR, 128), F32),
            pltpu.VMEM((3, NODES, NODES), BF16),
            pltpu.VMEM((3, NODES, NODES), BF16),
            pltpu.VMEM((ELEMS, 2 * EB), BF16),
            pltpu.VMEM((2, EB, 2 * EB), BF16),
            pltpu.VMEM((128, 512), BF16),
            pltpu.VMEM((128, 512), BF16),
            pltpu.VMEM((256, 128), F32),
            pltpu.VMEM((FR, 256), F32),
            pltpu.VMEM((FR, 256), F32),
            pltpu.VMEM((1, 128), F32),
            pltpu.VMEM((others, 1, 128), F32),
            pltpu.VMEM((1, 128), F32),
            pltpu.VMEM((1, 128), F32),
            dma((14,)),
            dma((2, 2)),
            dma((2, 2)),
            dma((2, 6)),
            dma((2, 6)),
            dma((9,)),
            dma((9,)),
            dma,
            dma,
            dma,
            dma,
        ],
        compiler_params=pltpu.CompilerParams(
            collective_id=0, has_side_effects=True, vmem_limit_bytes=40 * 1024 * 1024
        ),
    )(
        *(
            pltpu.with_memory_space_constraint(operand, pltpu.HBM)
            for operand in (right_side, stiffness, metric, *line, projection.transpose(1, 0, 2), pick, place, edge)
        )
    )
    return pl.pallas_call(
        finish,
        out_shape=(field, field),
        in_specs=[vmem] * 4,
        out_specs=(hbm, hbm),
        scratch_shapes=[pltpu.VMEM((2, NODES, ELEMS), F32), dma((2, 2))],
        compiler_params=pltpu.CompilerParams(vmem_limit_bytes=40 * 1024 * 1024),
    )(coef, right_side, q, w)


def solution(mesh):
    columns = P(None, ("gx", "gy"))
    faces = P(("gx", "gy"))
    in_specs = (columns, P(), columns, faces, P(), faces, faces, P(("gx", "gy"), None), faces, faces, faces)
    run = functools.partial(body, mesh.shape["gx"], mesh.shape["gy"])
    return jax.shard_map(run, mesh=mesh, in_specs=in_specs, out_specs=(columns, columns), check_vma=False)
```

```python
import functools

import jax
import jax.numpy as jnp
import numpy as np
from jax import lax
from jax.experimental import pallas as pl
from jax.experimental.pallas import tpu as pltpu
from jax.sharding import PartitionSpec as P

NP = 6
NODES = NP * NP * NP
SIDE = NP * NP
EA = 4
EB = 128
ELEMS = EA * EB
FR = 40
FACES = 6 * FR
SP = 224
PENALTY = 1.0

F32 = jnp.float32
BF16 = jnp.bfloat16
MESH = pl.DeviceIdType.MESH

DIRS = {d: (d // 3 - 1, d % 3 - 1) for d in range(9) if d != 4}
EDGE_DIRS = (3, 5, 0, 2, 6, 8)
CORNERS = {0: 8, 2: 9, 6: 10, 8: 11}
CORNER_SHIFT = {8: 7, 9: 9, 10: 3, 11: 5}


def face_nodes(face):
    ids = np.arange(NODES).reshape(NP, NP, NP)
    return [ids[0], ids[5], ids[:, 0], ids[:, 5], ids[:, :, 0], ids[:, :, 5]][face].reshape(-1)


def constant_tables():
    pick = np.zeros((FACES, NODES), np.float32)
    for face in range(6):
        pick[face * FR + np.arange(SIDE), face_nodes(face)] = 1.0
    return pick, pick.T.copy(), pick @ pick.T


def dot(a, b):
    return lax.dot_general(a, b, (((1,), (0,)), ((), ())), preferred_element_type=F32)


def dot_nt(a, b):
    return lax.dot_general(a, b, (((1,), (1,)), ((), ())), preferred_element_type=F32)


def split(value):
    high = value.astype(BF16)
    return high, (value - high.astype(F32)).astype(BF16)


def iota(shape, dim):
    return lax.broadcasted_iota(jnp.int32, shape, dim)


def one_hot(rows, code):
    return jnp.where(iota((rows, code.shape[1]), 0).astype(F32) == code, 1.0, 0.0).astype(BF16)


def pick_face(sides, face):
    out = None
    for f in range(6):
        part = jnp.where(face == float(f), sides[f * FR : (f + 1) * FR], 0.0)
        out = part if out is None else out + part
    return out


def spread_face(values, face):
    return jnp.concatenate([jnp.where(face == float(f), values, 0.0) for f in range(6)], axis=0)


def spread_split(values, face):
    high = values.astype(BF16).astype(F32)
    return spread_face(high, face).astype(BF16), spread_face(values - high, face).astype(BF16)


def by_subface(values, sub):
    return jnp.concatenate([jnp.where(sub == float(s), values, 0.0) for s in range(4)], axis=0).astype(BF16)


def column_sums(a, b):
    prod = a * b
    rows = jnp.sum(prod, axis=0, keepdims=True)
    return sum(rows[:, t * EB : (t + 1) * EB] for t in range(EA))


def kernel(
    n_gx,
    n_gy,
    b_hbm,
    stiff_hbm,
    metric_hbm,
    fine_hbm,
    face_hbm,
    owner_hbm,
    sub_hbm,
    coarse_hbm,
    cface_hbm,
    level_hbm,
    proj_hbm,
    pick_hbm,
    place_hbm,
    mix_hbm,
    q_ref,
    w_ref,
    coef_ref,
    b_ref,
    stiff_ref,
    metric_ref,
    ints_ref,
    proj_ref,
    pick_ref,
    place_ref,
    mix_ref,
    halo_x,
    halo_y,
    own_m,
    own_x,
    own_y,
    stiff_s,
    oh_self,
    oh_x,
    n_out,
    n_in,
    proj_s,
    proj_c,
    proj_t,
    red0,
    red1,
    mine0,
    mine1,
    in_sem,
    sx_send,
    sx_recv,
    sy_send,
    sy_recv,
    s0_send,
    s0_recv,
    s1_send,
    s1_recv,
):
    gx = lax.axis_index("gx")
    gy = lax.axis_index("gy")

    int_names = (fine_hbm, face_hbm, owner_hbm, sub_hbm, coarse_hbm, cface_hbm, level_hbm)
    loads = [(source, ints_ref.at[k]) for k, source in enumerate(int_names)]
    loads += [(b_hbm, b_ref), (pick_hbm, pick_ref), (proj_hbm, proj_ref), (mix_hbm, mix_ref)]
    loads += [(stiff_hbm, stiff_ref), (metric_hbm, metric_ref), (place_hbm, place_ref)]
    loads = [pltpu.make_async_copy(source, target, in_sem.at[k]) for k, (source, target) in enumerate(loads)]
    for load in loads:
        load.start()

    def there(d):
        dx, dy = DIRS[d]
        ok = (gx + dx >= 0) & (gx + dx < n_gx) & (gy + dy >= 0) & (gy + dy < n_gy)
        return ok, {"gx": gx + dx, "gy": gy + dy}

    def if_there(d, act):
        pl.when(there(d)[0])(act)

    size_x, size_y, size_z = n_gx // 2, n_gy // 4, 4
    chips = [(i, j, k) for i in range(size_x) for j in range(size_y) for k in range(size_z)][1:]
    chips.sort(key=lambda c: sum((v - 1) % n for v, n in zip(c, (size_x, size_y, size_z))))

    def chip(offset):
        y, z = gy // size_z, lax.rem(gy, size_z)
        return {
            "gx": lax.rem(gx + 2 * offset[0], n_gx),
            "gy": lax.rem(y + offset[1], size_y) * size_z + lax.rem(z + offset[2], size_z),
        }

    halo_x[...] = jnp.zeros_like(halo_x)
    halo_y[...] = jnp.zeros_like(halo_y)

    barrier = pltpu.get_barrier_semaphore()
    expected = jnp.int32(len(chips))
    for offset in chips:
        pl.semaphore_signal(barrier, inc=1, device_id=chip(offset), device_id_type=MESH)
    for d in (0, 2, 6, 8, 1, 7):
        ok, where = there(d)

        @pl.when(ok)
        def _():
            pl.semaphore_signal(barrier, inc=1, device_id=where, device_id_type=MESH)

        expected = expected + ok.astype(jnp.int32)

    def x_copy(t, side, arriving):
        slot = side if arriving else 1 - side
        rows = pl.ds(0, FACES + 8 * (1 - t))
        return pltpu.make_async_remote_copy(
            src_ref=own_x.at[t, side, rows],
            dst_ref=halo_x.at[t, slot, rows],
            send_sem=sx_send.at[t, side],
            recv_sem=sx_recv.at[t, slot],
            device_id=there((1, 7)[side])[1],
            device_id_type=MESH,
        )

    def y_copy(t, index, arriving):
        d = EDGE_DIRS[index]
        slot = index if arriving else EDGE_DIRS.index(8 - d)
        rows = pl.ds(0, FR + 8 * (1 - t))
        return pltpu.make_async_remote_copy(
            src_ref=own_y.at[t, index if t == 0 else 0, rows],
            dst_ref=halo_y.at[t, slot, rows],
            send_sem=sy_send.at[t, index],
            recv_sem=sy_recv.at[t, slot],
            device_id=there(d)[1],
            device_id_type=MESH,
        )

    def send(t):
        for index in (2, 3, 4, 5, 0, 1):
            if_there(EDGE_DIRS[index], lambda: y_copy(t, index, False).start())
        for side in range(2):
            if_there((1, 7)[side], lambda: x_copy(t, side, False).start())

    lane = iota((1, 128), 1)
    lane_face = lane >> 4
    lane_pair = lane & 15

    def stacked_table(value):
        high = value.astype(BF16)
        rest = value - high.astype(F32)
        return high, jnp.concatenate([high.astype(F32), rest], axis=0).astype(BF16)

    def by_table(table, value_h, value_l):
        high, both = table
        rows = high.shape[0]
        first = dot(both, value_h)
        return first[:rows] + first[rows:] + dot(high, value_l)

    def code(entry, active):
        return jnp.where(active > 0.0, entry, -1.0)

    for load in loads[:7]:
        load.wait()
    fine, face, owner, sub, coarse, cface, level = (ints_ref[k] for k in range(7))
    shift = n_gy.bit_length() - 1
    slot = ((owner >> shift) - gx + 1) * 3 + (owner & (n_gy - 1)) - gy + 1
    count = fine.shape[1]
    hits = jnp.where(iota((16, count), 0) == slot, 1.0, 0.0)
    parts = [hits[:, k : k + EB] for k in range(0, count, EB)]
    earlier = jnp.where(iota((EB, EB), 0) < iota((EB, EB), 1), 1.0, 0.0).astype(BF16)
    within = dot(jnp.concatenate(parts, axis=0).astype(BF16), earlier)
    offset, ranks = jnp.zeros((16, 1), F32), []
    for k, part in enumerate(parts):
        ranks.append(jnp.sum(part * (within[16 * k : 16 * k + 16] + offset), axis=0, keepdims=True))
        offset = offset + jnp.sum(part, axis=1, keepdims=True)
    position = jnp.concatenate(ranks, axis=1)
    row = iota((8, count), 0)
    facts = jnp.ones((8, count), jnp.int32)
    for index, entry in enumerate((fine >> 7, fine & 127, face, coarse >> 7, coarse & 127, cface, sub)):
        facts = jnp.where(row == index, entry, facts)
    facts = facts.astype(F32)
    stacked = jnp.concatenate([facts * hits[k : k + 1] for k in range(9)], axis=0).astype(BF16)
    packed = dot_nt(stacked, one_hot(EB, position))
    for k in range(9):
        own_m[k] = packed[8 * k : 8 * k + 8]
    for side in range(2):
        d = (1, 7)[side]
        own_x[0, side, FACES : FACES + 8, :] = packed[8 * d : 8 * d + 8]
    for index, d in enumerate(EDGE_DIRS):
        own_y[0, index, FR : FR + 8, :] = packed[8 * d : 8 * d + 8]
    scale = jnp.where(level == 0, 1.0, jnp.where(level == 1, 0.5, 0.25))

    def face_product(table, value):
        high, low = split(value)
        return dot(table, high) + dot(table, low)

    def edge_values(faces):
        ends = faces[:, 0:EB]
        for a in range(1, EA):
            moved = pltpu.roll(faces[:, a * EB : (a + 1) * EB], 2 * a, 1)
            ends = jnp.where((lane == 2 * a) | (lane == 2 * a - 1), moved, ends)
        own = jnp.zeros((FR, 128), F32)
        for f in range(6):
            moved = pltpu.roll(ends[f * FR : (f + 1) * FR], 16 * f + 1, 1)
            own = jnp.where((lane_face == f) & (lane_pair < 8), moved, own)
        rows = own
        for pair, by in CORNER_SHIFT.items():
            own = jnp.where(lane_pair == pair, pltpu.roll(rows, by, 1), own)
        return own

    def edge_spread(values):
        rows = jnp.where(lane_pair < 8, values, 0.0)
        for pair, by in CORNER_SHIFT.items():
            rows = rows + jnp.where(lane_pair == pair - by, pltpu.roll(values, 128 - by, 1), 0.0)
        ends = jnp.concatenate([pltpu.roll(rows, 127 - 16 * f, 1) for f in range(6)], axis=0)
        tiles = []
        for a in range(EA):
            moved = pltpu.roll(ends, 128 - 2 * a, 1) if a else ends
            tiles.append(jnp.where((lane == 0) | (lane == EB - 1), moved, 0.0))
        return tiles

    def publish(t, faces):
        own_x[t, 0, 0:FACES, :] = faces[:, 0:EB]
        own_x[t, 1, 0:FACES, :] = faces[:, (EA - 1) * EB :]
        own = edge_values(faces)
        for index in range(6 if t == 0 else 1):
            own_y[t, index, 0:FR, :] = own
        return own

    for load in loads[7:9]:
        load.wait()
    b = b_ref[...]
    faces = face_product(pick_ref[...], b)
    own = publish(0, faces)

    pl.semaphore_wait(barrier, expected)
    send(0)

    for load in loads[9:]:
        load.wait()
    for d in range(3):
        padded = jnp.concatenate([stiff_ref[d], jnp.zeros((SP - NODES, NODES), F32)], axis=0)
        high, low = split(padded)
        stiff_s[d * SP : (d + 1) * SP, :] = high
        stiff_s[(3 + d) * SP : (4 + d) * SP, :] = low
    proj_s[...] = jnp.zeros_like(proj_s)
    proj_c[...] = jnp.zeros_like(proj_c)
    for s in range(4):
        table = proj_ref[:, s, :]
        proj_s[s * FR : s * FR + SIDE, 0:SIDE] = table
        proj_c[0:SIDE, s * FR : s * FR + SIDE] = table
    proj_t[...] = proj_s[...].T[0:FR]
    table_s = stacked_table(proj_s[0 : 4 * FR, 0:FR])
    table_c = stacked_table(proj_c[:, 0 : 4 * FR])
    table_t = stacked_table(proj_t[:, 0 : 4 * FR])

    me = own_m[4]
    self_fine = code(me[0:1] * float(EB) + me[1:2], me[7:8])
    self_coarse = code(me[3:4] * float(EB) + me[4:5], me[7:8])
    oh_self[...] = one_hot(ELEMS, jnp.concatenate([self_fine, self_coarse], axis=1))

    wide = iota((32, 512), 1)
    repeat = jnp.where(iota((32, 512), 0) == (wide >> 7) * 8 + ((wide >> 4) & 7), 1.0, 0.0).astype(BF16)
    same_pair = (iota((128, 512), 0) & 15) == (iota((128, 512), 1) & 15)
    ones = jnp.ones((16, 6 * EB), BF16)

    def edge_counts(held):
        parts_f, parts_c = [], []
        for d, facts_d in zip(EDGE_DIRS, held):
            if d in (3, 5):
                pair = facts_d[0:1] * 2.0 + (1.0 if d == 3 else 0.0)
            else:
                pair = float(CORNERS[d])
            parts_f.append(code(facts_d[2:3] * 16.0 + pair, facts_d[7:8]))
            parts_c.append(code(facts_d[6:7] * 8.0 + facts_d[5:6], facts_d[7:8]))
        fine_hot = one_hot(128, jnp.concatenate(parts_f, axis=1))
        coarse_hot = one_hot(32, jnp.concatenate(parts_c, axis=1))
        joined = dot(dot_nt(fine_hot, coarse_hot).astype(BF16), repeat)
        return jnp.where(same_pair, joined, 0.0).astype(BF16), dot_nt(ones, fine_hot)[0:1]

    n_out[...], sum_out = edge_counts([own_m[d] for d in EDGE_DIRS])

    def mortar_jump(coarses, fines, subs):
        high = coarses.astype(BF16).astype(F32)
        return by_table(table_c, by_subface(high, subs), by_subface(coarses - high, subs)) - fines

    def mortar_back(jump, subs):
        high = jump.astype(BF16).astype(F32)
        return by_table(table_t, by_subface(high, subs), by_subface(jump - high, subs))

    def local_part(field, faces):
        f_h, f_l = split(faces)
        got = dot(f_h, oh_self[...]) + dot(f_l, oh_self[...])
        jump = mortar_jump(pick_face(got[:, EB:], me[5:6]), pick_face(got[:, 0:EB], me[2:3]), me[6:7])
        back = mortar_back(jump, me[6:7])
        terms = jnp.concatenate([-PENALTY * jump, PENALTY * back], axis=1)
        s_h, s_l = spread_split(terms, jnp.concatenate([me[2:3], me[5:6]], axis=1))
        gathered = dot_nt(s_h, oh_self[...]) + dot_nt(s_l, oh_self[...])

        blocks = []
        for a in range(EA):
            here = slice(a * EB, (a + 1) * EB)
            x_low, x_high = faces[0:FR, here], faces[FR : 2 * FR, here]
            y_low, y_high = faces[2 * FR : 3 * FR, here], faces[3 * FR : 4 * FR, here]
            left = x_low if a == 0 else x_low - faces[FR : 2 * FR, (a - 1) * EB : a * EB]
            right = x_high if a == EA - 1 else x_high - faces[0:FR, (a + 1) * EB : (a + 2) * EB]
            below = jnp.where(lane == 0, 0.0, pltpu.roll(y_high, 1, 1))
            above = jnp.where(lane == EB - 1, 0.0, pltpu.roll(y_low, EB - 1, 1))
            lateral = jnp.concatenate([left, right, y_low - below, y_high - above], axis=0)
            blocks.append(jnp.concatenate([PENALTY * lateral, jnp.zeros((2 * FR, EB), F32)], axis=0))
        gathered = gathered + jnp.concatenate(blocks, axis=1)

        field_h, field_l = split(field)
        both = dot(stiff_s[...], field_h)
        rest = dot(stiff_s[0 : 3 * SP, :], field_l)
        total = field
        for d in range(3):
            here = slice(d * SP, d * SP + NODES)
            again = slice((3 + d) * SP, (3 + d) * SP + NODES)
            total = total + metric_ref[d : d + 1, :] * (both[here] + both[again] + rest[here])
        return scale * total, gathered

    def side_jumps(t, faces):
        for side in range(2):
            if_there((1, 7)[side], lambda: x_copy(t, side, True).wait_recv())
        if t == 0:
            for side in range(2):
                d = (1, 7)[side]
                both = jnp.concatenate([own_m[d], halo_x[0, side, FACES : FACES + 8, :]], axis=1)
                oh_x[side] = one_hot(EB, code(both[1:2], both[7:8]))
        fines, coarses, subs = [], [], []
        for side in range(2):
            d = (1, 7)[side]
            theirs_m = halo_x[0, side, FACES : FACES + 8, :]
            here = slice(0, EB) if side == 0 else slice((EA - 1) * EB, EA * EB)
            pair = jnp.concatenate([faces[:, here], halo_x[t, side, 0:FACES, :]], axis=0)
            high, low = split(pair)
            got = dot(high, oh_x[side]) + dot(low, oh_x[side])
            ours, theirs = got[0:FACES], got[FACES:]
            fines += [pick_face(ours[:, 0:EB], own_m[d][2:3]), pick_face(theirs[:, EB:], theirs_m[2:3])]
            coarses += [pick_face(theirs[:, 0:EB], own_m[d][5:6]), pick_face(ours[:, EB:], theirs_m[5:6])]
            subs += [own_m[d][6:7], theirs_m[6:7]]
        jump = mortar_jump(*(jnp.concatenate(parts, axis=1) for parts in (coarses, fines, subs)))
        jump = [jump[:, k * EB : (k + 1) * EB] for k in range(4)]
        energy = jnp.zeros((FR, EB), F32)
        for side in range(2):
            energy = energy - PENALTY * jump[2 * side] * fines[2 * side]
            energy = energy + PENALTY * jump[2 * side + 1] * (jump[2 * side + 1] + fines[2 * side + 1])
        energy = energy - PENALTY * faces[0:FR, 0:EB] * halo_x[t, 0, FR : 2 * FR, :]
        energy = energy - PENALTY * faces[FR : 2 * FR, (EA - 1) * EB :] * halo_x[t, 1, 0:FR, :]
        return jump, subs, jnp.sum(energy, axis=0, keepdims=True)

    def side_terms(t, jump, subs):
        back = mortar_back(jnp.concatenate([jump[1], jump[3]], axis=1), jnp.concatenate([subs[1], subs[3]], axis=1))
        result = []
        for side in range(2):
            d = (1, 7)[side]
            terms = jnp.concatenate(
                [-PENALTY * jump[2 * side], PENALTY * back[:, side * EB : (side + 1) * EB]], axis=1
            )
            theirs_m = halo_x[0, side, FACES : FACES + 8, :]
            s_h, s_l = spread_split(terms, jnp.concatenate([own_m[d][2:3], theirs_m[5:6]], axis=1))
            side_term = dot_nt(s_h, oh_x[side]) + dot_nt(s_l, oh_x[side])
            if side == 0:
                beside = [-PENALTY * halo_x[t, 0, FR : 2 * FR, :], jnp.zeros((5 * FR, EB), F32)]
            else:
                beside = [jnp.zeros((FR, EB), F32), -PENALTY * halo_x[t, 1, 0:FR, :], jnp.zeros((4 * FR, EB), F32)]
            result.append(side_term + jnp.concatenate(beside, axis=0))
        return result

    def edge_jumps(t, own, sum_in):
        for index in range(6):
            if_there(EDGE_DIRS[index], lambda: y_copy(t, index, True).wait_recv())
        if t == 0:
            n_in[...], _ = edge_counts([halo_y[0, index, FR : FR + 8, :] for index in range(6)])
            sum_in = dot(jnp.ones((16, 128), BF16), n_in[...])[0:1]
        across = jnp.zeros((FR, 128), F32)
        for index, turn in enumerate((1, -1, -3, -1, 1, 3)):
            moved = pltpu.roll(halo_y[t, index, 0:FR, :], turn % 128, 1)
            if index < 2:
                across = jnp.where((lane_pair < 8) & ((lane_pair & 1) == 1 - index), moved, across)
            else:
                across = jnp.where(lane_pair == CORNERS[EDGE_DIRS[index]], moved, across)
        pairs = jnp.concatenate([own, across], axis=1)
        pairs_h, pairs_l = split(pairs)
        images = by_table(table_s, pairs_h, pairs_l)
        image_own = jnp.concatenate([images[s * FR : (s + 1) * FR, 0:128] for s in range(4)], axis=1)
        image_far = jnp.concatenate([images[s * FR : (s + 1) * FR, 128:] for s in range(4)], axis=1)
        far_h, far_l = split(image_far)
        on_fine = own * sum_out - dot_nt(far_h, n_out[...]) - dot_nt(far_l, n_out[...])
        jumps = image_own * sum_in - dot(pairs_h[:, 128:], n_in[...]) - dot(pairs_l[:, 128:], n_in[...])
        from_low = pltpu.roll(across, 128 - 16, 1)
        from_high = pltpu.roll(across, 16, 1)
        beside = jnp.where(
            (lane_face == 2) & (lane_pair < 8) & ((lane_pair & 1) == 1),
            from_low,
            jnp.where((lane_face == 3) & (lane_pair < 8) & ((lane_pair & 1) == 0), from_high, 0.0),
        )
        direct = PENALTY * (on_fine - beside)
        energy = jnp.sum(own * direct, axis=0, keepdims=True)
        both = PENALTY * jnp.sum(image_own * jumps, axis=0, keepdims=True)
        energy = energy + sum(both[:, s * 128 : (s + 1) * 128] for s in range(4))
        return direct, jumps, energy, sum_in

    def edge_terms(direct, jumps):
        jumps = jnp.concatenate([jumps[:, s * 128 : (s + 1) * 128] for s in range(4)], axis=0)
        jumps_h, jumps_l = split(jumps)
        return edge_spread(direct + PENALTY * by_table(table_t, jumps_h, jumps_l))

    def placed(value):
        return face_product(place_ref[...], value)

    b = b_ref[...]
    total, gathered = local_part(b, faces)
    total = total + placed(gathered)
    started = face_product(pick_ref[...], total)
    jump, subs, _ = side_jumps(0, faces)
    sides = side_terms(0, jump, subs)
    direct, jumps, _, sum_in = edge_jumps(0, own, None)
    tiles = edge_terms(direct, jumps)
    tiles[0] = tiles[0] + sides[0]
    tiles[EA - 1] = tiles[EA - 1] + sides[1]
    remote = jnp.concatenate(tiles, axis=1)
    faces = started + face_product(mix_ref[...], remote)
    own = publish(1, faces)
    send(1)
    q = total + placed(remote)
    q_ref[...] = q

    total, gathered = local_part(q, faces)
    b = b_ref[...]
    q = q_ref[...]
    early = [column_sums(b, b), column_sums(b, q), column_sums(q, q)]
    energy = column_sums(q, total) + column_sums(faces, gathered)
    jump, subs, more = side_jumps(1, faces)
    energy = energy + more
    direct, jumps, more, _ = edge_jumps(1, own, sum_in)
    energy = energy + more

    lanes = jnp.zeros((1, 128), F32)
    for index, sums in enumerate(early + [energy]):
        lanes = jnp.where(lane == index, jnp.sum(sums, axis=1, keepdims=True), lanes)
    mine0[...] = lanes
    core = pltpu.make_async_remote_copy(
        src_ref=mine0,
        dst_ref=red0,
        send_sem=s0_send,
        recv_sem=s0_recv,
        device_id={"gx": gx + 1 - 2 * lax.rem(gx, 2), "gy": gy},
        device_id_type=MESH,
    )
    core.start()
    core.wait_recv()
    lanes = mine0[...] + red0[...]
    mine1[...] = lanes
    for k, offset in enumerate(chips):
        pltpu.make_async_remote_copy(
            src_ref=mine1,
            dst_ref=red1.at[k],
            send_sem=s1_send,
            recv_sem=s1_recv,
            device_id=chip(offset),
            device_id_type=MESH,
        ).start()

    sides = side_terms(1, jump, subs)
    tiles = edge_terms(direct, jumps)
    tiles[0] = tiles[0] + sides[0]
    tiles[EA - 1] = tiles[EA - 1] + sides[1]
    w_ref[...] = total + placed(gathered + jnp.concatenate(tiles, axis=1))
    for t in range(2):
        for side in range(2):
            if_there((1, 7)[side], lambda: x_copy(t, side, False).wait_send())
        for index in range(6):
            if_there(EDGE_DIRS[index], lambda: y_copy(t, index, False).wait_send())
    core.wait_send()

    pltpu.make_async_copy(red1, red1, s1_recv).wait()
    lanes = lanes + jnp.sum(red1[...], axis=0)
    bb, bq, qq, qw = (lanes[:, i : i + 1] for i in range(4))
    alpha = bb / bq
    new = bb - 2.0 * alpha * bq + alpha * alpha * qq
    grow = 1.0 + new / bb
    alpha_next = new / (grow * grow * bq - 2.0 * grow * alpha * qq + alpha * alpha * qw)
    row = iota((8, 128), 0)
    coef_ref[...] = jnp.where(row == 0, alpha + alpha_next * grow, alpha * alpha_next)
    pltpu.make_async_copy(red1, red1, s1_send).wait()


def finish(coef_ref, b_ref, q_ref, w_ref, x_hbm, r_hbm, made, out_sem):
    first, second = coef_ref[0:1, 0:1], coef_ref[1:2, 0:1]
    stores = []
    for part, (start, size) in enumerate(((0, 104), (104, NODES - 104))):
        rows = pl.ds(start, size)
        b, q, w = b_ref[rows, :], q_ref[rows, :], w_ref[rows, :]
        made[0, rows, :] = first * b - second * q
        made[1, rows, :] = b - first * q + second * w
        for k, target in enumerate((x_hbm, r_hbm)):
            store = pltpu.make_async_copy(made.at[k, rows], target.at[rows], out_sem.at[part, k])
            store.start()
            stores.append(store)
    for store in stores:
        store.wait()


def body(
    n_gx,
    n_gy,
    right_side,
    stiffness,
    metric,
    levels,
    projection,
    mortar_fine,
    mortar_face,
    mortar_owner,
    mortar_subface,
    mortar_coarse,
    mortar_cface,
):
    pick, place, mix = (jnp.asarray(table, BF16) for table in constant_tables())
    field = jax.ShapeDtypeStruct(right_side.shape, F32)
    count = mortar_fine.shape[0]
    others = n_gx // 2 * n_gy - 1
    hbm = pl.BlockSpec(memory_space=pltpu.HBM)
    vmem = pl.BlockSpec(memory_space=pltpu.VMEM)
    dma = pltpu.SemaphoreType.DMA
    line = [
        entry.reshape(1, count)
        for entry in (
            mortar_fine,
            mortar_face,
            mortar_owner,
            mortar_subface,
            mortar_coarse,
            mortar_cface,
            levels,
        )
    ]
    q, w, coef = pl.pallas_call(
        functools.partial(kernel, n_gx, n_gy),
        out_shape=(field, field, jax.ShapeDtypeStruct((8, 128), F32)),
        in_specs=[hbm] * 14,
        out_specs=(vmem, vmem, vmem),
        scratch_shapes=[
            pltpu.VMEM((NODES, ELEMS), F32),
            pltpu.VMEM((3, NODES, NODES), F32),
            pltpu.VMEM((3, ELEMS), F32),
            pltpu.VMEM((7, 1, ELEMS), jnp.int32),
            pltpu.VMEM((SIDE, 4, SIDE), F32),
            pltpu.VMEM((FACES, NODES), BF16),
            pltpu.VMEM((NODES, FACES), BF16),
            pltpu.VMEM((FACES, FACES), BF16),
            pltpu.VMEM((2, 2, FACES + 8, EB), F32),
            pltpu.VMEM((2, 6, FR + 8, 128), F32),
            pltpu.VMEM((9, 8, 128), F32),
            pltpu.VMEM((2, 2, FACES + 8, EB), F32),
            pltpu.VMEM((2, 6, FR + 8, 128), F32),
            pltpu.VMEM((6 * SP, NODES), BF16),
            pltpu.VMEM((ELEMS, 2 * EB), BF16),
            pltpu.VMEM((2, EB, 2 * EB), BF16),
            pltpu.VMEM((128, 512), BF16),
            pltpu.VMEM((128, 512), BF16),
            pltpu.VMEM((256, 128), F32),
            pltpu.VMEM((FR, 256), F32),
            pltpu.VMEM((FR, 256), F32),
            pltpu.VMEM((1, 128), F32),
            pltpu.VMEM((others, 1, 128), F32),
            pltpu.VMEM((1, 128), F32),
            pltpu.VMEM((1, 128), F32),
            dma((14,)),
            dma((2, 2)),
            dma((2, 2)),
            dma((2, 6)),
            dma((2, 6)),
            dma,
            dma,
            dma,
            dma,
        ],
        compiler_params=pltpu.CompilerParams(
            collective_id=0, has_side_effects=True, vmem_limit_bytes=40 * 1024 * 1024
        ),
    )(
        *(
            pltpu.with_memory_space_constraint(operand, pltpu.HBM)
            for operand in (right_side, stiffness, metric, *line, projection.transpose(1, 0, 2), pick, place, mix)
        )
    )
    return pl.pallas_call(
        finish,
        out_shape=(field, field),
        in_specs=[vmem] * 4,
        out_specs=(hbm, hbm),
        scratch_shapes=[pltpu.VMEM((2, NODES, ELEMS), F32), dma((2, 2))],
        compiler_params=pltpu.CompilerParams(vmem_limit_bytes=40 * 1024 * 1024),
    )(coef, right_side, q, w)


def solution(mesh):
    columns = P(None, ("gx", "gy"))
    faces = P(("gx", "gy"))
    in_specs = (columns, P(), columns, faces, P(), faces, faces, P(("gx", "gy"), None), faces, faces, faces)
    run = functools.partial(body, mesh.shape["gx"], mesh.shape["gy"])
    return jax.shard_map(run, mesh=mesh, in_specs=in_specs, out_specs=(columns, columns), check_vma=False)
```

```python
import functools

import jax
import jax.numpy as jnp
import numpy as np
from jax import lax
from jax.experimental import pallas as pl
from jax.experimental.pallas import tpu as pltpu
from jax.sharding import PartitionSpec as P

NP = 6
NODES = NP * NP * NP
SIDE = NP * NP
EA = 4
EB = 128
ELEMS = EA * EB
FR = 40
FACES = 6 * FR
SP = 224
PENALTY = 1.0

F32 = jnp.float32
BF16 = jnp.bfloat16
MESH = pl.DeviceIdType.MESH

DIRS = {d: (d // 3 - 1, d % 3 - 1) for d in range(9) if d != 4}
EDGE_DIRS = (3, 5, 0, 2, 6, 8)
CORNERS = {0: 8, 2: 9, 6: 10, 8: 11}
CORNER_SHIFT = {8: 7, 9: 9, 10: 3, 11: 5}


def face_nodes(face):
    ids = np.arange(NODES).reshape(NP, NP, NP)
    return [ids[0], ids[5], ids[:, 0], ids[:, 5], ids[:, :, 0], ids[:, :, 5]][face].reshape(-1)


def constant_tables():
    pick = np.zeros((FACES, NODES), np.float32)
    for face in range(6):
        pick[face * FR + np.arange(SIDE), face_nodes(face)] = 1.0
    return pick, pick.T.copy(), pick @ pick.T


def dot(a, b):
    return lax.dot_general(a, b, (((1,), (0,)), ((), ())), preferred_element_type=F32)


def dot_nt(a, b):
    return lax.dot_general(a, b, (((1,), (1,)), ((), ())), preferred_element_type=F32)


def split(value):
    high = value.astype(BF16)
    return high, (value - high.astype(F32)).astype(BF16)


def iota(shape, dim):
    return lax.broadcasted_iota(jnp.int32, shape, dim)


def one_hot(rows, code):
    return jnp.where(iota((rows, code.shape[1]), 0).astype(F32) == code, 1.0, 0.0).astype(BF16)


def pick_face(sides, face):
    out = None
    for f in range(6):
        part = jnp.where(face == float(f), sides[f * FR : (f + 1) * FR], 0.0)
        out = part if out is None else out + part
    return out


def spread_face(values, face):
    return jnp.concatenate([jnp.where(face == float(f), values, 0.0) for f in range(6)], axis=0)


def spread_split(values, face):
    high = values.astype(BF16).astype(F32)
    return spread_face(high, face).astype(BF16), spread_face(values - high, face).astype(BF16)


def by_subface(values, sub):
    return jnp.concatenate([jnp.where(sub == float(s), values, 0.0) for s in range(4)], axis=0).astype(BF16)


def column_sums(a, b):
    prod = a * b
    rows = jnp.sum(prod, axis=0, keepdims=True)
    return sum(rows[:, t * EB : (t + 1) * EB] for t in range(EA))


def kernel(
    n_gx,
    n_gy,
    b_hbm,
    stiff_hbm,
    metric_hbm,
    fine_hbm,
    face_hbm,
    owner_hbm,
    sub_hbm,
    coarse_hbm,
    cface_hbm,
    level_hbm,
    proj_hbm,
    pick_hbm,
    place_hbm,
    mix_hbm,
    q_ref,
    w_ref,
    coef_ref,
    b_ref,
    stiff_ref,
    metric_ref,
    ints_ref,
    proj_ref,
    pick_ref,
    place_ref,
    mix_ref,
    halo_x,
    halo_y,
    own_m,
    own_x,
    own_y,
    stiff_s,
    oh_self,
    oh_x,
    n_out,
    n_in,
    proj_s,
    proj_c,
    proj_t,
    red1,
    mine0,
    in_sem,
    sx_send,
    sx_recv,
    sy_send,
    sy_recv,
    ready_sem,
    s1_send,
    s1_recv,
):
    gx = lax.axis_index("gx")
    gy = lax.axis_index("gy")

    int_names = (fine_hbm, face_hbm, owner_hbm, sub_hbm, coarse_hbm, cface_hbm, level_hbm)
    loads = [(source, ints_ref.at[k]) for k, source in enumerate(int_names)]
    loads += [(b_hbm, b_ref), (pick_hbm, pick_ref), (proj_hbm, proj_ref), (mix_hbm, mix_ref)]
    loads += [(stiff_hbm, stiff_ref), (metric_hbm, metric_ref), (place_hbm, place_ref)]
    loads = [pltpu.make_async_copy(source, target, in_sem.at[k]) for k, (source, target) in enumerate(loads)]
    for load in loads:
        load.start()

    def there(d):
        dx, dy = DIRS[d]
        ok = (gx + dx >= 0) & (gx + dx < n_gx) & (gy + dy >= 0) & (gy + dy < n_gy)
        return ok, {"gx": gx + dx, "gy": gy + dy}

    def if_there(d, act):
        pl.when(there(d)[0])(act)

    size_x, size_y, size_z = n_gx // 2, n_gy // 4, 4
    chips = [(i, j, k) for i in range(size_x) for j in range(size_y) for k in range(size_z)][1:]
    chips.sort(key=lambda c: sum((v - 1) % n for v, n in zip(c, (size_x, size_y, size_z))))

    def chip(offset):
        y, z = gy // size_z, lax.rem(gy, size_z)
        return {
            "gx": lax.rem(gx + 2 * offset[0], n_gx),
            "gy": lax.rem(y + offset[1], size_y) * size_z + lax.rem(z + offset[2], size_z),
        }

    halo_x[...] = jnp.zeros_like(halo_x)
    halo_y[...] = jnp.zeros_like(halo_y)

    barrier = pltpu.get_barrier_semaphore()
    expected = jnp.int32(0)
    for d in DIRS:
        ok, where = there(d)

        @pl.when(ok)
        def _():
            pl.semaphore_signal(barrier, inc=1, device_id=where, device_id_type=MESH)

        expected = expected + ok.astype(jnp.int32)

    def x_copy(t, side, arriving):
        slot = side if arriving else 1 - side
        rows = pl.ds(0, FACES + 8 * (1 - t))
        return pltpu.make_async_remote_copy(
            src_ref=own_x.at[t, side, rows],
            dst_ref=halo_x.at[t, slot, rows],
            send_sem=sx_send.at[t, side],
            recv_sem=sx_recv.at[t, slot],
            device_id=there((1, 7)[side])[1],
            device_id_type=MESH,
        )

    def y_copy(t, index, arriving):
        d = EDGE_DIRS[index]
        slot = index if arriving else EDGE_DIRS.index(8 - d)
        rows = pl.ds(0, FR + 8 * (1 - t))
        return pltpu.make_async_remote_copy(
            src_ref=own_y.at[t, index if t == 0 else 0, rows],
            dst_ref=halo_y.at[t, slot, rows],
            send_sem=sy_send.at[t, index],
            recv_sem=sy_recv.at[t, slot],
            device_id=there(d)[1],
            device_id_type=MESH,
        )

    rounds = [("gx", k) for k in (1, 2, 4, 8, 16) if k < n_gx] + [("gy", k) for k in (1, 2, 4, 8, 16) if k < n_gy]

    def partners(k):
        axis, by = rounds[k]
        for step in (-by, by):
            if axis == "gx":
                yield (gx + step >= 0) & (gx + step < n_gx), {"gx": gx + step, "gy": gy}
            else:
                yield (gy + step >= 0) & (gy + step < n_gy), {"gx": gx, "gy": gy + step}

    def pass_on(k):
        for ok, where in partners(k):

            @pl.when(ok)
            def _():
                pl.semaphore_signal(ready_sem.at[k], inc=1, device_id=where, device_id_type=MESH)

    pending = list(range(len(rounds)))

    def learn():
        if pending:
            k = pending.pop(0)
            pl.semaphore_wait(ready_sem.at[k], sum(ok.astype(jnp.int32) for ok, _ in partners(k)))
            if pending:
                pass_on(k + 1)

    def send(t):
        for index in (2, 3, 4, 5, 0, 1):
            if_there(EDGE_DIRS[index], lambda: y_copy(t, index, False).start())
        for side in range(2):
            if_there((1, 7)[side], lambda: x_copy(t, side, False).start())

    lane = iota((1, 128), 1)
    lane_face = lane >> 4
    lane_pair = lane & 15

    def stacked_table(value):
        high = value.astype(BF16)
        rest = value - high.astype(F32)
        return high, jnp.concatenate([high.astype(F32), rest], axis=0).astype(BF16)

    def by_table(table, value_h, value_l):
        high, both = table
        rows = high.shape[0]
        first = dot(both, value_h)
        return first[:rows] + first[rows:] + dot(high, value_l)

    def code(entry, active):
        return jnp.where(active > 0.0, entry, -1.0)

    for load in loads[:7]:
        load.wait()
    fine, face, owner, sub, coarse, cface, level = (ints_ref[k] for k in range(7))
    shift = n_gy.bit_length() - 1
    slot = ((owner >> shift) - gx + 1) * 3 + (owner & (n_gy - 1)) - gy + 1
    count = fine.shape[1]
    hits = jnp.where(iota((16, count), 0) == slot, 1.0, 0.0)
    parts = [hits[:, k : k + EB] for k in range(0, count, EB)]
    earlier = jnp.where(iota((EB, EB), 0) < iota((EB, EB), 1), 1.0, 0.0).astype(BF16)
    within = dot(jnp.concatenate(parts, axis=0).astype(BF16), earlier)
    offset, ranks = jnp.zeros((16, 1), F32), []
    for k, part in enumerate(parts):
        ranks.append(jnp.sum(part * (within[16 * k : 16 * k + 16] + offset), axis=0, keepdims=True))
        offset = offset + jnp.sum(part, axis=1, keepdims=True)
    position = jnp.concatenate(ranks, axis=1)
    row = iota((8, count), 0)
    facts = jnp.ones((8, count), jnp.int32)
    for index, entry in enumerate((fine >> 7, fine & 127, face, coarse >> 7, coarse & 127, cface, sub)):
        facts = jnp.where(row == index, entry, facts)
    facts = facts.astype(F32)
    stacked = jnp.concatenate([facts * hits[k : k + 1] for k in range(9)], axis=0).astype(BF16)
    packed = dot_nt(stacked, one_hot(EB, position))
    for k in range(9):
        own_m[k] = packed[8 * k : 8 * k + 8]
    for side in range(2):
        d = (1, 7)[side]
        own_x[0, side, FACES : FACES + 8, :] = packed[8 * d : 8 * d + 8]
    for index, d in enumerate(EDGE_DIRS):
        own_y[0, index, FR : FR + 8, :] = packed[8 * d : 8 * d + 8]
    scale = jnp.where(level == 0, 1.0, jnp.where(level == 1, 0.5, 0.25))

    def face_product(table, value):
        high, low = split(value)
        return dot(table, high) + dot(table, low)

    def edge_values(faces):
        ends = faces[:, 0:EB]
        for a in range(1, EA):
            moved = pltpu.roll(faces[:, a * EB : (a + 1) * EB], 2 * a, 1)
            ends = jnp.where((lane == 2 * a) | (lane == 2 * a - 1), moved, ends)
        own = jnp.zeros((FR, 128), F32)
        for f in range(6):
            moved = pltpu.roll(ends[f * FR : (f + 1) * FR], 16 * f + 1, 1)
            own = jnp.where((lane_face == f) & (lane_pair < 8), moved, own)
        rows = own
        for pair, by in CORNER_SHIFT.items():
            own = jnp.where(lane_pair == pair, pltpu.roll(rows, by, 1), own)
        return own

    def edge_spread(values):
        rows = jnp.where(lane_pair < 8, values, 0.0)
        for pair, by in CORNER_SHIFT.items():
            rows = rows + jnp.where(lane_pair == pair - by, pltpu.roll(values, 128 - by, 1), 0.0)
        ends = jnp.concatenate([pltpu.roll(rows, 127 - 16 * f, 1) for f in range(6)], axis=0)
        tiles = []
        for a in range(EA):
            moved = pltpu.roll(ends, 128 - 2 * a, 1) if a else ends
            tiles.append(jnp.where((lane == 0) | (lane == EB - 1), moved, 0.0))
        return tiles

    def publish(t, faces):
        own_x[t, 0, 0:FACES, :] = faces[:, 0:EB]
        own_x[t, 1, 0:FACES, :] = faces[:, (EA - 1) * EB :]
        own = edge_values(faces)
        for index in range(6 if t == 0 else 1):
            own_y[t, index, 0:FR, :] = own
        return own

    for load in loads[7:9]:
        load.wait()
    b = b_ref[...]
    faces = face_product(pick_ref[...], b)
    own = publish(0, faces)

    pl.semaphore_wait(barrier, expected)
    send(0)
    pass_on(0)

    for load in loads[9:]:
        load.wait()
    for d in range(3):
        padded = jnp.concatenate([stiff_ref[d], jnp.zeros((SP - NODES, NODES), F32)], axis=0)
        high, low = split(padded)
        stiff_s[d * SP : (d + 1) * SP, :] = high
        stiff_s[(3 + d) * SP : (4 + d) * SP, :] = low
    proj_s[...] = jnp.zeros_like(proj_s)
    proj_c[...] = jnp.zeros_like(proj_c)
    for s in range(4):
        table = proj_ref[:, s, :]
        proj_s[s * FR : s * FR + SIDE, 0:SIDE] = table
        proj_c[0:SIDE, s * FR : s * FR + SIDE] = table
    proj_t[...] = proj_s[...].T[0:FR]
    table_s = stacked_table(proj_s[0 : 4 * FR, 0:FR])
    table_c = stacked_table(proj_c[:, 0 : 4 * FR])
    table_t = stacked_table(proj_t[:, 0 : 4 * FR])

    me = own_m[4]
    self_fine = code(me[0:1] * float(EB) + me[1:2], me[7:8])
    self_coarse = code(me[3:4] * float(EB) + me[4:5], me[7:8])
    oh_self[...] = one_hot(ELEMS, jnp.concatenate([self_fine, self_coarse], axis=1))

    wide = iota((32, 512), 1)
    repeat = jnp.where(iota((32, 512), 0) == (wide >> 7) * 8 + ((wide >> 4) & 7), 1.0, 0.0).astype(BF16)
    same_pair = (iota((128, 512), 0) & 15) == (iota((128, 512), 1) & 15)
    ones = jnp.ones((16, 6 * EB), BF16)

    def edge_counts(held):
        parts_f, parts_c = [], []
        for d, facts_d in zip(EDGE_DIRS, held):
            if d in (3, 5):
                pair = facts_d[0:1] * 2.0 + (1.0 if d == 3 else 0.0)
            else:
                pair = float(CORNERS[d])
            parts_f.append(code(facts_d[2:3] * 16.0 + pair, facts_d[7:8]))
            parts_c.append(code(facts_d[6:7] * 8.0 + facts_d[5:6], facts_d[7:8]))
        fine_hot = one_hot(128, jnp.concatenate(parts_f, axis=1))
        coarse_hot = one_hot(32, jnp.concatenate(parts_c, axis=1))
        joined = dot(dot_nt(fine_hot, coarse_hot).astype(BF16), repeat)
        return jnp.where(same_pair, joined, 0.0).astype(BF16), dot_nt(ones, fine_hot)[0:1]

    learn()
    n_out[...], sum_out = edge_counts([own_m[d] for d in EDGE_DIRS])

    def mortar_jump(coarses, fines, subs):
        high = coarses.astype(BF16).astype(F32)
        return by_table(table_c, by_subface(high, subs), by_subface(coarses - high, subs)) - fines

    def mortar_back(jump, subs):
        high = jump.astype(BF16).astype(F32)
        return by_table(table_t, by_subface(high, subs), by_subface(jump - high, subs))

    def local_part(field, faces):
        f_h, f_l = split(faces)
        got = dot(f_h, oh_self[...]) + dot(f_l, oh_self[...])
        jump = mortar_jump(pick_face(got[:, EB:], me[5:6]), pick_face(got[:, 0:EB], me[2:3]), me[6:7])
        back = mortar_back(jump, me[6:7])
        terms = jnp.concatenate([-PENALTY * jump, PENALTY * back], axis=1)
        s_h, s_l = spread_split(terms, jnp.concatenate([me[2:3], me[5:6]], axis=1))
        gathered = dot_nt(s_h, oh_self[...]) + dot_nt(s_l, oh_self[...])

        blocks = []
        for a in range(EA):
            here = slice(a * EB, (a + 1) * EB)
            x_low, x_high = faces[0:FR, here], faces[FR : 2 * FR, here]
            y_low, y_high = faces[2 * FR : 3 * FR, here], faces[3 * FR : 4 * FR, here]
            left = x_low if a == 0 else x_low - faces[FR : 2 * FR, (a - 1) * EB : a * EB]
            right = x_high if a == EA - 1 else x_high - faces[0:FR, (a + 1) * EB : (a + 2) * EB]
            below = jnp.where(lane == 0, 0.0, pltpu.roll(y_high, 1, 1))
            above = jnp.where(lane == EB - 1, 0.0, pltpu.roll(y_low, EB - 1, 1))
            lateral = jnp.concatenate([left, right, y_low - below, y_high - above], axis=0)
            blocks.append(jnp.concatenate([PENALTY * lateral, jnp.zeros((2 * FR, EB), F32)], axis=0))
        gathered = gathered + jnp.concatenate(blocks, axis=1)

        field_h, field_l = split(field)
        both = dot(stiff_s[...], field_h)
        rest = dot(stiff_s[0 : 3 * SP, :], field_l)
        total = field
        for d in range(3):
            here = slice(d * SP, d * SP + NODES)
            again = slice((3 + d) * SP, (3 + d) * SP + NODES)
            total = total + metric_ref[d : d + 1, :] * (both[here] + both[again] + rest[here])
        return scale * total, gathered

    def side_jumps(t, faces):
        for side in range(2):
            if_there((1, 7)[side], lambda: x_copy(t, side, True).wait_recv())
        if t == 0:
            for side in range(2):
                d = (1, 7)[side]
                both = jnp.concatenate([own_m[d], halo_x[0, side, FACES : FACES + 8, :]], axis=1)
                oh_x[side] = one_hot(EB, code(both[1:2], both[7:8]))
        fines, coarses, subs = [], [], []
        for side in range(2):
            d = (1, 7)[side]
            theirs_m = halo_x[0, side, FACES : FACES + 8, :]
            here = slice(0, EB) if side == 0 else slice((EA - 1) * EB, EA * EB)
            pair = jnp.concatenate([faces[:, here], halo_x[t, side, 0:FACES, :]], axis=0)
            high, low = split(pair)
            got = dot(high, oh_x[side]) + dot(low, oh_x[side])
            ours, theirs = got[0:FACES], got[FACES:]
            fines += [pick_face(ours[:, 0:EB], own_m[d][2:3]), pick_face(theirs[:, EB:], theirs_m[2:3])]
            coarses += [pick_face(theirs[:, 0:EB], own_m[d][5:6]), pick_face(ours[:, EB:], theirs_m[5:6])]
            subs += [own_m[d][6:7], theirs_m[6:7]]
        jump = mortar_jump(*(jnp.concatenate(parts, axis=1) for parts in (coarses, fines, subs)))
        jump = [jump[:, k * EB : (k + 1) * EB] for k in range(4)]
        energy = jnp.zeros((FR, EB), F32)
        for side in range(2):
            energy = energy - PENALTY * jump[2 * side] * fines[2 * side]
            energy = energy + PENALTY * jump[2 * side + 1] * (jump[2 * side + 1] + fines[2 * side + 1])
        energy = energy - PENALTY * faces[0:FR, 0:EB] * halo_x[t, 0, FR : 2 * FR, :]
        energy = energy - PENALTY * faces[FR : 2 * FR, (EA - 1) * EB :] * halo_x[t, 1, 0:FR, :]
        return jump, subs, jnp.sum(energy, axis=0, keepdims=True)

    def side_terms(t, jump, subs):
        back = mortar_back(jnp.concatenate([jump[1], jump[3]], axis=1), jnp.concatenate([subs[1], subs[3]], axis=1))
        result = []
        for side in range(2):
            d = (1, 7)[side]
            terms = jnp.concatenate(
                [-PENALTY * jump[2 * side], PENALTY * back[:, side * EB : (side + 1) * EB]], axis=1
            )
            theirs_m = halo_x[0, side, FACES : FACES + 8, :]
            s_h, s_l = spread_split(terms, jnp.concatenate([own_m[d][2:3], theirs_m[5:6]], axis=1))
            side_term = dot_nt(s_h, oh_x[side]) + dot_nt(s_l, oh_x[side])
            if side == 0:
                beside = [-PENALTY * halo_x[t, 0, FR : 2 * FR, :], jnp.zeros((5 * FR, EB), F32)]
            else:
                beside = [jnp.zeros((FR, EB), F32), -PENALTY * halo_x[t, 1, 0:FR, :], jnp.zeros((4 * FR, EB), F32)]
            result.append(side_term + jnp.concatenate(beside, axis=0))
        return result

    def edge_jumps(t, own, sum_in):
        for index in range(6):
            if_there(EDGE_DIRS[index], lambda: y_copy(t, index, True).wait_recv())
        if t == 0:
            n_in[...], _ = edge_counts([halo_y[0, index, FR : FR + 8, :] for index in range(6)])
            sum_in = dot(jnp.ones((16, 128), BF16), n_in[...])[0:1]
        across = jnp.zeros((FR, 128), F32)
        for index, turn in enumerate((1, -1, -3, -1, 1, 3)):
            moved = pltpu.roll(halo_y[t, index, 0:FR, :], turn % 128, 1)
            if index < 2:
                across = jnp.where((lane_pair < 8) & ((lane_pair & 1) == 1 - index), moved, across)
            else:
                across = jnp.where(lane_pair == CORNERS[EDGE_DIRS[index]], moved, across)
        pairs = jnp.concatenate([own, across], axis=1)
        pairs_h, pairs_l = split(pairs)
        images = by_table(table_s, pairs_h, pairs_l)
        image_own = jnp.concatenate([images[s * FR : (s + 1) * FR, 0:128] for s in range(4)], axis=1)
        image_far = jnp.concatenate([images[s * FR : (s + 1) * FR, 128:] for s in range(4)], axis=1)
        far_h, far_l = split(image_far)
        on_fine = own * sum_out - dot_nt(far_h, n_out[...]) - dot_nt(far_l, n_out[...])
        jumps = image_own * sum_in - dot(pairs_h[:, 128:], n_in[...]) - dot(pairs_l[:, 128:], n_in[...])
        from_low = pltpu.roll(across, 128 - 16, 1)
        from_high = pltpu.roll(across, 16, 1)
        beside = jnp.where(
            (lane_face == 2) & (lane_pair < 8) & ((lane_pair & 1) == 1),
            from_low,
            jnp.where((lane_face == 3) & (lane_pair < 8) & ((lane_pair & 1) == 0), from_high, 0.0),
        )
        direct = PENALTY * (on_fine - beside)
        energy = jnp.sum(own * direct, axis=0, keepdims=True)
        both = PENALTY * jnp.sum(image_own * jumps, axis=0, keepdims=True)
        energy = energy + sum(both[:, s * 128 : (s + 1) * 128] for s in range(4))
        return direct, jumps, energy, sum_in

    def edge_terms(direct, jumps):
        jumps = jnp.concatenate([jumps[:, s * 128 : (s + 1) * 128] for s in range(4)], axis=0)
        jumps_h, jumps_l = split(jumps)
        return edge_spread(direct + PENALTY * by_table(table_t, jumps_h, jumps_l))

    def placed(value):
        return face_product(place_ref[...], value)

    learn()
    b = b_ref[...]
    total, gathered = local_part(b, faces)
    total = total + placed(gathered)
    started = face_product(pick_ref[...], total)
    learn()
    jump, subs, _ = side_jumps(0, faces)
    sides = side_terms(0, jump, subs)
    direct, jumps, _, sum_in = edge_jumps(0, own, None)
    tiles = edge_terms(direct, jumps)
    tiles[0] = tiles[0] + sides[0]
    tiles[EA - 1] = tiles[EA - 1] + sides[1]
    remote = jnp.concatenate(tiles, axis=1)
    faces = started + face_product(mix_ref[...], remote)
    own = publish(1, faces)
    send(1)
    learn()
    q = total + placed(remote)
    q_ref[...] = q
    learn()

    total, gathered = local_part(q, faces)
    b = b_ref[...]
    q = q_ref[...]
    early = [column_sums(b, b), column_sums(b, q), column_sums(q, q)]
    energy = column_sums(q, total) + column_sums(faces, gathered)
    learn()
    jump, subs, more = side_jumps(1, faces)
    energy = energy + more
    direct, jumps, more, _ = edge_jumps(1, own, sum_in)
    energy = energy + more

    lanes = jnp.zeros((1, 128), F32)
    for index, sums in enumerate(early + [energy]):
        lanes = jnp.where(lane == index, jnp.sum(sums, axis=1, keepdims=True), lanes)
    mine0[...] = lanes
    while pending:
        learn()
    others = [(c, o) for o in [(0, 0, 0)] + chips for c in range(2) if c or o != (0, 0, 0)]
    others.sort(key=lambda t: sum((v - 1) % n for v, n in zip(t[1], (size_x, size_y, size_z))))
    for k, (flip, offset) in enumerate(others):
        where = chip(offset)
        if flip:
            core = lax.rem(gx, 2)
            where["gx"] = where["gx"] + 1 - 2 * core
        pltpu.make_async_remote_copy(
            src_ref=mine0,
            dst_ref=red1.at[k],
            send_sem=s1_send,
            recv_sem=s1_recv,
            device_id=where,
            device_id_type=MESH,
        ).start()

    sides = side_terms(1, jump, subs)
    tiles = edge_terms(direct, jumps)
    tiles[0] = tiles[0] + sides[0]
    tiles[EA - 1] = tiles[EA - 1] + sides[1]
    w_ref[...] = total + placed(gathered + jnp.concatenate(tiles, axis=1))
    for t in range(2):
        for side in range(2):
            if_there((1, 7)[side], lambda: x_copy(t, side, False).wait_send())
        for index in range(6):
            if_there(EDGE_DIRS[index], lambda: y_copy(t, index, False).wait_send())

    pltpu.make_async_copy(red1, red1, s1_recv).wait()
    lanes = lanes + jnp.sum(red1[...], axis=0)
    bb, bq, qq, qw = (lanes[:, i : i + 1] for i in range(4))
    alpha = bb / bq
    new = bb - 2.0 * alpha * bq + alpha * alpha * qq
    grow = 1.0 + new / bb
    alpha_next = new / (grow * grow * bq - 2.0 * grow * alpha * qq + alpha * alpha * qw)
    row = iota((8, 128), 0)
    coef_ref[...] = jnp.where(row == 0, alpha + alpha_next * grow, alpha * alpha_next)
    pltpu.make_async_copy(red1, red1, s1_send).wait()


def finish(coef_ref, b_ref, q_ref, w_ref, x_hbm, r_hbm, made, out_sem):
    first, second = coef_ref[0:1, 0:1], coef_ref[1:2, 0:1]
    stores = []
    for part, (start, size) in enumerate(((0, 104), (104, NODES - 104))):
        rows = pl.ds(start, size)
        b, q, w = b_ref[rows, :], q_ref[rows, :], w_ref[rows, :]
        made[0, rows, :] = first * b - second * q
        made[1, rows, :] = b - first * q + second * w
        for k, target in enumerate((x_hbm, r_hbm)):
            store = pltpu.make_async_copy(made.at[k, rows], target.at[rows], out_sem.at[part, k])
            store.start()
            stores.append(store)
    for store in stores:
        store.wait()


def body(
    n_gx,
    n_gy,
    right_side,
    stiffness,
    metric,
    levels,
    projection,
    mortar_fine,
    mortar_face,
    mortar_owner,
    mortar_subface,
    mortar_coarse,
    mortar_cface,
):
    pick, place, mix = (jnp.asarray(table, BF16) for table in constant_tables())
    field = jax.ShapeDtypeStruct(right_side.shape, F32)
    count = mortar_fine.shape[0]
    others = n_gx * n_gy - 1
    hbm = pl.BlockSpec(memory_space=pltpu.HBM)
    vmem = pl.BlockSpec(memory_space=pltpu.VMEM)
    dma = pltpu.SemaphoreType.DMA
    line = [
        entry.reshape(1, count)
        for entry in (
            mortar_fine,
            mortar_face,
            mortar_owner,
            mortar_subface,
            mortar_coarse,
            mortar_cface,
            levels,
        )
    ]
    q, w, coef = pl.pallas_call(
        functools.partial(kernel, n_gx, n_gy),
        out_shape=(field, field, jax.ShapeDtypeStruct((8, 128), F32)),
        in_specs=[hbm] * 14,
        out_specs=(vmem, vmem, vmem),
        scratch_shapes=[
            pltpu.VMEM((NODES, ELEMS), F32),
            pltpu.VMEM((3, NODES, NODES), F32),
            pltpu.VMEM((3, ELEMS), F32),
            pltpu.VMEM((7, 1, ELEMS), jnp.int32),
            pltpu.VMEM((SIDE, 4, SIDE), F32),
            pltpu.VMEM((FACES, NODES), BF16),
            pltpu.VMEM((NODES, FACES), BF16),
            pltpu.VMEM((FACES, FACES), BF16),
            pltpu.VMEM((2, 2, FACES + 8, EB), F32),
            pltpu.VMEM((2, 6, FR + 8, 128), F32),
            pltpu.VMEM((9, 8, 128), F32),
            pltpu.VMEM((2, 2, FACES + 8, EB), F32),
            pltpu.VMEM((2, 6, FR + 8, 128), F32),
            pltpu.VMEM((6 * SP, NODES), BF16),
            pltpu.VMEM((ELEMS, 2 * EB), BF16),
            pltpu.VMEM((2, EB, 2 * EB), BF16),
            pltpu.VMEM((128, 512), BF16),
            pltpu.VMEM((128, 512), BF16),
            pltpu.VMEM((256, 128), F32),
            pltpu.VMEM((FR, 256), F32),
            pltpu.VMEM((FR, 256), F32),
            pltpu.VMEM((others, 1, 128), F32),
            pltpu.VMEM((1, 128), F32),
            dma((14,)),
            dma((2, 2)),
            dma((2, 2)),
            dma((2, 6)),
            dma((2, 6)),
            pltpu.SemaphoreType.REGULAR((8,)),
            dma,
            dma,
        ],
        compiler_params=pltpu.CompilerParams(
            collective_id=0, has_side_effects=True, vmem_limit_bytes=40 * 1024 * 1024
        ),
    )(
        *(
            pltpu.with_memory_space_constraint(operand, pltpu.HBM)
            for operand in (right_side, stiffness, metric, *line, projection.transpose(1, 0, 2), pick, place, mix)
        )
    )
    return pl.pallas_call(
        finish,
        out_shape=(field, field),
        in_specs=[vmem] * 4,
        out_specs=(hbm, hbm),
        scratch_shapes=[pltpu.VMEM((2, NODES, ELEMS), F32), dma((2, 2))],
        compiler_params=pltpu.CompilerParams(vmem_limit_bytes=40 * 1024 * 1024),
    )(coef, right_side, q, w)


def solution(mesh):
    columns = P(None, ("gx", "gy"))
    faces = P(("gx", "gy"))
    in_specs = (columns, P(), columns, faces, P(), faces, faces, P(("gx", "gy"), None), faces, faces, faces)
    run = functools.partial(body, mesh.shape["gx"], mesh.shape["gy"])
    return jax.shard_map(run, mesh=mesh, in_specs=in_specs, out_specs=(columns, columns), check_vma=False)
```

```python
import functools

import jax
import jax.numpy as jnp
import numpy as np
from jax import lax
from jax.experimental import pallas as pl
from jax.experimental.pallas import tpu as pltpu
from jax.sharding import PartitionSpec as P

NP = 6
NODES = NP * NP * NP
SIDE = NP * NP
EA = 4
EB = 128
ELEMS = EA * EB
FR = 40
FACES = 6 * FR
SP = 224
PENALTY = 1.0

F32 = jnp.float32
BF16 = jnp.bfloat16
MESH = pl.DeviceIdType.MESH

DIRS = {d: (d // 3 - 1, d % 3 - 1) for d in range(9) if d != 4}
EDGE_DIRS = (3, 5, 0, 2, 6, 8)
CORNERS = {0: 8, 2: 9, 6: 10, 8: 11}
CORNER_SHIFT = {8: 7, 9: 9, 10: 3, 11: 5}
TURNS = (1, -1, -3, -1, 1, 3)


def face_nodes(face):
    ids = np.arange(NODES).reshape(NP, NP, NP)
    return [ids[0], ids[5], ids[:, 0], ids[:, 5], ids[:, :, 0], ids[:, :, 5]][face].reshape(-1)


def constant_tables():
    pick = np.zeros((FACES, NODES), np.float32)
    for face in range(6):
        pick[face * FR + np.arange(SIDE), face_nodes(face)] = 1.0
    return pick, pick.T.copy(), pick @ pick.T


def dot(a, b):
    return lax.dot_general(a, b, (((1,), (0,)), ((), ())), preferred_element_type=F32)


def dot_nt(a, b):
    return lax.dot_general(a, b, (((1,), (1,)), ((), ())), preferred_element_type=F32)


def split(value):
    high = value.astype(BF16)
    return high, (value - high.astype(F32)).astype(BF16)


def iota(shape, dim):
    return lax.broadcasted_iota(jnp.int32, shape, dim)


def one_hot(rows, code):
    return jnp.where(iota((rows, code.shape[1]), 0).astype(F32) == code, 1.0, 0.0).astype(BF16)


def pick_face(sides, face):
    out = None
    for f in range(6):
        part = jnp.where(face == float(f), sides[f * FR : (f + 1) * FR], 0.0)
        out = part if out is None else out + part
    return out


def spread_face(values, face):
    return jnp.concatenate([jnp.where(face == float(f), values, 0.0) for f in range(6)], axis=0)


def spread_split(values, face):
    high = values.astype(BF16).astype(F32)
    return spread_face(high, face).astype(BF16), spread_face(values - high, face).astype(BF16)


def by_subface(values, sub):
    return jnp.concatenate([jnp.where(sub == float(s), values, 0.0) for s in range(4)], axis=0).astype(BF16)


def column_sums(a, b):
    prod = a * b
    rows = jnp.sum(prod, axis=0, keepdims=True)
    return sum(rows[:, t * EB : (t + 1) * EB] for t in range(EA))


def kernel(
    n_gx,
    n_gy,
    b_hbm,
    stiff_hbm,
    metric_hbm,
    fine_hbm,
    face_hbm,
    owner_hbm,
    sub_hbm,
    coarse_hbm,
    cface_hbm,
    level_hbm,
    proj_hbm,
    pick_hbm,
    place_hbm,
    mix_hbm,
    q_ref,
    w_ref,
    coef_ref,
    b_ref,
    stiff_ref,
    metric_ref,
    ints_ref,
    proj_ref,
    pick_ref,
    place_ref,
    mix_ref,
    halo_x,
    halo_y,
    own_m,
    own_x,
    own_y,
    stiff_s,
    oh_self,
    oh_x,
    n_out,
    n_in,
    proj_s,
    proj_c,
    proj_t,
    red1,
    mine0,
    in_sem,
    sx_send,
    sx_recv,
    sy_send,
    sy_recv,
    ready_sem,
    s1_send,
    s1_recv,
):
    gx = lax.axis_index("gx")
    gy = lax.axis_index("gy")

    int_names = (fine_hbm, face_hbm, owner_hbm, sub_hbm, coarse_hbm, cface_hbm, level_hbm)
    loads = [(source, ints_ref.at[k]) for k, source in enumerate(int_names)]
    loads += [(b_hbm, b_ref), (pick_hbm, pick_ref), (proj_hbm, proj_ref), (mix_hbm, mix_ref)]
    loads += [(stiff_hbm, stiff_ref), (metric_hbm, metric_ref), (place_hbm, place_ref)]
    loads = [pltpu.make_async_copy(source, target, in_sem.at[k]) for k, (source, target) in enumerate(loads)]
    for load in loads:
        load.start()

    def there(d):
        dx, dy = DIRS[d]
        ok = (gx + dx >= 0) & (gx + dx < n_gx) & (gy + dy >= 0) & (gy + dy < n_gy)
        return ok, {"gx": gx + dx, "gy": gy + dy}

    def if_there(d, act):
        pl.when(there(d)[0])(act)

    size_x, size_y, size_z = n_gx // 2, n_gy // 4, 4
    chips = [(i, j, k) for i in range(size_x) for j in range(size_y) for k in range(size_z)][1:]
    chips.sort(key=lambda c: sum((v - 1) % n for v, n in zip(c, (size_x, size_y, size_z))))

    def chip(offset):
        y, z = gy // size_z, lax.rem(gy, size_z)
        return {
            "gx": lax.rem(gx + 2 * offset[0], n_gx),
            "gy": lax.rem(y + offset[1], size_y) * size_z + lax.rem(z + offset[2], size_z),
        }

    halo_x[...] = jnp.zeros_like(halo_x)
    halo_y[...] = jnp.zeros_like(halo_y)

    barrier = pltpu.get_barrier_semaphore()
    expected = jnp.int32(0)
    for d in DIRS:
        ok, where = there(d)

        @pl.when(ok)
        def _():
            pl.semaphore_signal(barrier, inc=1, device_id=where, device_id_type=MESH)

        expected = expected + ok.astype(jnp.int32)

    def x_copy(t, side, arriving):
        slot = side if arriving else 1 - side
        rows = pl.ds(0, FACES + 8 * (1 - t))
        return pltpu.make_async_remote_copy(
            src_ref=own_x.at[t, side, rows],
            dst_ref=halo_x.at[t, slot, rows],
            send_sem=sx_send.at[t, side],
            recv_sem=sx_recv.at[t, slot],
            device_id=there((1, 7)[side])[1],
            device_id_type=MESH,
        )

    def y_copy(t, index, arriving):
        d = EDGE_DIRS[index]
        slot = index if arriving else EDGE_DIRS.index(8 - d)
        rows = pl.ds(0, FR + 8 * (1 - t))
        return pltpu.make_async_remote_copy(
            src_ref=own_y.at[t, index if t == 0 else 0, rows],
            dst_ref=halo_y.at[t, slot, rows],
            send_sem=sy_send.at[t, index],
            recv_sem=sy_recv.at[t, slot],
            device_id=there(d)[1],
            device_id_type=MESH,
        )

    strides = [k for k in (1, 2, 4, 8, 16) if k < max(n_gx, n_gy)]

    def partners(k):
        by = strides[k]
        for dx in (-by, 0, by) if by < n_gx else (0,):
            for dy in (-by, 0, by) if by < n_gy else (0,):
                if dx or dy:
                    ok = (gx + dx >= 0) & (gx + dx < n_gx) & (gy + dy >= 0) & (gy + dy < n_gy)
                    yield ok, {"gx": gx + dx, "gy": gy + dy}

    def pass_on(k):
        for ok, where in partners(k):

            @pl.when(ok)
            def _():
                pl.semaphore_signal(ready_sem.at[k], inc=1, device_id=where, device_id_type=MESH)

    pending = list(range(len(strides)))

    def learn():
        if pending:
            k = pending.pop(0)
            pl.semaphore_wait(ready_sem.at[k], sum(ok.astype(jnp.int32) for ok, _ in partners(k)))
            if pending:
                pass_on(k + 1)

    def send(t):
        for index in (2, 3, 4, 5, 0, 1):
            if_there(EDGE_DIRS[index], lambda: y_copy(t, index, False).start())
        for side in range(2):
            if_there((1, 7)[side], lambda: x_copy(t, side, False).start())

    lane = iota((1, 128), 1)
    lane_face = lane >> 4
    lane_pair = lane & 15

    def stacked_table(value):
        high = value.astype(BF16)
        rest = value - high.astype(F32)
        return high, jnp.concatenate([high.astype(F32), rest], axis=0).astype(BF16)

    def by_table(table, value_h, value_l):
        high, both = table
        rows = high.shape[0]
        first = dot(both, value_h)
        return first[:rows] + first[rows:] + dot(high, value_l)

    def code(entry, active):
        return jnp.where(active > 0.0, entry, -1.0)

    for load in loads[:9]:
        load.wait()
    fine, face, owner, sub, coarse, cface, level = (ints_ref[k] for k in range(7))
    shift = n_gy.bit_length() - 1
    slot = ((owner >> shift) - gx + 1) * 3 + (owner & (n_gy - 1)) - gy + 1
    count = fine.shape[1]
    hits = jnp.where(iota((16, count), 0) == slot, 1.0, 0.0)
    parts = [hits[:, k : k + EB] for k in range(0, count, EB)]
    earlier = jnp.where(iota((EB, EB), 0) < iota((EB, EB), 1), 1.0, 0.0).astype(BF16)
    within = dot(jnp.concatenate(parts, axis=0).astype(BF16), earlier)
    offset, ranks = jnp.zeros((16, 1), F32), []
    for k, part in enumerate(parts):
        ranks.append(jnp.sum(part * (within[16 * k : 16 * k + 16] + offset), axis=0, keepdims=True))
        offset = offset + jnp.sum(part, axis=1, keepdims=True)
    position = jnp.concatenate(ranks, axis=1)
    row = iota((8, count), 0)
    facts = jnp.ones((8, count), jnp.int32)
    for index, entry in enumerate((fine >> 7, fine & 127, face, coarse >> 7, coarse & 127, cface, sub)):
        facts = jnp.where(row == index, entry, facts)
    facts = facts.astype(F32)
    stacked = jnp.concatenate([facts * hits[k : k + 1] for k in range(9)], axis=0).astype(BF16)
    packed = dot_nt(stacked, one_hot(EB, position))
    for k in range(9):
        own_m[k] = packed[8 * k : 8 * k + 8]
    for side in range(2):
        d = (1, 7)[side]
        own_x[0, side, FACES : FACES + 8, :] = packed[8 * d : 8 * d + 8]
    for index, d in enumerate(EDGE_DIRS):
        own_y[0, index, FR : FR + 8, :] = packed[8 * d : 8 * d + 8]
    scale = jnp.where(level == 0, 1.0, jnp.where(level == 1, 0.5, 0.25))

    def face_product(table, value):
        high, low = split(value)
        return dot(table, high) + dot(table, low)

    def edge_values(faces):
        ends = faces[:, 0:EB]
        for a in range(1, EA):
            moved = pltpu.roll(faces[:, a * EB : (a + 1) * EB], 2 * a, 1)
            ends = jnp.where((lane == 2 * a) | (lane == 2 * a - 1), moved, ends)
        own = jnp.zeros((FR, 128), F32)
        for f in range(6):
            moved = pltpu.roll(ends[f * FR : (f + 1) * FR], 16 * f + 1, 1)
            own = jnp.where((lane_face == f) & (lane_pair < 8), moved, own)
        rows = own
        for pair, by in CORNER_SHIFT.items():
            own = jnp.where(lane_pair == pair, pltpu.roll(rows, by, 1), own)
        return own

    def edge_spread(values):
        rows = jnp.where(lane_pair < 8, values, 0.0)
        for pair, by in CORNER_SHIFT.items():
            rows = rows + jnp.where(lane_pair == pair - by, pltpu.roll(values, 128 - by, 1), 0.0)
        ends = jnp.concatenate([pltpu.roll(rows, 127 - 16 * f, 1) for f in range(6)], axis=0)
        tiles = []
        for a in range(EA):
            moved = pltpu.roll(ends, 128 - 2 * a, 1) if a else ends
            tiles.append(jnp.where((lane == 0) | (lane == EB - 1), moved, 0.0))
        return tiles

    def publish(t, faces):
        own_x[t, 0, 0:FACES, :] = faces[:, 0:EB]
        own_x[t, 1, 0:FACES, :] = faces[:, (EA - 1) * EB :]
        own = edge_values(faces)
        for index in range(6 if t == 0 else 1):
            own_y[t, index, 0:FR, :] = own
        return own

    b = b_ref[...]
    faces = face_product(pick_ref[...], b)
    own = publish(0, faces)

    pl.semaphore_wait(barrier, expected)
    send(0)
    pass_on(0)

    for load in loads[9:]:
        load.wait()
    for d in range(3):
        padded = jnp.concatenate([stiff_ref[d], jnp.zeros((SP - NODES, NODES), F32)], axis=0)
        high, low = split(padded)
        stiff_s[d * SP : (d + 1) * SP, :] = high
        stiff_s[(3 + d) * SP : (4 + d) * SP, :] = low
    proj_s[...] = jnp.zeros_like(proj_s)
    proj_c[...] = jnp.zeros_like(proj_c)
    for s in range(4):
        table = proj_ref[:, s, :]
        proj_s[s * FR : s * FR + SIDE, 0:SIDE] = table
        proj_c[0:SIDE, s * FR : s * FR + SIDE] = table
    proj_t[...] = proj_s[...].T[0:FR]
    table_s = stacked_table(proj_s[0 : 4 * FR, 0:FR])
    table_c = stacked_table(proj_c[:, 0 : 4 * FR])
    table_t = stacked_table(proj_t[:, 0 : 4 * FR])

    me = own_m[4]
    self_fine = code(me[0:1] * float(EB) + me[1:2], me[7:8])
    self_coarse = code(me[3:4] * float(EB) + me[4:5], me[7:8])
    oh_self[...] = one_hot(ELEMS, jnp.concatenate([self_fine, self_coarse], axis=1))

    wide = iota((32, 512), 1)
    repeat = jnp.where(iota((32, 512), 0) == (wide >> 7) * 8 + ((wide >> 4) & 7), 1.0, 0.0).astype(BF16)
    same_pair = (iota((128, 512), 0) & 15) == (iota((128, 512), 1) & 15)
    ones = jnp.ones((16, 6 * EB), BF16)

    def edge_counts(held):
        parts_f, parts_c = [], []
        for d, facts_d in zip(EDGE_DIRS, held):
            if d in (3, 5):
                pair = facts_d[0:1] * 2.0 + (1.0 if d == 3 else 0.0)
            else:
                pair = float(CORNERS[d])
            parts_f.append(code(facts_d[2:3] * 16.0 + pair, facts_d[7:8]))
            parts_c.append(code(facts_d[6:7] * 8.0 + facts_d[5:6], facts_d[7:8]))
        fine_hot = one_hot(128, jnp.concatenate(parts_f, axis=1))
        coarse_hot = one_hot(32, jnp.concatenate(parts_c, axis=1))
        joined = dot(dot_nt(fine_hot, coarse_hot).astype(BF16), repeat)
        return jnp.where(same_pair, joined, 0.0).astype(BF16), dot_nt(ones, fine_hot)[0:1]

    n_out[...], sum_out = edge_counts([own_m[d] for d in EDGE_DIRS])

    def mortar_jump(coarses, fines, subs):
        high = coarses.astype(BF16).astype(F32)
        return by_table(table_c, by_subface(high, subs), by_subface(coarses - high, subs)) - fines

    def mortar_back(jump, subs):
        high = jump.astype(BF16).astype(F32)
        return by_table(table_t, by_subface(high, subs), by_subface(jump - high, subs))

    def local_part(field, faces):
        f_h, f_l = split(faces)
        got = dot(f_h, oh_self[...]) + dot(f_l, oh_self[...])
        jump = mortar_jump(pick_face(got[:, EB:], me[5:6]), pick_face(got[:, 0:EB], me[2:3]), me[6:7])
        back = mortar_back(jump, me[6:7])
        terms = jnp.concatenate([-PENALTY * jump, PENALTY * back], axis=1)
        s_h, s_l = spread_split(terms, jnp.concatenate([me[2:3], me[5:6]], axis=1))
        gathered = dot_nt(s_h, oh_self[...]) + dot_nt(s_l, oh_self[...])

        blocks = []
        for a in range(EA):
            here = slice(a * EB, (a + 1) * EB)
            x_low, x_high = faces[0:FR, here], faces[FR : 2 * FR, here]
            y_low, y_high = faces[2 * FR : 3 * FR, here], faces[3 * FR : 4 * FR, here]
            left = x_low if a == 0 else x_low - faces[FR : 2 * FR, (a - 1) * EB : a * EB]
            right = x_high if a == EA - 1 else x_high - faces[0:FR, (a + 1) * EB : (a + 2) * EB]
            below = jnp.where(lane == 0, 0.0, pltpu.roll(y_high, 1, 1))
            above = jnp.where(lane == EB - 1, 0.0, pltpu.roll(y_low, EB - 1, 1))
            lateral = jnp.concatenate([left, right, y_low - below, y_high - above], axis=0)
            blocks.append(jnp.concatenate([PENALTY * lateral, jnp.zeros((2 * FR, EB), F32)], axis=0))
        gathered = gathered + jnp.concatenate(blocks, axis=1)

        field_h, field_l = split(field)
        both = dot(stiff_s[...], field_h)
        rest = dot(stiff_s[0 : 3 * SP, :], field_l)
        total = field
        for d in range(3):
            here = slice(d * SP, d * SP + NODES)
            again = slice((3 + d) * SP, (3 + d) * SP + NODES)
            total = total + metric_ref[d : d + 1, :] * (both[here] + both[again] + rest[here])
        return scale * total, gathered

    def side_jumps(faces):
        for side in range(2):
            d = (1, 7)[side]
            both = jnp.concatenate([own_m[d], halo_x[0, side, FACES : FACES + 8, :]], axis=1)
            oh_x[side] = one_hot(EB, code(both[1:2], both[7:8]))
        fines, coarses, subs = [], [], []
        for side in range(2):
            d = (1, 7)[side]
            theirs_m = halo_x[0, side, FACES : FACES + 8, :]
            here = slice(0, EB) if side == 0 else slice((EA - 1) * EB, EA * EB)
            pair = jnp.concatenate([faces[:, here], halo_x[0, side, 0:FACES, :]], axis=0)
            high, low = split(pair)
            got = dot(high, oh_x[side]) + dot(low, oh_x[side])
            ours, theirs = got[0:FACES], got[FACES:]
            fines += [pick_face(ours[:, 0:EB], own_m[d][2:3]), pick_face(theirs[:, EB:], theirs_m[2:3])]
            coarses += [pick_face(theirs[:, 0:EB], own_m[d][5:6]), pick_face(ours[:, EB:], theirs_m[5:6])]
            subs += [own_m[d][6:7], theirs_m[6:7]]
        jump = mortar_jump(*(jnp.concatenate(parts, axis=1) for parts in (coarses, fines, subs)))
        jump = [jump[:, k * EB : (k + 1) * EB] for k in range(4)]
        return jump, subs

    def side_adjoint(faces):
        fines, coarses, subs = [], [], []
        for side in range(2):
            d = (1, 7)[side]
            theirs_m = halo_x[0, side, FACES : FACES + 8, :]
            high, low = split(faces[:, 0:EB] if side == 0 else faces[:, (EA - 1) * EB :])
            got = dot(high, oh_x[side]) + dot(low, oh_x[side])
            fines.append(pick_face(got[:, 0:EB], own_m[d][2:3]))
            coarses.append(pick_face(got[:, EB:], theirs_m[5:6]))
            subs += [own_m[d][6:7], theirs_m[6:7]]
        fines = jnp.concatenate(fines, axis=1)
        images = mortar_jump(jnp.concatenate(coarses, axis=1), 0.0, jnp.concatenate([subs[1], subs[3]], axis=1))
        backs = mortar_back(fines, jnp.concatenate([subs[0], subs[2]], axis=1))
        against = []
        for side in range(2):
            d = (1, 7)[side]
            here = slice(side * EB, (side + 1) * EB)
            theirs_m = halo_x[0, side, FACES : FACES + 8, :]
            s_h, s_l = spread_split(
                jnp.concatenate([backs[:, here], images[:, here]], axis=1),
                jnp.concatenate([own_m[d][5:6], theirs_m[2:3]], axis=1),
            )
            against.append(dot_nt(s_h, oh_x[side]) + dot_nt(s_l, oh_x[side]))
        low_face, high_face = faces[0:FR, 0:EB], faces[FR : 2 * FR, (EA - 1) * EB :]
        against[0] = against[0] + jnp.concatenate([jnp.zeros((FR, EB), F32), low_face, jnp.zeros((4 * FR, EB), F32)], axis=0)
        against[1] = against[1] + jnp.concatenate([high_face, jnp.zeros((5 * FR, EB), F32)], axis=0)
        known = jnp.sum(fines * fines + images * images, axis=0, keepdims=True)
        return fines, images, subs, against, known[:, 0:EB] + known[:, EB:]

    def side_jumps_after(fines, images, subs):
        far_fines, far_coarses = [], []
        for side in range(2):
            d = (1, 7)[side]
            theirs_m = halo_x[0, side, FACES : FACES + 8, :]
            high, low = split(halo_x[1, side, 0:FACES, :])
            got = dot(high, oh_x[side]) + dot(low, oh_x[side])
            far_coarses.append(pick_face(got[:, 0:EB], own_m[d][5:6]))
            far_fines.append(pick_face(got[:, EB:], theirs_m[2:3]))
        out = mortar_jump(
            jnp.concatenate(far_coarses, axis=1), fines, jnp.concatenate([subs[0], subs[2]], axis=1)
        )
        into = images - jnp.concatenate(far_fines, axis=1)
        return [out[:, 0:EB], into[:, 0:EB], out[:, EB:], into[:, EB:]]

    def side_terms(t, jump, subs):
        back = mortar_back(jnp.concatenate([jump[1], jump[3]], axis=1), jnp.concatenate([subs[1], subs[3]], axis=1))
        result = []
        for side in range(2):
            d = (1, 7)[side]
            terms = jnp.concatenate(
                [-PENALTY * jump[2 * side], PENALTY * back[:, side * EB : (side + 1) * EB]], axis=1
            )
            theirs_m = halo_x[0, side, FACES : FACES + 8, :]
            s_h, s_l = spread_split(terms, jnp.concatenate([own_m[d][2:3], theirs_m[5:6]], axis=1))
            side_term = dot_nt(s_h, oh_x[side]) + dot_nt(s_l, oh_x[side])
            if side == 0:
                beside = [-PENALTY * halo_x[t, 0, FR : 2 * FR, :], jnp.zeros((5 * FR, EB), F32)]
            else:
                beside = [jnp.zeros((FR, EB), F32), -PENALTY * halo_x[t, 1, 0:FR, :], jnp.zeros((4 * FR, EB), F32)]
            result.append(side_term + jnp.concatenate(beside, axis=0))
        return result

    low_face = (lane_face == 2) & (lane_pair < 8) & ((lane_pair & 1) == 1)
    high_face = (lane_face == 3) & (lane_pair < 8) & ((lane_pair & 1) == 0)

    def pair_mask(index):
        if index < 2:
            return (lane_pair < 8) & ((lane_pair & 1) == 1 - index)
        return lane_pair == CORNERS[EDGE_DIRS[index]]

    def edges_arrive(t):
        for index in range(6):
            if_there(EDGE_DIRS[index], lambda: y_copy(t, index, True).wait_recv())

    def sides_arrive(t):
        for side in range(2):
            if_there((1, 7)[side], lambda: x_copy(t, side, True).wait_recv())

    def edge_jumps(t, own, sum_in):
        across = jnp.zeros((FR, 128), F32)
        for index, turn in enumerate(TURNS):
            across = jnp.where(pair_mask(index), pltpu.roll(halo_y[t, index, 0:FR, :], turn % 128, 1), across)
        pairs = jnp.concatenate([own, across], axis=1)
        pairs_h, pairs_l = split(pairs)
        images = by_table(table_s, pairs_h, pairs_l)
        image_own = jnp.concatenate([images[s * FR : (s + 1) * FR, 0:128] for s in range(4)], axis=1)
        image_far = jnp.concatenate([images[s * FR : (s + 1) * FR, 128:] for s in range(4)], axis=1)
        far_h, far_l = split(image_far)
        on_fine = own * sum_out - dot_nt(far_h, n_out[...]) - dot_nt(far_l, n_out[...])
        jumps = image_own * sum_in - dot(pairs_h[:, 128:], n_in[...]) - dot(pairs_l[:, 128:], n_in[...])
        from_low = pltpu.roll(across, 128 - 16, 1)
        from_high = pltpu.roll(across, 16, 1)
        beside = jnp.where(low_face, from_low, jnp.where(high_face, from_high, 0.0))
        return PENALTY * (on_fine - beside), jumps

    def edge_adjoint(own, sum_in):
        own_h, own_l = split(own)
        images = by_table(table_s, own_h, own_l)
        images = jnp.concatenate([images[s * FR : (s + 1) * FR] for s in range(4)], axis=1)
        images_h, images_l = split(images)
        joined = dot(own_h, n_out[...]) + dot(own_l, n_out[...])
        joined_h, joined_l = split(jnp.concatenate([joined[:, s * 128 : (s + 1) * 128] for s in range(4)], axis=0))
        meets = by_table(table_t, joined_h, joined_l) + dot_nt(images_h, n_in[...]) + dot_nt(images_l, n_in[...])
        meets = meets + pltpu.roll(jnp.where(low_face, own, 0.0), 16, 1)
        meets = meets + pltpu.roll(jnp.where(high_face, own, 0.0), 128 - 16, 1)
        against = []
        for index, turn in enumerate(TURNS):
            against.append(pltpu.roll(jnp.where(pair_mask(index), meets, 0.0), -turn % 128, 1))
        known = jnp.sum(own * own * sum_out, axis=0, keepdims=True)
        both = jnp.sum(images * images * sum_in, axis=0, keepdims=True)
        return against, known + sum(both[:, s * 128 : (s + 1) * 128] for s in range(4))

    def edge_terms(direct, jumps):
        jumps = jnp.concatenate([jumps[:, s * 128 : (s + 1) * 128] for s in range(4)], axis=0)
        jumps_h, jumps_l = split(jumps)
        return edge_spread(direct + PENALTY * by_table(table_t, jumps_h, jumps_l))

    def placed(value):
        return face_product(place_ref[...], value)

    learn()
    b = b_ref[...]
    total, gathered = local_part(b, faces)
    total = total + placed(gathered)
    started = face_product(pick_ref[...], total)
    learn()
    sides_arrive(0)
    jump, subs = side_jumps(faces)
    sides = side_terms(0, jump, subs)
    edges_arrive(0)
    n_in[...], _ = edge_counts([halo_y[0, index, FR : FR + 8, :] for index in range(6)])
    sum_in = dot(jnp.ones((16, 128), BF16), n_in[...])[0:1]
    direct, jumps = edge_jumps(0, own, sum_in)
    tiles = edge_terms(direct, jumps)
    tiles[0] = tiles[0] + sides[0]
    tiles[EA - 1] = tiles[EA - 1] + sides[1]
    remote = jnp.concatenate(tiles, axis=1)
    faces = started + face_product(mix_ref[...], remote)
    own = publish(1, faces)
    send(1)
    learn()
    q = total + placed(remote)
    q_ref[...] = q

    total, gathered = local_part(q, faces)
    b = b_ref[...]
    q = q_ref[...]
    early = [column_sums(b, b), column_sums(b, q), column_sums(q, q)]
    energy = column_sums(q, total) + column_sums(faces, gathered)
    fines, images, subs, side_against, known = side_adjoint(faces)
    energy = energy + PENALTY * known
    edge_against, known = edge_adjoint(own, sum_in)
    energy = energy + PENALTY * known
    sides_arrive(1)
    met = jnp.zeros((1, 128), F32)
    for side in range(2):
        met = met + jnp.sum(halo_x[1, side, 0:FACES, :] * side_against[side], axis=0, keepdims=True)
    energy = energy - PENALTY * met
    edges_arrive(1)
    met = sum(halo_y[1, index, 0:FR, :] * edge_against[index] for index in range(6))
    energy = energy - PENALTY * jnp.sum(met, axis=0, keepdims=True)

    lanes = jnp.zeros((1, 128), F32)
    for index, sums in enumerate(early + [energy]):
        lanes = jnp.where(lane == index, jnp.sum(sums, axis=1, keepdims=True), lanes)
    mine0[...] = lanes
    while pending:
        learn()
    others = [(c, o) for o in [(0, 0, 0)] + chips for c in range(2) if c or o != (0, 0, 0)]
    others.sort(key=lambda t: sum((v - 1) % n for v, n in zip(t[1], (size_x, size_y, size_z))))
    for k, (flip, offset) in enumerate(others):
        where = chip(offset)
        if flip:
            core = lax.rem(gx, 2)
            where["gx"] = where["gx"] + 1 - 2 * core
        pltpu.make_async_remote_copy(
            src_ref=mine0,
            dst_ref=red1.at[k],
            send_sem=s1_send,
            recv_sem=s1_recv,
            device_id=where,
            device_id_type=MESH,
        ).start()

    sides = side_terms(1, side_jumps_after(fines, images, subs), subs)
    tiles = edge_terms(*edge_jumps(1, own, sum_in))
    tiles[0] = tiles[0] + sides[0]
    tiles[EA - 1] = tiles[EA - 1] + sides[1]
    w_ref[...] = total + placed(gathered + jnp.concatenate(tiles, axis=1))
    for t in range(2):
        for side in range(2):
            if_there((1, 7)[side], lambda: x_copy(t, side, False).wait_send())
        for index in range(6):
            if_there(EDGE_DIRS[index], lambda: y_copy(t, index, False).wait_send())

    pltpu.make_async_copy(red1, red1, s1_recv).wait()
    lanes = lanes + jnp.sum(red1[...], axis=0)
    bb, bq, qq, qw = (lanes[:, i : i + 1] for i in range(4))
    alpha = bb / bq
    new = bb - 2.0 * alpha * bq + alpha * alpha * qq
    grow = 1.0 + new / bb
    alpha_next = new / (grow * grow * bq - 2.0 * grow * alpha * qq + alpha * alpha * qw)
    row = iota((8, 128), 0)
    coef_ref[...] = jnp.where(row == 0, alpha + alpha_next * grow, alpha * alpha_next)
    pltpu.make_async_copy(red1, red1, s1_send).wait()


def finish(coef_ref, b_ref, q_ref, w_ref, x_hbm, r_hbm, made, out_sem):
    first, second = coef_ref[0:1, 0:1], coef_ref[1:2, 0:1]
    stores = []
    for part, (start, size) in enumerate(((0, 104), (104, NODES - 104))):
        rows = pl.ds(start, size)
        b, q, w = b_ref[rows, :], q_ref[rows, :], w_ref[rows, :]
        made[0, rows, :] = first * b - second * q
        made[1, rows, :] = b - first * q + second * w
        for k, target in enumerate((x_hbm, r_hbm)):
            store = pltpu.make_async_copy(made.at[k, rows], target.at[rows], out_sem.at[part, k])
            store.start()
            stores.append(store)
    for store in stores:
        store.wait()


def body(
    n_gx,
    n_gy,
    right_side,
    stiffness,
    metric,
    levels,
    projection,
    mortar_fine,
    mortar_face,
    mortar_owner,
    mortar_subface,
    mortar_coarse,
    mortar_cface,
):
    pick, place, mix = (jnp.asarray(table, BF16) for table in constant_tables())
    field = jax.ShapeDtypeStruct(right_side.shape, F32)
    count = mortar_fine.shape[0]
    others = n_gx * n_gy - 1
    hbm = pl.BlockSpec(memory_space=pltpu.HBM)
    vmem = pl.BlockSpec(memory_space=pltpu.VMEM)
    dma = pltpu.SemaphoreType.DMA
    line = [
        entry.reshape(1, count)
        for entry in (
            mortar_fine,
            mortar_face,
            mortar_owner,
            mortar_subface,
            mortar_coarse,
            mortar_cface,
            levels,
        )
    ]
    q, w, coef = pl.pallas_call(
        functools.partial(kernel, n_gx, n_gy),
        out_shape=(field, field, jax.ShapeDtypeStruct((8, 128), F32)),
        in_specs=[hbm] * 14,
        out_specs=(vmem, vmem, vmem),
        scratch_shapes=[
            pltpu.VMEM((NODES, ELEMS), F32),
            pltpu.VMEM((3, NODES, NODES), F32),
            pltpu.VMEM((3, ELEMS), F32),
            pltpu.VMEM((7, 1, ELEMS), jnp.int32),
            pltpu.VMEM((SIDE, 4, SIDE), F32),
            pltpu.VMEM((FACES, NODES), BF16),
            pltpu.VMEM((NODES, FACES), BF16),
            pltpu.VMEM((FACES, FACES), BF16),
            pltpu.VMEM((2, 2, FACES + 8, EB), F32),
            pltpu.VMEM((2, 6, FR + 8, 128), F32),
            pltpu.VMEM((9, 8, 128), F32),
            pltpu.VMEM((2, 2, FACES + 8, EB), F32),
            pltpu.VMEM((2, 6, FR + 8, 128), F32),
            pltpu.VMEM((6 * SP, NODES), BF16),
            pltpu.VMEM((ELEMS, 2 * EB), BF16),
            pltpu.VMEM((2, EB, 2 * EB), BF16),
            pltpu.VMEM((128, 512), BF16),
            pltpu.VMEM((128, 512), BF16),
            pltpu.VMEM((256, 128), F32),
            pltpu.VMEM((FR, 256), F32),
            pltpu.VMEM((FR, 256), F32),
            pltpu.VMEM((others, 1, 128), F32),
            pltpu.VMEM((1, 128), F32),
            dma((14,)),
            dma((2, 2)),
            dma((2, 2)),
            dma((2, 6)),
            dma((2, 6)),
            pltpu.SemaphoreType.REGULAR((8,)),
            dma,
            dma,
        ],
        compiler_params=pltpu.CompilerParams(
            collective_id=0, has_side_effects=True, vmem_limit_bytes=40 * 1024 * 1024
        ),
    )(
        *(
            pltpu.with_memory_space_constraint(operand, pltpu.HBM)
            for operand in (right_side, stiffness, metric, *line, projection.transpose(1, 0, 2), pick, place, mix)
        )
    )
    return pl.pallas_call(
        finish,
        out_shape=(field, field),
        in_specs=[vmem] * 4,
        out_specs=(hbm, hbm),
        scratch_shapes=[pltpu.VMEM((2, NODES, ELEMS), F32), dma((2, 2))],
        compiler_params=pltpu.CompilerParams(vmem_limit_bytes=40 * 1024 * 1024),
    )(coef, right_side, q, w)


def solution(mesh):
    columns = P(None, ("gx", "gy"))
    faces = P(("gx", "gy"))
    in_specs = (columns, P(), columns, faces, P(), faces, faces, P(("gx", "gy"), None), faces, faces, faces)
    run = functools.partial(body, mesh.shape["gx"], mesh.shape["gy"])
    return jax.shard_map(run, mesh=mesh, in_specs=in_specs, out_specs=(columns, columns), check_vma=False)
```

```python
import functools

import jax
import jax.numpy as jnp
import numpy as np
from jax import lax
from jax.experimental import pallas as pl
from jax.experimental.pallas import tpu as pltpu
from jax.sharding import PartitionSpec as P

NP = 6
NODES = NP * NP * NP
SIDE = NP * NP
EA = 4
EB = 128
ELEMS = EA * EB
FR = 40
FACES = 6 * FR
SP = 224
PENALTY = 1.0

F32 = jnp.float32
BF16 = jnp.bfloat16
MESH = pl.DeviceIdType.MESH

DIRS = {d: (d // 3 - 1, d % 3 - 1) for d in range(9) if d != 4}
EDGE_DIRS = (3, 5, 0, 2, 6, 8)
CORNERS = {0: 8, 2: 10, 6: 12, 8: 14}
CORNER_SHIFT = {8: 7, 10: 10, 12: 5, 14: 8}
PACK = {(f, g): 8 * ((5 * f + g) // 2) + (5 * f + g) % 2 for f in range(6) for g in range(FR // 8)}
CORNER_ROWS = (EA - 1, EA - 1, 0, 0)


def face_nodes(face):
    ids = np.arange(NODES).reshape(NP, NP, NP)
    return [ids[0], ids[5], ids[:, 0], ids[:, 5], ids[:, :, 0], ids[:, :, 5]][face].reshape(-1)


def constant_tables():
    pick = np.zeros((FACES, NODES), np.float32)
    for face in range(6):
        pick[face * FR + np.arange(SIDE), face_nodes(face)] = 1.0
    return pick, pick.T.copy(), pick @ pick.T


def dot(a, b):
    return lax.dot_general(a, b, (((1,), (0,)), ((), ())), preferred_element_type=F32)


def dot_nt(a, b):
    return lax.dot_general(a, b, (((1,), (1,)), ((), ())), preferred_element_type=F32)


def split(value):
    high = value.astype(BF16)
    return high, (value - high.astype(F32)).astype(BF16)


def iota(shape, dim):
    return lax.broadcasted_iota(jnp.int32, shape, dim)


def one_hot(rows, code):
    return jnp.where(iota((rows, code.shape[1]), 0).astype(F32) == code, 1.0, 0.0).astype(BF16)


def pick_face(sides, face):
    out = None
    for f in range(6):
        part = jnp.where(face == float(f), sides[f * FR : (f + 1) * FR], 0.0)
        out = part if out is None else out + part
    return out


def spread_face(values, face):
    return jnp.concatenate([jnp.where(face == float(f), values, 0.0) for f in range(6)], axis=0)


def spread_split(values, face):
    high = values.astype(BF16).astype(F32)
    return spread_face(high, face).astype(BF16), spread_face(values - high, face).astype(BF16)


def by_subface(values, sub):
    return jnp.concatenate([jnp.where(sub == float(s), values, 0.0) for s in range(4)], axis=0).astype(BF16)


def column_sums(a, b):
    prod = a * b
    rows = jnp.sum(prod, axis=0, keepdims=True)
    return sum(rows[:, t * EB : (t + 1) * EB] for t in range(EA))


def kernel(
    n_gx,
    n_gy,
    b_hbm,
    stiff_hbm,
    metric_hbm,
    fine_hbm,
    face_hbm,
    owner_hbm,
    sub_hbm,
    coarse_hbm,
    cface_hbm,
    level_hbm,
    proj_hbm,
    pick_hbm,
    place_hbm,
    mix_hbm,
    q_ref,
    w_ref,
    coef_ref,
    b_ref,
    stiff_ref,
    metric_ref,
    ints_ref,
    proj_ref,
    pick_ref,
    place_ref,
    mix_ref,
    halo_x,
    halo_y,
    own_m,
    own_x,
    own_y,
    stiff_s,
    oh_self,
    oh_x,
    n_out,
    n_in,
    proj_s,
    proj_c,
    proj_t,
    red1,
    mine0,
    in_sem,
    sx_send,
    sx_recv,
    sy_send,
    sy_recv,
    ready_sem,
    s1_send,
    s1_recv,
):
    gx = lax.axis_index("gx")
    gy = lax.axis_index("gy")

    int_names = (fine_hbm, face_hbm, owner_hbm, sub_hbm, coarse_hbm, cface_hbm, level_hbm)
    loads = [(source, ints_ref.at[k]) for k, source in enumerate(int_names)]
    loads += [(b_hbm, b_ref), (pick_hbm, pick_ref), (proj_hbm, proj_ref), (mix_hbm, mix_ref)]
    loads += [(stiff_hbm, stiff_ref), (metric_hbm, metric_ref), (place_hbm, place_ref)]
    loads = [pltpu.make_async_copy(source, target, in_sem.at[k]) for k, (source, target) in enumerate(loads)]
    for load in loads:
        load.start()

    def there(d):
        dx, dy = DIRS[d]
        ok = (gx + dx >= 0) & (gx + dx < n_gx) & (gy + dy >= 0) & (gy + dy < n_gy)
        return ok, {"gx": gx + dx, "gy": gy + dy}

    def if_there(d, act):
        pl.when(there(d)[0])(act)

    size_x, size_y, size_z = n_gx // 2, n_gy // 4, 4
    chips = [(i, j, k) for i in range(size_x) for j in range(size_y) for k in range(size_z)][1:]
    chips.sort(key=lambda c: sum((v - 1) % n for v, n in zip(c, (size_x, size_y, size_z))))

    def chip(offset):
        y, z = gy // size_z, lax.rem(gy, size_z)
        return {
            "gx": lax.rem(gx + 2 * offset[0], n_gx),
            "gy": lax.rem(y + offset[1], size_y) * size_z + lax.rem(z + offset[2], size_z),
        }

    halo_x[...] = jnp.zeros_like(halo_x)
    halo_y[...] = jnp.zeros_like(halo_y)

    barrier = pltpu.get_barrier_semaphore()
    expected = jnp.int32(0)
    for d in DIRS:
        ok, where = there(d)

        @pl.when(ok)
        def _():
            pl.semaphore_signal(barrier, inc=1, device_id=where, device_id_type=MESH)

        expected = expected + ok.astype(jnp.int32)

    def x_copy(t, side, arriving):
        slot = side if arriving else 1 - side
        rows = pl.ds(0, FACES + 8 * (1 - t))
        return pltpu.make_async_remote_copy(
            src_ref=own_x.at[t, side, rows],
            dst_ref=halo_x.at[t, slot, rows],
            send_sem=sx_send.at[t, side],
            recv_sem=sx_recv.at[t, slot],
            device_id=there((1, 7)[side])[1],
            device_id_type=MESH,
        )

    def y_copy(t, index, arriving):
        d = EDGE_DIRS[index]
        slot = index if arriving else EDGE_DIRS.index(8 - d)
        rows = pl.ds(0, 8 + 8 * (1 - t))
        return pltpu.make_async_remote_copy(
            src_ref=own_y.at[t, index, rows],
            dst_ref=halo_y.at[t, slot, rows],
            send_sem=sy_send.at[t, index],
            recv_sem=sy_recv.at[t, slot],
            device_id=there(d)[1],
            device_id_type=MESH,
        )

    strides = [k for k in (1, 2, 4, 8, 16) if k < max(n_gx, n_gy)]

    def partners(k):
        by = strides[k]
        for dx in (-by, 0, by) if by < n_gx else (0,):
            for dy in (-by, 0, by) if by < n_gy else (0,):
                if dx or dy:
                    ok = (gx + dx >= 0) & (gx + dx < n_gx) & (gy + dy >= 0) & (gy + dy < n_gy)
                    yield ok, {"gx": gx + dx, "gy": gy + dy}

    def pass_on(k):
        for ok, where in partners(k):

            @pl.when(ok)
            def _():
                pl.semaphore_signal(ready_sem.at[k], inc=1, device_id=where, device_id_type=MESH)

    pending = list(range(len(strides)))

    def learn():
        if pending:
            k = pending.pop(0)
            pl.semaphore_wait(ready_sem.at[k], sum(ok.astype(jnp.int32) for ok, _ in partners(k)))
            if pending:
                pass_on(k + 1)

    def send(t):
        for index in (2, 3, 4, 5, 0, 1):
            if_there(EDGE_DIRS[index], lambda: y_copy(t, index, False).start())
        for side in range(2):
            if_there((1, 7)[side], lambda: x_copy(t, side, False).start())

    lane = iota((1, 128), 1)
    lane_face = lane >> 4
    lane_pair = lane & 15

    def stacked_table(value):
        high = value.astype(BF16)
        rest = value - high.astype(F32)
        return high, jnp.concatenate([high.astype(F32), rest], axis=0).astype(BF16)

    def by_table(table, value_h, value_l):
        high, both = table
        rows = high.shape[0]
        first = dot(both, value_h)
        return first[:rows] + first[rows:] + dot(high, value_l)

    def code(entry, active):
        return jnp.where(active > 0.0, entry, -1.0)

    for load in loads[:9]:
        load.wait()
    fine, face, owner, sub, coarse, cface, level = (ints_ref[k] for k in range(7))
    shift = n_gy.bit_length() - 1
    slot = ((owner >> shift) - gx + 1) * 3 + (owner & (n_gy - 1)) - gy + 1
    count = fine.shape[1]
    hits = jnp.where(iota((16, count), 0) == slot, 1.0, 0.0)
    parts = [hits[:, k : k + EB] for k in range(0, count, EB)]
    earlier = jnp.where(iota((EB, EB), 0) < iota((EB, EB), 1), 1.0, 0.0).astype(BF16)
    within = dot(jnp.concatenate(parts, axis=0).astype(BF16), earlier)
    offset, ranks = jnp.zeros((16, 1), F32), []
    for k, part in enumerate(parts):
        ranks.append(jnp.sum(part * (within[16 * k : 16 * k + 16] + offset), axis=0, keepdims=True))
        offset = offset + jnp.sum(part, axis=1, keepdims=True)
    position = jnp.concatenate(ranks, axis=1)
    row = iota((8, count), 0)
    facts = jnp.ones((8, count), jnp.int32)
    for index, entry in enumerate((fine >> 7, fine & 127, face, coarse >> 7, coarse & 127, cface, sub)):
        facts = jnp.where(row == index, entry, facts)
    facts = facts.astype(F32)
    stacked = jnp.concatenate([facts * hits[k : k + 1] for k in range(9)], axis=0).astype(BF16)
    packed = dot_nt(stacked, one_hot(EB, position))
    for k in range(9):
        own_m[k] = packed[8 * k : 8 * k + 8]
    for side in range(2):
        d = (1, 7)[side]
        own_x[0, side, FACES : FACES + 8, :] = packed[8 * d : 8 * d + 8]
    for index, d in enumerate(EDGE_DIRS):
        own_y[0, index, 8:16, :] = packed[8 * d : 8 * d + 8]
    scale = jnp.where(level == 0, 1.0, jnp.where(level == 1, 0.5, 0.25))

    def face_product(table, value):
        high, low = split(value)
        return dot(table, high) + dot(table, low)

    def edge_ends(faces):
        ends = faces[:, 0:EB]
        for a in range(1, EA):
            moved = pltpu.roll(faces[:, a * EB : (a + 1) * EB], 2 * a, 1)
            ends = jnp.where((lane == 2 * a) | (lane == 2 * a - 1), moved, ends)
        return ends

    def edge_values(ends):
        own = jnp.zeros((FR, 128), F32)
        for f in range(6):
            moved = pltpu.roll(ends[f * FR : (f + 1) * FR], 16 * f + 1, 1)
            own = jnp.where((lane_face == f) & (lane_pair < 8), moved, own)
        rows = own
        for pair, by in CORNER_SHIFT.items():
            own = jnp.where(lane_pair == pair, pltpu.roll(rows, by, 1), own)
        return own

    def lanes_of(start):
        return (lane >= start) & (lane < start + 8) & ((lane & 1) == start % 2)

    def pack(part, turn):
        result = jnp.zeros((8, 128), F32)
        for (f, g), start in PACK.items():
            result = jnp.where(lanes_of(start), pltpu.roll(part(f, g), (start + turn(f)) % 128, 1), result)
        return result

    def pack_pairs(values, first):
        return pack(lambda f, g: values[8 * g : 8 * g + 8], lambda f: -16 * f - first)

    def corner_lanes(c):
        return ((lane & 7) >> 1) == c

    def edge_across(t):
        corners = jnp.zeros((8, 128), F32)
        for c, a in enumerate(CORNER_ROWS):
            moved = pltpu.roll(halo_y[t, 2 + c, 0:8, :], 2 * (c - a) % 128, 1)
            corners = jnp.where(corner_lanes(c), moved, corners)
        groups = []
        for g in range(FR // 8):
            group = jnp.zeros((8, 128), F32)
            for packed_rows, first in ((halo_y[t, 0, 0:8, :], 1), (halo_y[t, 1, 0:8, :], 0), (corners, 8)):
                for f in range(6):
                    moved = pltpu.roll(packed_rows, (16 * f + first - PACK[f, g]) % 128, 1)
                    group = jnp.where(lanes_of(16 * f + first), moved, group)
            groups.append(group)
        return jnp.concatenate(groups, axis=0)

    def edge_spread(values):
        rows = jnp.where(lane_pair < 8, values, 0.0)
        for pair, by in CORNER_SHIFT.items():
            rows = rows + jnp.where(lane_pair == pair - by, pltpu.roll(values, 128 - by, 1), 0.0)
        ends = jnp.concatenate([pltpu.roll(rows, 127 - 16 * f, 1) for f in range(6)], axis=0)
        tiles = []
        for a in range(EA):
            moved = pltpu.roll(ends, 128 - 2 * a, 1) if a else ends
            tiles.append(jnp.where((lane == 0) | (lane == EB - 1), moved, 0.0))
        return tiles

    def publish(t, faces):
        own_x[t, 0, 0:FACES, :] = faces[:, 0:EB]
        own_x[t, 1, 0:FACES, :] = faces[:, (EA - 1) * EB :]
        ends = edge_ends(faces)

        def rows(f, g):
            return ends[f * FR + 8 * g : f * FR + 8 * g + 8]

        toward = (pack(rows, lambda f: 0), pack(rows, lambda f: 1))
        for index, d in enumerate(EDGE_DIRS):
            own_y[t, index, 0:8, :] = toward[0 if DIRS[d][1] < 0 else 1]
        return ends

    b = b_ref[...]
    faces = face_product(pick_ref[...], b)
    ends = publish(0, faces)

    pl.semaphore_wait(barrier, expected)
    send(0)
    pass_on(0)
    own = edge_values(ends)

    for load in loads[9:]:
        load.wait()
    for d in range(3):
        padded = jnp.concatenate([stiff_ref[d], jnp.zeros((SP - NODES, NODES), F32)], axis=0)
        high, low = split(padded)
        stiff_s[d * SP : (d + 1) * SP, :] = high
        stiff_s[(3 + d) * SP : (4 + d) * SP, :] = low
    proj_s[...] = jnp.zeros_like(proj_s)
    proj_c[...] = jnp.zeros_like(proj_c)
    for s in range(4):
        table = proj_ref[:, s, :]
        proj_s[s * FR : s * FR + SIDE, 0:SIDE] = table
        proj_c[0:SIDE, s * FR : s * FR + SIDE] = table
    proj_t[...] = proj_s[...].T[0:FR]
    table_s = stacked_table(proj_s[0 : 4 * FR, 0:FR])
    table_c = stacked_table(proj_c[:, 0 : 4 * FR])
    table_t = stacked_table(proj_t[:, 0 : 4 * FR])

    me = own_m[4]
    self_fine = code(me[0:1] * float(EB) + me[1:2], me[7:8])
    self_coarse = code(me[3:4] * float(EB) + me[4:5], me[7:8])
    oh_self[...] = one_hot(ELEMS, jnp.concatenate([self_fine, self_coarse], axis=1))

    wide = iota((32, 512), 1)
    repeat = jnp.where(iota((32, 512), 0) == (wide >> 7) * 8 + ((wide >> 4) & 7), 1.0, 0.0).astype(BF16)
    same_pair = (iota((128, 512), 0) & 15) == (iota((128, 512), 1) & 15)
    ones = jnp.ones((16, 6 * EB), BF16)

    def edge_counts(held):
        parts_f, parts_c = [], []
        for d, facts_d in zip(EDGE_DIRS, held):
            if d in (3, 5):
                pair = facts_d[0:1] * 2.0 + (1.0 if d == 3 else 0.0)
            else:
                pair = float(CORNERS[d])
            parts_f.append(code(facts_d[2:3] * 16.0 + pair, facts_d[7:8]))
            parts_c.append(code(facts_d[6:7] * 8.0 + facts_d[5:6], facts_d[7:8]))
        fine_hot = one_hot(128, jnp.concatenate(parts_f, axis=1))
        coarse_hot = one_hot(32, jnp.concatenate(parts_c, axis=1))
        joined = dot(dot_nt(fine_hot, coarse_hot).astype(BF16), repeat)
        return jnp.where(same_pair, joined, 0.0).astype(BF16), dot_nt(ones, fine_hot)[0:1]

    n_out[...], sum_out = edge_counts([own_m[d] for d in EDGE_DIRS])

    def mortar_jump(coarses, fines, subs):
        high = coarses.astype(BF16).astype(F32)
        return by_table(table_c, by_subface(high, subs), by_subface(coarses - high, subs)) - fines

    def mortar_back(jump, subs):
        high = jump.astype(BF16).astype(F32)
        return by_table(table_t, by_subface(high, subs), by_subface(jump - high, subs))

    def local_part(field, faces):
        f_h, f_l = split(faces)
        got = dot(f_h, oh_self[...]) + dot(f_l, oh_self[...])
        jump = mortar_jump(pick_face(got[:, EB:], me[5:6]), pick_face(got[:, 0:EB], me[2:3]), me[6:7])
        back = mortar_back(jump, me[6:7])
        terms = jnp.concatenate([-PENALTY * jump, PENALTY * back], axis=1)
        s_h, s_l = spread_split(terms, jnp.concatenate([me[2:3], me[5:6]], axis=1))
        gathered = dot_nt(s_h, oh_self[...]) + dot_nt(s_l, oh_self[...])

        blocks = []
        for a in range(EA):
            here = slice(a * EB, (a + 1) * EB)
            x_low, x_high = faces[0:FR, here], faces[FR : 2 * FR, here]
            y_low, y_high = faces[2 * FR : 3 * FR, here], faces[3 * FR : 4 * FR, here]
            left = x_low if a == 0 else x_low - faces[FR : 2 * FR, (a - 1) * EB : a * EB]
            right = x_high if a == EA - 1 else x_high - faces[0:FR, (a + 1) * EB : (a + 2) * EB]
            below = jnp.where(lane == 0, 0.0, pltpu.roll(y_high, 1, 1))
            above = jnp.where(lane == EB - 1, 0.0, pltpu.roll(y_low, EB - 1, 1))
            lateral = jnp.concatenate([left, right, y_low - below, y_high - above], axis=0)
            blocks.append(jnp.concatenate([PENALTY * lateral, jnp.zeros((2 * FR, EB), F32)], axis=0))
        gathered = gathered + jnp.concatenate(blocks, axis=1)

        field_h, field_l = split(field)
        both = dot(stiff_s[...], field_h)
        rest = dot(stiff_s[0 : 3 * SP, :], field_l)
        total = field
        for d in range(3):
            here = slice(d * SP, d * SP + NODES)
            again = slice((3 + d) * SP, (3 + d) * SP + NODES)
            total = total + metric_ref[d : d + 1, :] * (both[here] + both[again] + rest[here])
        return scale * total, gathered

    def side_jumps(faces):
        for side in range(2):
            d = (1, 7)[side]
            both = jnp.concatenate([own_m[d], halo_x[0, side, FACES : FACES + 8, :]], axis=1)
            oh_x[side] = one_hot(EB, code(both[1:2], both[7:8]))
        fines, coarses, subs = [], [], []
        for side in range(2):
            d = (1, 7)[side]
            theirs_m = halo_x[0, side, FACES : FACES + 8, :]
            here = slice(0, EB) if side == 0 else slice((EA - 1) * EB, EA * EB)
            pair = jnp.concatenate([faces[:, here], halo_x[0, side, 0:FACES, :]], axis=0)
            high, low = split(pair)
            got = dot(high, oh_x[side]) + dot(low, oh_x[side])
            ours, theirs = got[0:FACES], got[FACES:]
            fines += [pick_face(ours[:, 0:EB], own_m[d][2:3]), pick_face(theirs[:, EB:], theirs_m[2:3])]
            coarses += [pick_face(theirs[:, 0:EB], own_m[d][5:6]), pick_face(ours[:, EB:], theirs_m[5:6])]
            subs += [own_m[d][6:7], theirs_m[6:7]]
        jump = mortar_jump(*(jnp.concatenate(parts, axis=1) for parts in (coarses, fines, subs)))
        jump = [jump[:, k * EB : (k + 1) * EB] for k in range(4)]
        return jump, subs

    def side_adjoint(faces):
        fines, coarses, subs = [], [], []
        for side in range(2):
            d = (1, 7)[side]
            theirs_m = halo_x[0, side, FACES : FACES + 8, :]
            high, low = split(faces[:, 0:EB] if side == 0 else faces[:, (EA - 1) * EB :])
            got = dot(high, oh_x[side]) + dot(low, oh_x[side])
            fines.append(pick_face(got[:, 0:EB], own_m[d][2:3]))
            coarses.append(pick_face(got[:, EB:], theirs_m[5:6]))
            subs += [own_m[d][6:7], theirs_m[6:7]]
        fines = jnp.concatenate(fines, axis=1)
        images = mortar_jump(jnp.concatenate(coarses, axis=1), 0.0, jnp.concatenate([subs[1], subs[3]], axis=1))
        backs = mortar_back(fines, jnp.concatenate([subs[0], subs[2]], axis=1))
        against = []
        for side in range(2):
            d = (1, 7)[side]
            here = slice(side * EB, (side + 1) * EB)
            theirs_m = halo_x[0, side, FACES : FACES + 8, :]
            s_h, s_l = spread_split(
                jnp.concatenate([backs[:, here], images[:, here]], axis=1),
                jnp.concatenate([own_m[d][5:6], theirs_m[2:3]], axis=1),
            )
            against.append(dot_nt(s_h, oh_x[side]) + dot_nt(s_l, oh_x[side]))
        low_face, high_face = faces[0:FR, 0:EB], faces[FR : 2 * FR, (EA - 1) * EB :]
        against[0] = against[0] + jnp.concatenate([jnp.zeros((FR, EB), F32), low_face, jnp.zeros((4 * FR, EB), F32)], axis=0)
        against[1] = against[1] + jnp.concatenate([high_face, jnp.zeros((5 * FR, EB), F32)], axis=0)
        known = jnp.sum(fines * fines + images * images, axis=0, keepdims=True)
        return fines, images, subs, against, known[:, 0:EB] + known[:, EB:]

    def side_jumps_after(fines, images, subs):
        far_fines, far_coarses = [], []
        for side in range(2):
            d = (1, 7)[side]
            theirs_m = halo_x[0, side, FACES : FACES + 8, :]
            high, low = split(halo_x[1, side, 0:FACES, :])
            got = dot(high, oh_x[side]) + dot(low, oh_x[side])
            far_coarses.append(pick_face(got[:, 0:EB], own_m[d][5:6]))
            far_fines.append(pick_face(got[:, EB:], theirs_m[2:3]))
        out = mortar_jump(
            jnp.concatenate(far_coarses, axis=1), fines, jnp.concatenate([subs[0], subs[2]], axis=1)
        )
        into = images - jnp.concatenate(far_fines, axis=1)
        return [out[:, 0:EB], into[:, 0:EB], out[:, EB:], into[:, EB:]]

    def side_terms(t, jump, subs):
        back = mortar_back(jnp.concatenate([jump[1], jump[3]], axis=1), jnp.concatenate([subs[1], subs[3]], axis=1))
        result = []
        for side in range(2):
            d = (1, 7)[side]
            terms = jnp.concatenate(
                [-PENALTY * jump[2 * side], PENALTY * back[:, side * EB : (side + 1) * EB]], axis=1
            )
            theirs_m = halo_x[0, side, FACES : FACES + 8, :]
            s_h, s_l = spread_split(terms, jnp.concatenate([own_m[d][2:3], theirs_m[5:6]], axis=1))
            side_term = dot_nt(s_h, oh_x[side]) + dot_nt(s_l, oh_x[side])
            if side == 0:
                beside = [-PENALTY * halo_x[t, 0, FR : 2 * FR, :], jnp.zeros((5 * FR, EB), F32)]
            else:
                beside = [jnp.zeros((FR, EB), F32), -PENALTY * halo_x[t, 1, 0:FR, :], jnp.zeros((4 * FR, EB), F32)]
            result.append(side_term + jnp.concatenate(beside, axis=0))
        return result

    low_face = (lane_face == 2) & (lane_pair < 8) & ((lane_pair & 1) == 1)
    high_face = (lane_face == 3) & (lane_pair < 8) & ((lane_pair & 1) == 0)

    def edges_arrive(t):
        for index in range(6):
            if_there(EDGE_DIRS[index], lambda: y_copy(t, index, True).wait_recv())

    def sides_arrive(t):
        for side in range(2):
            if_there((1, 7)[side], lambda: x_copy(t, side, True).wait_recv())

    def edge_jumps(t, own, sum_in):
        across = edge_across(t)
        pairs = jnp.concatenate([own, across], axis=1)
        pairs_h, pairs_l = split(pairs)
        images = by_table(table_s, pairs_h, pairs_l)
        image_own = jnp.concatenate([images[s * FR : (s + 1) * FR, 0:128] for s in range(4)], axis=1)
        image_far = jnp.concatenate([images[s * FR : (s + 1) * FR, 128:] for s in range(4)], axis=1)
        far_h, far_l = split(image_far)
        on_fine = own * sum_out - dot_nt(far_h, n_out[...]) - dot_nt(far_l, n_out[...])
        jumps = image_own * sum_in - dot(pairs_h[:, 128:], n_in[...]) - dot(pairs_l[:, 128:], n_in[...])
        from_low = pltpu.roll(across, 128 - 16, 1)
        from_high = pltpu.roll(across, 16, 1)
        beside = jnp.where(low_face, from_low, jnp.where(high_face, from_high, 0.0))
        return PENALTY * (on_fine - beside), jumps

    def edge_adjoint(own, sum_in):
        own_h, own_l = split(own)
        images = by_table(table_s, own_h, own_l)
        images = jnp.concatenate([images[s * FR : (s + 1) * FR] for s in range(4)], axis=1)
        images_h, images_l = split(images)
        joined = dot(own_h, n_out[...]) + dot(own_l, n_out[...])
        joined_h, joined_l = split(jnp.concatenate([joined[:, s * 128 : (s + 1) * 128] for s in range(4)], axis=0))
        meets = by_table(table_t, joined_h, joined_l) + dot_nt(images_h, n_in[...]) + dot_nt(images_l, n_in[...])
        meets = meets + pltpu.roll(jnp.where(low_face, own, 0.0), 16, 1)
        meets = meets + pltpu.roll(jnp.where(high_face, own, 0.0), 128 - 16, 1)
        against = [pack_pairs(meets, 1), pack_pairs(meets, 0)]
        corners = pack_pairs(meets, 8)
        for c, a in enumerate(CORNER_ROWS):
            against.append(pltpu.roll(jnp.where(corner_lanes(c), corners, 0.0), 2 * (a - c) % 128, 1))
        known = jnp.sum(own * own * sum_out, axis=0, keepdims=True)
        both = jnp.sum(images * images * sum_in, axis=0, keepdims=True)
        return against, known + sum(both[:, s * 128 : (s + 1) * 128] for s in range(4))

    def edge_terms(direct, jumps):
        jumps = jnp.concatenate([jumps[:, s * 128 : (s + 1) * 128] for s in range(4)], axis=0)
        jumps_h, jumps_l = split(jumps)
        return edge_spread(direct + PENALTY * by_table(table_t, jumps_h, jumps_l))

    def placed(value):
        return face_product(place_ref[...], value)

    learn()
    b = b_ref[...]
    total, gathered = local_part(b, faces)
    total = total + placed(gathered)
    started = face_product(pick_ref[...], total)
    learn()
    sides_arrive(0)
    jump, subs = side_jumps(faces)
    sides = side_terms(0, jump, subs)
    edges_arrive(0)
    n_in[...], _ = edge_counts([halo_y[0, index, 8:16, :] for index in range(6)])
    sum_in = dot(jnp.ones((16, 128), BF16), n_in[...])[0:1]
    direct, jumps = edge_jumps(0, own, sum_in)
    tiles = edge_terms(direct, jumps)
    tiles[0] = tiles[0] + sides[0]
    tiles[EA - 1] = tiles[EA - 1] + sides[1]
    remote = jnp.concatenate(tiles, axis=1)
    faces = started + face_product(mix_ref[...], remote)
    ends = publish(1, faces)
    send(1)
    learn()
    own = edge_values(ends)
    q = total + placed(remote)
    q_ref[...] = q

    total, gathered = local_part(q, faces)
    b = b_ref[...]
    q = q_ref[...]
    early = [column_sums(b, b), column_sums(b, q), column_sums(q, q)]
    energy = column_sums(q, total) + column_sums(faces, gathered)
    fines, images, subs, side_against, known = side_adjoint(faces)
    energy = energy + PENALTY * known
    edge_against, known = edge_adjoint(own, sum_in)
    energy = energy + PENALTY * known
    sides_arrive(1)
    met = jnp.zeros((1, 128), F32)
    for side in range(2):
        met = met + jnp.sum(halo_x[1, side, 0:FACES, :] * side_against[side], axis=0, keepdims=True)
    energy = energy - PENALTY * met
    edges_arrive(1)
    met = sum(halo_y[1, index, 0:8, :] * edge_against[index] for index in range(6))
    energy = energy - PENALTY * jnp.sum(met, axis=0, keepdims=True)

    lanes = jnp.zeros((1, 128), F32)
    for index, sums in enumerate(early + [energy]):
        lanes = jnp.where(lane == index, jnp.sum(sums, axis=1, keepdims=True), lanes)
    mine0[...] = lanes
    while pending:
        learn()
    others = [(c, o) for o in [(0, 0, 0)] + chips for c in range(2) if c or o != (0, 0, 0)]
    others.sort(key=lambda t: sum((v - 1) % n for v, n in zip(t[1], (size_x, size_y, size_z))))
    for k, (flip, offset) in enumerate(others):
        where = chip(offset)
        if flip:
            core = lax.rem(gx, 2)
            where["gx"] = where["gx"] + 1 - 2 * core
        pltpu.make_async_remote_copy(
            src_ref=mine0,
            dst_ref=red1.at[k],
            send_sem=s1_send,
            recv_sem=s1_recv,
            device_id=where,
            device_id_type=MESH,
        ).start()

    sides = side_terms(1, side_jumps_after(fines, images, subs), subs)
    tiles = edge_terms(*edge_jumps(1, own, sum_in))
    tiles[0] = tiles[0] + sides[0]
    tiles[EA - 1] = tiles[EA - 1] + sides[1]
    w_ref[...] = total + placed(gathered + jnp.concatenate(tiles, axis=1))
    for t in range(2):
        for side in range(2):
            if_there((1, 7)[side], lambda: x_copy(t, side, False).wait_send())
        for index in range(6):
            if_there(EDGE_DIRS[index], lambda: y_copy(t, index, False).wait_send())

    pltpu.make_async_copy(red1, red1, s1_recv).wait()
    lanes = lanes + jnp.sum(red1[...], axis=0)
    bb, bq, qq, qw = (lanes[:, i : i + 1] for i in range(4))
    alpha = bb / bq
    new = bb - 2.0 * alpha * bq + alpha * alpha * qq
    grow = 1.0 + new / bb
    alpha_next = new / (grow * grow * bq - 2.0 * grow * alpha * qq + alpha * alpha * qw)
    row = iota((8, 128), 0)
    coef_ref[...] = jnp.where(row == 0, alpha + alpha_next * grow, alpha * alpha_next)
    pltpu.make_async_copy(red1, red1, s1_send).wait()


def finish(coef_ref, b_ref, q_ref, w_ref, x_hbm, r_hbm, made, out_sem):
    first, second = coef_ref[0:1, 0:1], coef_ref[1:2, 0:1]
    stores = []
    for part, (start, size) in enumerate(((0, 104), (104, NODES - 104))):
        rows = pl.ds(start, size)
        b, q, w = b_ref[rows, :], q_ref[rows, :], w_ref[rows, :]
        made[0, rows, :] = first * b - second * q
        made[1, rows, :] = b - first * q + second * w
        for k, target in enumerate((x_hbm, r_hbm)):
            store = pltpu.make_async_copy(made.at[k, rows], target.at[rows], out_sem.at[part, k])
            store.start()
            stores.append(store)
    for store in stores:
        store.wait()


def body(
    n_gx,
    n_gy,
    right_side,
    stiffness,
    metric,
    levels,
    projection,
    mortar_fine,
    mortar_face,
    mortar_owner,
    mortar_subface,
    mortar_coarse,
    mortar_cface,
):
    pick, place, mix = (jnp.asarray(table, BF16) for table in constant_tables())
    field = jax.ShapeDtypeStruct(right_side.shape, F32)
    count = mortar_fine.shape[0]
    others = n_gx * n_gy - 1
    hbm = pl.BlockSpec(memory_space=pltpu.HBM)
    vmem = pl.BlockSpec(memory_space=pltpu.VMEM)
    dma = pltpu.SemaphoreType.DMA
    line = [
        entry.reshape(1, count)
        for entry in (
            mortar_fine,
            mortar_face,
            mortar_owner,
            mortar_subface,
            mortar_coarse,
            mortar_cface,
            levels,
        )
    ]
    q, w, coef = pl.pallas_call(
        functools.partial(kernel, n_gx, n_gy),
        out_shape=(field, field, jax.ShapeDtypeStruct((8, 128), F32)),
        in_specs=[hbm] * 14,
        out_specs=(vmem, vmem, vmem),
        scratch_shapes=[
            pltpu.VMEM((NODES, ELEMS), F32),
            pltpu.VMEM((3, NODES, NODES), F32),
            pltpu.VMEM((3, ELEMS), F32),
            pltpu.VMEM((7, 1, ELEMS), jnp.int32),
            pltpu.VMEM((SIDE, 4, SIDE), F32),
            pltpu.VMEM((FACES, NODES), BF16),
            pltpu.VMEM((NODES, FACES), BF16),
            pltpu.VMEM((FACES, FACES), BF16),
            pltpu.VMEM((2, 2, FACES + 8, EB), F32),
            pltpu.VMEM((2, 6, 16, 128), F32),
            pltpu.VMEM((9, 8, 128), F32),
            pltpu.VMEM((2, 2, FACES + 8, EB), F32),
            pltpu.VMEM((2, 6, 16, 128), F32),
            pltpu.VMEM((6 * SP, NODES), BF16),
            pltpu.VMEM((ELEMS, 2 * EB), BF16),
            pltpu.VMEM((2, EB, 2 * EB), BF16),
            pltpu.VMEM((128, 512), BF16),
            pltpu.VMEM((128, 512), BF16),
            pltpu.VMEM((256, 128), F32),
            pltpu.VMEM((FR, 256), F32),
            pltpu.VMEM((FR, 256), F32),
            pltpu.VMEM((others, 1, 128), F32),
            pltpu.VMEM((1, 128), F32),
            dma((14,)),
            dma((2, 2)),
            dma((2, 2)),
            dma((2, 6)),
            dma((2, 6)),
            pltpu.SemaphoreType.REGULAR((8,)),
            dma,
            dma,
        ],
        compiler_params=pltpu.CompilerParams(
            collective_id=0, has_side_effects=True, vmem_limit_bytes=40 * 1024 * 1024
        ),
    )(
        *(
            pltpu.with_memory_space_constraint(operand, pltpu.HBM)
            for operand in (right_side, stiffness, metric, *line, projection.transpose(1, 0, 2), pick, place, mix)
        )
    )
    return pl.pallas_call(
        finish,
        out_shape=(field, field),
        in_specs=[vmem] * 4,
        out_specs=(hbm, hbm),
        scratch_shapes=[pltpu.VMEM((2, NODES, ELEMS), F32), dma((2, 2))],
        compiler_params=pltpu.CompilerParams(vmem_limit_bytes=40 * 1024 * 1024),
    )(coef, right_side, q, w)


def solution(mesh):
    columns = P(None, ("gx", "gy"))
    faces = P(("gx", "gy"))
    in_specs = (columns, P(), columns, faces, P(), faces, faces, P(("gx", "gy"), None), faces, faces, faces)
    run = functools.partial(body, mesh.shape["gx"], mesh.shape["gy"])
    return jax.shard_map(run, mesh=mesh, in_specs=in_specs, out_specs=(columns, columns), check_vma=False)
```

```python
import functools

import jax
import jax.numpy as jnp
import numpy as np
from jax import lax
from jax.experimental import pallas as pl
from jax.experimental.pallas import tpu as pltpu
from jax.sharding import PartitionSpec as P

NP = 6
NODES = NP * NP * NP
SIDE = NP * NP
EA = 4
EB = 128
ELEMS = EA * EB
FR = 40
FACES = 6 * FR
SP = 224
PENALTY = 1.0

F32 = jnp.float32
BF16 = jnp.bfloat16
MESH = pl.DeviceIdType.MESH

DIRS = {d: (d // 3 - 1, d % 3 - 1) for d in range(9) if d != 4}
EDGE_DIRS = (3, 5, 0, 2, 6, 8)
CORNERS = {0: 8, 2: 10, 6: 12, 8: 14}
CORNER_SHIFT = {8: 7, 10: 10, 12: 5, 14: 8}
PACK = {(f, g): 8 * ((5 * f + g) // 2) + (5 * f + g) % 2 for f in range(6) for g in range(FR // 8)}
CORNER_ROWS = (EA - 1, EA - 1, 0, 0)


def face_nodes(face):
    ids = np.arange(NODES).reshape(NP, NP, NP)
    return [ids[0], ids[5], ids[:, 0], ids[:, 5], ids[:, :, 0], ids[:, :, 5]][face].reshape(-1)


def constant_tables():
    pick = np.zeros((FACES, NODES), np.float32)
    for face in range(6):
        pick[face * FR + np.arange(SIDE), face_nodes(face)] = 1.0
    return pick, pick.T.copy(), pick @ pick.T


def dot(a, b):
    return lax.dot_general(a, b, (((1,), (0,)), ((), ())), preferred_element_type=F32)


def dot_nt(a, b):
    return lax.dot_general(a, b, (((1,), (1,)), ((), ())), preferred_element_type=F32)


def split(value):
    high = value.astype(BF16)
    return high, (value - high.astype(F32)).astype(BF16)


def iota(shape, dim):
    return lax.broadcasted_iota(jnp.int32, shape, dim)


def one_hot(rows, code):
    return jnp.where(iota((rows, code.shape[1]), 0).astype(F32) == code, 1.0, 0.0).astype(BF16)


def pick_face(sides, face):
    out = None
    for f in range(6):
        part = jnp.where(face == float(f), sides[f * FR : (f + 1) * FR], 0.0)
        out = part if out is None else out + part
    return out


def spread_face(values, face):
    return jnp.concatenate([jnp.where(face == float(f), values, 0.0) for f in range(6)], axis=0)


def spread_split(values, face):
    high = values.astype(BF16).astype(F32)
    return spread_face(high, face).astype(BF16), spread_face(values - high, face).astype(BF16)


def by_subface(values, sub):
    return jnp.concatenate([jnp.where(sub == float(s), values, 0.0) for s in range(4)], axis=0).astype(BF16)


def column_sums(a, b):
    prod = a * b
    rows = jnp.sum(prod, axis=0, keepdims=True)
    return sum(rows[:, t * EB : (t + 1) * EB] for t in range(EA))


def kernel(
    n_gx,
    n_gy,
    b_hbm,
    stiff_hbm,
    metric_hbm,
    fine_hbm,
    face_hbm,
    owner_hbm,
    sub_hbm,
    coarse_hbm,
    cface_hbm,
    level_hbm,
    proj_hbm,
    pick_hbm,
    place_hbm,
    mix_hbm,
    q_ref,
    w_ref,
    coef_ref,
    b_ref,
    stiff_ref,
    metric_ref,
    ints_ref,
    proj_ref,
    pick_ref,
    place_ref,
    mix_ref,
    halo_x,
    halo_y,
    own_m,
    own_x,
    own_y,
    stiff_s,
    oh_self,
    oh_x,
    n_out,
    n_in,
    proj_s,
    proj_c,
    proj_t,
    red1,
    mine0,
    in_sem,
    sx_send,
    sx_recv,
    sy_send,
    sy_recv,
    ready_sem,
    s1_send,
    s1_recv,
):
    gx = lax.axis_index("gx")
    gy = lax.axis_index("gy")

    int_names = (fine_hbm, face_hbm, owner_hbm, sub_hbm, coarse_hbm, cface_hbm, level_hbm)
    loads = [(source, ints_ref.at[k]) for k, source in enumerate(int_names)]
    loads += [(b_hbm, b_ref), (pick_hbm, pick_ref), (proj_hbm, proj_ref), (mix_hbm, mix_ref)]
    loads += [(stiff_hbm, stiff_ref), (metric_hbm, metric_ref), (place_hbm, place_ref)]
    loads = [pltpu.make_async_copy(source, target, in_sem.at[k]) for k, (source, target) in enumerate(loads)]
    for load in loads:
        load.start()

    def there(d):
        dx, dy = DIRS[d]
        ok = (gx + dx >= 0) & (gx + dx < n_gx) & (gy + dy >= 0) & (gy + dy < n_gy)
        return ok, {"gx": gx + dx, "gy": gy + dy}

    def if_there(d, act):
        pl.when(there(d)[0])(act)

    size_x, size_y, size_z = n_gx // 2, n_gy // 4, 4
    chips = [(i, j, k) for i in range(size_x) for j in range(size_y) for k in range(size_z)][1:]
    chips.sort(key=lambda c: sum((v - 1) % n for v, n in zip(c, (size_x, size_y, size_z))))

    def chip(offset):
        y, z = gy // size_z, lax.rem(gy, size_z)
        return {
            "gx": lax.rem(gx + 2 * offset[0], n_gx),
            "gy": lax.rem(y + offset[1], size_y) * size_z + lax.rem(z + offset[2], size_z),
        }

    halo_x[...] = jnp.zeros_like(halo_x)
    halo_y[...] = jnp.zeros_like(halo_y)

    barrier = pltpu.get_barrier_semaphore()
    expected = jnp.int32(0)
    for d in DIRS:
        ok, where = there(d)

        @pl.when(ok)
        def _():
            pl.semaphore_signal(barrier, inc=1, device_id=where, device_id_type=MESH)

        expected = expected + ok.astype(jnp.int32)

    def x_copy(t, side, arriving):
        slot = side if arriving else 1 - side
        rows = pl.ds(0, FACES + 8 * (1 - t))
        return pltpu.make_async_remote_copy(
            src_ref=own_x.at[t, side, rows],
            dst_ref=halo_x.at[t, slot, rows],
            send_sem=sx_send.at[t, side],
            recv_sem=sx_recv.at[t, slot],
            device_id=there((1, 7)[side])[1],
            device_id_type=MESH,
        )

    def y_copy(t, index, arriving):
        d = EDGE_DIRS[index]
        slot = index if arriving else EDGE_DIRS.index(8 - d)
        rows = pl.ds(0, 8 + 8 * (1 - t))
        return pltpu.make_async_remote_copy(
            src_ref=own_y.at[t, index, rows],
            dst_ref=halo_y.at[t, slot, rows],
            send_sem=sy_send.at[t, index],
            recv_sem=sy_recv.at[t, slot],
            device_id=there(d)[1],
            device_id_type=MESH,
        )

    strides = [k for k in (1, 2, 4, 8, 16) if k < max(n_gx, n_gy)]

    def partners(k):
        by = strides[k]
        for dx in (-by, 0, by) if by < n_gx else (0,):
            for dy in (-by, 0, by) if by < n_gy else (0,):
                if dx or dy:
                    ok = (gx + dx >= 0) & (gx + dx < n_gx) & (gy + dy >= 0) & (gy + dy < n_gy)
                    yield ok, {"gx": gx + dx, "gy": gy + dy}

    def pass_on(k):
        for ok, where in partners(k):

            @pl.when(ok)
            def _():
                pl.semaphore_signal(ready_sem.at[k], inc=1, device_id=where, device_id_type=MESH)

    pending = list(range(len(strides)))

    def learn():
        if pending:
            k = pending.pop(0)
            pl.semaphore_wait(ready_sem.at[k], sum(ok.astype(jnp.int32) for ok, _ in partners(k)))
            if pending:
                pass_on(k + 1)

    def send(t):
        for index in (2, 3, 4, 5, 0, 1):
            if_there(EDGE_DIRS[index], lambda: y_copy(t, index, False).start())
        for side in range(2):
            if_there((1, 7)[side], lambda: x_copy(t, side, False).start())

    lane = iota((1, 128), 1)
    lane_face = lane >> 4
    lane_pair = lane & 15

    def stacked_table(value):
        high = value.astype(BF16)
        rest = value - high.astype(F32)
        return high, jnp.concatenate([high.astype(F32), rest], axis=0).astype(BF16)

    def by_table(table, value_h, value_l):
        high, both = table
        rows = high.shape[0]
        first = dot(both, value_h)
        return first[:rows] + first[rows:] + dot(high, value_l)

    def code(entry, active):
        return jnp.where(active > 0.0, entry, -1.0)

    for load in loads[:9]:
        load.wait()
    fine, face, owner, sub, coarse, cface, level = (ints_ref[k] for k in range(7))
    shift = n_gy.bit_length() - 1
    slot = ((owner >> shift) - gx + 1) * 3 + (owner & (n_gy - 1)) - gy + 1
    count = fine.shape[1]
    hits = jnp.where(iota((16, count), 0) == slot, 1.0, 0.0)
    parts = [hits[:, k : k + EB] for k in range(0, count, EB)]
    earlier = jnp.where(iota((EB, EB), 0) < iota((EB, EB), 1), 1.0, 0.0).astype(BF16)
    within = dot(jnp.concatenate(parts, axis=0).astype(BF16), earlier)
    offset, ranks = jnp.zeros((16, 1), F32), []
    for k, part in enumerate(parts):
        ranks.append(jnp.sum(part * (within[16 * k : 16 * k + 16] + offset), axis=0, keepdims=True))
        offset = offset + jnp.sum(part, axis=1, keepdims=True)
    position = jnp.concatenate(ranks, axis=1)
    row = iota((8, count), 0)
    facts = jnp.ones((8, count), jnp.int32)
    for index, entry in enumerate((fine >> 7, fine & 127, face, coarse >> 7, coarse & 127, cface, sub)):
        facts = jnp.where(row == index, entry, facts)
    facts = facts.astype(F32)
    stacked = jnp.concatenate([facts * hits[k : k + 1] for k in range(9)], axis=0).astype(BF16)
    packed = dot_nt(stacked, one_hot(EB, position))
    for k in range(9):
        own_m[k] = packed[8 * k : 8 * k + 8]
    for side in range(2):
        d = (1, 7)[side]
        own_x[0, side, FACES : FACES + 8, :] = packed[8 * d : 8 * d + 8]
    for index, d in enumerate(EDGE_DIRS):
        own_y[0, index, 8:16, :] = packed[8 * d : 8 * d + 8]
    scale = jnp.where(level == 0, 1.0, jnp.where(level == 1, 0.5, 0.25))

    def face_product(table, value):
        high, low = split(value)
        return dot(table, high) + dot(table, low)

    def edge_ends(faces):
        ends = faces[:, 0:EB]
        for a in range(1, EA):
            moved = pltpu.roll(faces[:, a * EB : (a + 1) * EB], 2 * a, 1)
            ends = jnp.where((lane == 2 * a) | (lane == 2 * a - 1), moved, ends)
        return ends

    def edge_values(ends):
        own = jnp.zeros((FR, 128), F32)
        for f in range(6):
            moved = pltpu.roll(ends[f * FR : (f + 1) * FR], 16 * f + 1, 1)
            own = jnp.where((lane_face == f) & (lane_pair < 8), moved, own)
        rows = own
        for pair, by in CORNER_SHIFT.items():
            own = jnp.where(lane_pair == pair, pltpu.roll(rows, by, 1), own)
        return own

    def lanes_of(start):
        return (lane >= start) & (lane < start + 8) & ((lane & 1) == start % 2)

    def pack(part, turn):
        result = jnp.zeros((8, 128), F32)
        for (f, g), start in PACK.items():
            result = jnp.where(lanes_of(start), pltpu.roll(part(f, g), (start + turn(f)) % 128, 1), result)
        return result

    def pack_pairs(values, first):
        return pack(lambda f, g: values[8 * g : 8 * g + 8], lambda f: -16 * f - first)

    def corner_lanes(c):
        return ((lane & 7) >> 1) == c

    def edge_across(t):
        corners = jnp.zeros((8, 128), F32)
        for c, a in enumerate(CORNER_ROWS):
            moved = pltpu.roll(halo_y[t, 2 + c, 0:8, :], 2 * (c - a) % 128, 1)
            corners = jnp.where(corner_lanes(c), moved, corners)
        groups = []
        for g in range(FR // 8):
            group = jnp.zeros((8, 128), F32)
            for packed_rows, first in ((halo_y[t, 0, 0:8, :], 1), (halo_y[t, 1, 0:8, :], 0), (corners, 8)):
                for f in range(6):
                    moved = pltpu.roll(packed_rows, (16 * f + first - PACK[f, g]) % 128, 1)
                    group = jnp.where(lanes_of(16 * f + first), moved, group)
            groups.append(group)
        return jnp.concatenate(groups, axis=0)

    def edge_spread(values):
        rows = jnp.where(lane_pair < 8, values, 0.0)
        for pair, by in CORNER_SHIFT.items():
            rows = rows + jnp.where(lane_pair == pair - by, pltpu.roll(values, 128 - by, 1), 0.0)
        ends = jnp.concatenate([pltpu.roll(rows, 127 - 16 * f, 1) for f in range(6)], axis=0)
        tiles = []
        for a in range(EA):
            moved = pltpu.roll(ends, 128 - 2 * a, 1) if a else ends
            tiles.append(jnp.where((lane == 0) | (lane == EB - 1), moved, 0.0))
        return tiles

    def publish(t, faces):
        own_x[t, 0, 0:FACES, :] = faces[:, 0:EB]
        own_x[t, 1, 0:FACES, :] = faces[:, (EA - 1) * EB :]
        ends = edge_ends(faces)

        def rows(f, g):
            return ends[f * FR + 8 * g : f * FR + 8 * g + 8]

        toward = (pack(rows, lambda f: 0), pack(rows, lambda f: 1))
        for index, d in enumerate(EDGE_DIRS):
            own_y[t, index, 0:8, :] = toward[0 if DIRS[d][1] < 0 else 1]
        return ends

    b = b_ref[...]
    faces = face_product(pick_ref[...], b)
    ends = publish(0, faces)

    pl.semaphore_wait(barrier, expected)
    send(0)
    pass_on(0)
    own = edge_values(ends)

    for load in loads[9:]:
        load.wait()
    for d in range(3):
        padded = jnp.concatenate([stiff_ref[d], jnp.zeros((SP - NODES, NODES), F32)], axis=0)
        high, low = split(padded)
        stiff_s[d * SP : (d + 1) * SP, :] = high
        stiff_s[(3 + d) * SP : (4 + d) * SP, :] = low
    proj_s[...] = jnp.zeros_like(proj_s)
    proj_c[...] = jnp.zeros_like(proj_c)
    for s in range(4):
        table = proj_ref[:, s, :]
        proj_s[s * FR : s * FR + SIDE, 0:SIDE] = table
        proj_c[0:SIDE, s * FR : s * FR + SIDE] = table
    proj_t[...] = proj_s[...].T[0:FR]
    table_s = stacked_table(proj_s[0 : 4 * FR, 0:FR])
    table_c = stacked_table(proj_c[:, 0 : 4 * FR])
    table_t = stacked_table(proj_t[:, 0 : 4 * FR])

    me = own_m[4]
    self_fine = code(me[0:1] * float(EB) + me[1:2], me[7:8])
    self_coarse = code(me[3:4] * float(EB) + me[4:5], me[7:8])
    oh_self[...] = one_hot(ELEMS, jnp.concatenate([self_fine, self_coarse], axis=1))

    wide = iota((32, 512), 1)
    repeat = jnp.where(iota((32, 512), 0) == (wide >> 7) * 8 + ((wide >> 4) & 7), 1.0, 0.0).astype(BF16)
    same_pair = (iota((128, 512), 0) & 15) == (iota((128, 512), 1) & 15)
    ones = jnp.ones((16, 6 * EB), BF16)

    def edge_counts(held):
        parts_f, parts_c = [], []
        for d, facts_d in zip(EDGE_DIRS, held):
            if d in (3, 5):
                pair = facts_d[0:1] * 2.0 + (1.0 if d == 3 else 0.0)
            else:
                pair = float(CORNERS[d])
            parts_f.append(code(facts_d[2:3] * 16.0 + pair, facts_d[7:8]))
            parts_c.append(code(facts_d[6:7] * 8.0 + facts_d[5:6], facts_d[7:8]))
        fine_hot = one_hot(128, jnp.concatenate(parts_f, axis=1))
        coarse_hot = one_hot(32, jnp.concatenate(parts_c, axis=1))
        joined = dot(dot_nt(fine_hot, coarse_hot).astype(BF16), repeat)
        return jnp.where(same_pair, joined, 0.0).astype(BF16), dot_nt(ones, fine_hot)[0:1]

    n_out[...], sum_out = edge_counts([own_m[d] for d in EDGE_DIRS])

    def mortar_jump(coarses, fines, subs):
        high = coarses.astype(BF16).astype(F32)
        return by_table(table_c, by_subface(high, subs), by_subface(coarses - high, subs)) - fines

    def mortar_back(jump, subs):
        high = jump.astype(BF16).astype(F32)
        return by_table(table_t, by_subface(high, subs), by_subface(jump - high, subs))

    def local_part(field, faces):
        f_h, f_l = split(faces)
        got = dot(f_h, oh_self[...]) + dot(f_l, oh_self[...])
        jump = mortar_jump(pick_face(got[:, EB:], me[5:6]), pick_face(got[:, 0:EB], me[2:3]), me[6:7])
        back = mortar_back(jump, me[6:7])
        terms = jnp.concatenate([-PENALTY * jump, PENALTY * back], axis=1)
        s_h, s_l = spread_split(terms, jnp.concatenate([me[2:3], me[5:6]], axis=1))
        gathered = dot_nt(s_h, oh_self[...]) + dot_nt(s_l, oh_self[...])

        blocks = []
        for a in range(EA):
            here = slice(a * EB, (a + 1) * EB)
            x_low, x_high = faces[0:FR, here], faces[FR : 2 * FR, here]
            y_low, y_high = faces[2 * FR : 3 * FR, here], faces[3 * FR : 4 * FR, here]
            left = x_low if a == 0 else x_low - faces[FR : 2 * FR, (a - 1) * EB : a * EB]
            right = x_high if a == EA - 1 else x_high - faces[0:FR, (a + 1) * EB : (a + 2) * EB]
            below = jnp.where(lane == 0, 0.0, pltpu.roll(y_high, 1, 1))
            above = jnp.where(lane == EB - 1, 0.0, pltpu.roll(y_low, EB - 1, 1))
            lateral = jnp.concatenate([left, right, y_low - below, y_high - above], axis=0)
            blocks.append(jnp.concatenate([PENALTY * lateral, jnp.zeros((2 * FR, EB), F32)], axis=0))
        gathered = gathered + jnp.concatenate(blocks, axis=1)

        field_h, field_l = split(field)
        both = dot(stiff_s[...], field_h)
        rest = dot(stiff_s[0 : 3 * SP, :], field_l)
        total = field
        for d in range(3):
            here = slice(d * SP, d * SP + NODES)
            again = slice((3 + d) * SP, (3 + d) * SP + NODES)
            total = total + metric_ref[d : d + 1, :] * (both[here] + both[again] + rest[here])
        return scale * total, gathered

    def side_jumps(faces):
        for side in range(2):
            d = (1, 7)[side]
            both = jnp.concatenate([own_m[d], halo_x[0, side, FACES : FACES + 8, :]], axis=1)
            oh_x[side] = one_hot(EB, code(both[1:2], both[7:8]))
        fines, coarses, subs = [], [], []
        for side in range(2):
            d = (1, 7)[side]
            theirs_m = halo_x[0, side, FACES : FACES + 8, :]
            here = slice(0, EB) if side == 0 else slice((EA - 1) * EB, EA * EB)
            pair = jnp.concatenate([faces[:, here], halo_x[0, side, 0:FACES, :]], axis=0)
            high, low = split(pair)
            got = dot(high, oh_x[side]) + dot(low, oh_x[side])
            ours, theirs = got[0:FACES], got[FACES:]
            fines += [pick_face(ours[:, 0:EB], own_m[d][2:3]), pick_face(theirs[:, EB:], theirs_m[2:3])]
            coarses += [pick_face(theirs[:, 0:EB], own_m[d][5:6]), pick_face(ours[:, EB:], theirs_m[5:6])]
            subs += [own_m[d][6:7], theirs_m[6:7]]
        jump = mortar_jump(*(jnp.concatenate(parts, axis=1) for parts in (coarses, fines, subs)))
        jump = [jump[:, k * EB : (k + 1) * EB] for k in range(4)]
        return jump, subs

    def side_adjoint(faces):
        fines, coarses, subs = [], [], []
        for side in range(2):
            d = (1, 7)[side]
            theirs_m = halo_x[0, side, FACES : FACES + 8, :]
            high, low = split(faces[:, 0:EB] if side == 0 else faces[:, (EA - 1) * EB :])
            got = dot(high, oh_x[side]) + dot(low, oh_x[side])
            fines.append(pick_face(got[:, 0:EB], own_m[d][2:3]))
            coarses.append(pick_face(got[:, EB:], theirs_m[5:6]))
            subs += [own_m[d][6:7], theirs_m[6:7]]
        fines = jnp.concatenate(fines, axis=1)
        images = mortar_jump(jnp.concatenate(coarses, axis=1), 0.0, jnp.concatenate([subs[1], subs[3]], axis=1))
        backs = mortar_back(fines, jnp.concatenate([subs[0], subs[2]], axis=1))
        against = []
        for side in range(2):
            d = (1, 7)[side]
            here = slice(side * EB, (side + 1) * EB)
            theirs_m = halo_x[0, side, FACES : FACES + 8, :]
            s_h, s_l = spread_split(
                jnp.concatenate([backs[:, here], images[:, here]], axis=1),
                jnp.concatenate([own_m[d][5:6], theirs_m[2:3]], axis=1),
            )
            against.append(dot_nt(s_h, oh_x[side]) + dot_nt(s_l, oh_x[side]))
        low_face, high_face = faces[0:FR, 0:EB], faces[FR : 2 * FR, (EA - 1) * EB :]
        against[0] = against[0] + jnp.concatenate([jnp.zeros((FR, EB), F32), low_face, jnp.zeros((4 * FR, EB), F32)], axis=0)
        against[1] = against[1] + jnp.concatenate([high_face, jnp.zeros((5 * FR, EB), F32)], axis=0)
        known = jnp.sum(fines * fines + images * images, axis=0, keepdims=True)
        return fines, images, subs, against, known[:, 0:EB] + known[:, EB:]

    def side_jumps_after(fines, images, subs):
        far_fines, far_coarses = [], []
        for side in range(2):
            d = (1, 7)[side]
            theirs_m = halo_x[0, side, FACES : FACES + 8, :]
            high, low = split(halo_x[1, side, 0:FACES, :])
            got = dot(high, oh_x[side]) + dot(low, oh_x[side])
            far_coarses.append(pick_face(got[:, 0:EB], own_m[d][5:6]))
            far_fines.append(pick_face(got[:, EB:], theirs_m[2:3]))
        out = mortar_jump(
            jnp.concatenate(far_coarses, axis=1), fines, jnp.concatenate([subs[0], subs[2]], axis=1)
        )
        into = images - jnp.concatenate(far_fines, axis=1)
        return [out[:, 0:EB], into[:, 0:EB], out[:, EB:], into[:, EB:]]

    def side_terms(t, jump, subs):
        back = mortar_back(jnp.concatenate([jump[1], jump[3]], axis=1), jnp.concatenate([subs[1], subs[3]], axis=1))
        result = []
        for side in range(2):
            d = (1, 7)[side]
            terms = jnp.concatenate(
                [-PENALTY * jump[2 * side], PENALTY * back[:, side * EB : (side + 1) * EB]], axis=1
            )
            theirs_m = halo_x[0, side, FACES : FACES + 8, :]
            s_h, s_l = spread_split(terms, jnp.concatenate([own_m[d][2:3], theirs_m[5:6]], axis=1))
            side_term = dot_nt(s_h, oh_x[side]) + dot_nt(s_l, oh_x[side])
            if side == 0:
                beside = [-PENALTY * halo_x[t, 0, FR : 2 * FR, :], jnp.zeros((5 * FR, EB), F32)]
            else:
                beside = [jnp.zeros((FR, EB), F32), -PENALTY * halo_x[t, 1, 0:FR, :], jnp.zeros((4 * FR, EB), F32)]
            result.append(side_term + jnp.concatenate(beside, axis=0))
        return result

    low_face = (lane_face == 2) & (lane_pair < 8) & ((lane_pair & 1) == 1)
    high_face = (lane_face == 3) & (lane_pair < 8) & ((lane_pair & 1) == 0)

    def edges_arrive(t):
        for index in range(6):
            if_there(EDGE_DIRS[index], lambda: y_copy(t, index, True).wait_recv())

    def sides_arrive(t):
        for side in range(2):
            if_there((1, 7)[side], lambda: x_copy(t, side, True).wait_recv())

    def edge_jumps(t, own, sum_in):
        across = edge_across(t)
        pairs = jnp.concatenate([own, across], axis=1)
        pairs_h, pairs_l = split(pairs)
        images = by_table(table_s, pairs_h, pairs_l)
        image_own = jnp.concatenate([images[s * FR : (s + 1) * FR, 0:128] for s in range(4)], axis=1)
        image_far = jnp.concatenate([images[s * FR : (s + 1) * FR, 128:] for s in range(4)], axis=1)
        far_h, far_l = split(image_far)
        on_fine = own * sum_out - dot_nt(far_h, n_out[...]) - dot_nt(far_l, n_out[...])
        jumps = image_own * sum_in - dot(pairs_h[:, 128:], n_in[...]) - dot(pairs_l[:, 128:], n_in[...])
        from_low = pltpu.roll(across, 128 - 16, 1)
        from_high = pltpu.roll(across, 16, 1)
        beside = jnp.where(low_face, from_low, jnp.where(high_face, from_high, 0.0))
        return PENALTY * (on_fine - beside), jumps

    def edge_adjoint(own, sum_in):
        own_h, own_l = split(own)
        images = by_table(table_s, own_h, own_l)
        images = jnp.concatenate([images[s * FR : (s + 1) * FR] for s in range(4)], axis=1)
        images_h, images_l = split(images)
        joined = dot(own_h, n_out[...]) + dot(own_l, n_out[...])
        joined_h, joined_l = split(jnp.concatenate([joined[:, s * 128 : (s + 1) * 128] for s in range(4)], axis=0))
        meets = by_table(table_t, joined_h, joined_l) + dot_nt(images_h, n_in[...]) + dot_nt(images_l, n_in[...])
        meets = meets + pltpu.roll(jnp.where(low_face, own, 0.0), 16, 1)
        meets = meets + pltpu.roll(jnp.where(high_face, own, 0.0), 128 - 16, 1)
        against = [pack_pairs(meets, 1), pack_pairs(meets, 0)]
        corners = pack_pairs(meets, 8)
        for c, a in enumerate(CORNER_ROWS):
            against.append(pltpu.roll(jnp.where(corner_lanes(c), corners, 0.0), 2 * (a - c) % 128, 1))
        known = jnp.sum(own * own * sum_out, axis=0, keepdims=True)
        both = jnp.sum(images * images * sum_in, axis=0, keepdims=True)
        return against, known + sum(both[:, s * 128 : (s + 1) * 128] for s in range(4))

    def edge_terms(direct, jumps):
        jumps = jnp.concatenate([jumps[:, s * 128 : (s + 1) * 128] for s in range(4)], axis=0)
        jumps_h, jumps_l = split(jumps)
        return edge_spread(direct + PENALTY * by_table(table_t, jumps_h, jumps_l))

    def placed(value):
        return face_product(place_ref[...], value)

    b = b_ref[...]
    total, gathered = local_part(b, faces)
    learn()
    total = total + placed(gathered)
    started = face_product(pick_ref[...], total)
    sides_arrive(0)
    edges_arrive(0)
    jump, subs = side_jumps(faces)
    sides = side_terms(0, jump, subs)
    n_in[...], _ = edge_counts([halo_y[0, index, 8:16, :] for index in range(6)])
    sum_in = dot(jnp.ones((16, 128), BF16), n_in[...])[0:1]
    direct, jumps = edge_jumps(0, own, sum_in)
    tiles = edge_terms(direct, jumps)
    tiles[0] = tiles[0] + sides[0]
    tiles[EA - 1] = tiles[EA - 1] + sides[1]
    remote = jnp.concatenate(tiles, axis=1)
    faces = started + face_product(mix_ref[...], remote)
    ends = publish(1, faces)
    send(1)
    learn()
    own = edge_values(ends)
    q = total + placed(remote)
    q_ref[...] = q

    total, gathered = local_part(q, faces)
    b = b_ref[...]
    q = q_ref[...]
    learn()
    early = [column_sums(b, b), column_sums(b, q), column_sums(q, q)]
    energy = column_sums(q, total) + column_sums(faces, gathered)
    fines, images, subs, side_against, known = side_adjoint(faces)
    energy = energy + PENALTY * known
    edge_against, known = edge_adjoint(own, sum_in)
    energy = energy + PENALTY * known
    sides_arrive(1)
    met = jnp.zeros((1, 128), F32)
    for side in range(2):
        met = met + jnp.sum(halo_x[1, side, 0:FACES, :] * side_against[side], axis=0, keepdims=True)
    energy = energy - PENALTY * met
    edges_arrive(1)
    met = sum(halo_y[1, index, 0:8, :] * edge_against[index] for index in range(6))
    energy = energy - PENALTY * jnp.sum(met, axis=0, keepdims=True)

    lanes = jnp.zeros((1, 128), F32)
    for index, sums in enumerate(early + [energy]):
        lanes = jnp.where(lane == index, jnp.sum(sums, axis=1, keepdims=True), lanes)
    mine0[...] = lanes
    while pending:
        learn()
    others = [(c, o) for o in [(0, 0, 0)] + chips for c in range(2) if c or o != (0, 0, 0)]
    others.sort(key=lambda t: sum((v - 1) % n for v, n in zip(t[1], (size_x, size_y, size_z))))
    for k, (flip, offset) in enumerate(others):
        where = chip(offset)
        if flip:
            core = lax.rem(gx, 2)
            where["gx"] = where["gx"] + 1 - 2 * core
        pltpu.make_async_remote_copy(
            src_ref=mine0,
            dst_ref=red1.at[k],
            send_sem=s1_send,
            recv_sem=s1_recv,
            device_id=where,
            device_id_type=MESH,
        ).start()

    sides = side_terms(1, side_jumps_after(fines, images, subs), subs)
    tiles = edge_terms(*edge_jumps(1, own, sum_in))
    tiles[0] = tiles[0] + sides[0]
    tiles[EA - 1] = tiles[EA - 1] + sides[1]
    w_ref[...] = total + placed(gathered + jnp.concatenate(tiles, axis=1))
    for t in range(2):
        for side in range(2):
            if_there((1, 7)[side], lambda: x_copy(t, side, False).wait_send())
        for index in range(6):
            if_there(EDGE_DIRS[index], lambda: y_copy(t, index, False).wait_send())

    pltpu.make_async_copy(red1, red1, s1_recv).wait()
    lanes = lanes + jnp.sum(red1[...], axis=0)
    bb, bq, qq, qw = (lanes[:, i : i + 1] for i in range(4))
    alpha = bb / bq
    new = bb - 2.0 * alpha * bq + alpha * alpha * qq
    grow = 1.0 + new / bb
    alpha_next = new / (grow * grow * bq - 2.0 * grow * alpha * qq + alpha * alpha * qw)
    row = iota((8, 128), 0)
    coef_ref[...] = jnp.where(row == 0, alpha + alpha_next * grow, alpha * alpha_next)
    pltpu.make_async_copy(red1, red1, s1_send).wait()


def finish(coef_ref, b_ref, q_ref, w_ref, x_hbm, r_hbm, made, out_sem):
    first, second = coef_ref[0:1, 0:1], coef_ref[1:2, 0:1]
    stores = []
    for part, (start, size) in enumerate(((0, 104), (104, NODES - 104))):
        rows = pl.ds(start, size)
        b, q, w = b_ref[rows, :], q_ref[rows, :], w_ref[rows, :]
        made[0, rows, :] = first * b - second * q
        made[1, rows, :] = b - first * q + second * w
        for k, target in enumerate((x_hbm, r_hbm)):
            store = pltpu.make_async_copy(made.at[k, rows], target.at[rows], out_sem.at[part, k])
            store.start()
            stores.append(store)
    for store in stores:
        store.wait()


def body(
    n_gx,
    n_gy,
    right_side,
    stiffness,
    metric,
    levels,
    projection,
    mortar_fine,
    mortar_face,
    mortar_owner,
    mortar_subface,
    mortar_coarse,
    mortar_cface,
):
    pick, place, mix = (jnp.asarray(table, BF16) for table in constant_tables())
    field = jax.ShapeDtypeStruct(right_side.shape, F32)
    count = mortar_fine.shape[0]
    others = n_gx * n_gy - 1
    hbm = pl.BlockSpec(memory_space=pltpu.HBM)
    vmem = pl.BlockSpec(memory_space=pltpu.VMEM)
    dma = pltpu.SemaphoreType.DMA
    line = [
        entry.reshape(1, count)
        for entry in (
            mortar_fine,
            mortar_face,
            mortar_owner,
            mortar_subface,
            mortar_coarse,
            mortar_cface,
            levels,
        )
    ]
    q, w, coef = pl.pallas_call(
        functools.partial(kernel, n_gx, n_gy),
        out_shape=(field, field, jax.ShapeDtypeStruct((8, 128), F32)),
        in_specs=[hbm] * 14,
        out_specs=(vmem, vmem, vmem),
        scratch_shapes=[
            pltpu.VMEM((NODES, ELEMS), F32),
            pltpu.VMEM((3, NODES, NODES), F32),
            pltpu.VMEM((3, ELEMS), F32),
            pltpu.VMEM((7, 1, ELEMS), jnp.int32),
            pltpu.VMEM((SIDE, 4, SIDE), F32),
            pltpu.VMEM((FACES, NODES), BF16),
            pltpu.VMEM((NODES, FACES), BF16),
            pltpu.VMEM((FACES, FACES), BF16),
            pltpu.VMEM((2, 2, FACES + 8, EB), F32),
            pltpu.VMEM((2, 6, 16, 128), F32),
            pltpu.VMEM((9, 8, 128), F32),
            pltpu.VMEM((2, 2, FACES + 8, EB), F32),
            pltpu.VMEM((2, 6, 16, 128), F32),
            pltpu.VMEM((6 * SP, NODES), BF16),
            pltpu.VMEM((ELEMS, 2 * EB), BF16),
            pltpu.VMEM((2, EB, 2 * EB), BF16),
            pltpu.VMEM((128, 512), BF16),
            pltpu.VMEM((128, 512), BF16),
            pltpu.VMEM((256, 128), F32),
            pltpu.VMEM((FR, 256), F32),
            pltpu.VMEM((FR, 256), F32),
            pltpu.VMEM((others, 1, 128), F32),
            pltpu.VMEM((1, 128), F32),
            dma((14,)),
            dma((2, 2)),
            dma((2, 2)),
            dma((2, 6)),
            dma((2, 6)),
            pltpu.SemaphoreType.REGULAR((8,)),
            dma,
            dma,
        ],
        compiler_params=pltpu.CompilerParams(
            collective_id=0, has_side_effects=True, vmem_limit_bytes=40 * 1024 * 1024
        ),
    )(
        *(
            pltpu.with_memory_space_constraint(operand, pltpu.HBM)
            for operand in (right_side, stiffness, metric, *line, projection.transpose(1, 0, 2), pick, place, mix)
        )
    )
    return pl.pallas_call(
        finish,
        out_shape=(field, field),
        in_specs=[vmem] * 4,
        out_specs=(hbm, hbm),
        scratch_shapes=[pltpu.VMEM((2, NODES, ELEMS), F32), dma((2, 2))],
        compiler_params=pltpu.CompilerParams(vmem_limit_bytes=40 * 1024 * 1024),
    )(coef, right_side, q, w)


def solution(mesh):
    columns = P(None, ("gx", "gy"))
    faces = P(("gx", "gy"))
    in_specs = (columns, P(), columns, faces, P(), faces, faces, P(("gx", "gy"), None), faces, faces, faces)
    run = functools.partial(body, mesh.shape["gx"], mesh.shape["gy"])
    return jax.shard_map(run, mesh=mesh, in_specs=in_specs, out_specs=(columns, columns), check_vma=False)
```

```python
import functools

import jax
import jax.numpy as jnp
import numpy as np
from jax import lax
from jax.experimental import pallas as pl
from jax.experimental.pallas import tpu as pltpu
from jax.sharding import PartitionSpec as P

NP = 6
NODES = NP * NP * NP
SIDE = NP * NP
EA = 4
EB = 128
ELEMS = EA * EB
FR = 40
FACES = 6 * FR
SP = 224
PENALTY = 1.0

F32 = jnp.float32
BF16 = jnp.bfloat16
MESH = pl.DeviceIdType.MESH

DIRS = {d: (d // 3 - 1, d % 3 - 1) for d in range(9) if d != 4}
EDGE_DIRS = (3, 5, 0, 2, 6, 8)
CORNERS = {0: 8, 2: 10, 6: 12, 8: 14}
CORNER_SHIFT = {8: 7, 10: 10, 12: 5, 14: 8}
PACK = {(f, g): 8 * ((5 * f + g) // 2) + (5 * f + g) % 2 for f in range(6) for g in range(FR // 8)}
CORNER_ROWS = (EA - 1, EA - 1, 0, 0)


def face_nodes(face):
    ids = np.arange(NODES).reshape(NP, NP, NP)
    return [ids[0], ids[5], ids[:, 0], ids[:, 5], ids[:, :, 0], ids[:, :, 5]][face].reshape(-1)


def constant_tables():
    pick = np.zeros((FACES, NODES), np.float32)
    for face in range(6):
        pick[face * FR + np.arange(SIDE), face_nodes(face)] = 1.0
    return pick, pick.T.copy(), pick @ pick.T


def dot(a, b):
    return lax.dot_general(a, b, (((1,), (0,)), ((), ())), preferred_element_type=F32)


def dot_nt(a, b):
    return lax.dot_general(a, b, (((1,), (1,)), ((), ())), preferred_element_type=F32)


def split(value):
    high = value.astype(BF16)
    return high, (value - high.astype(F32)).astype(BF16)


def iota(shape, dim):
    return lax.broadcasted_iota(jnp.int32, shape, dim)


def one_hot(rows, code):
    return jnp.where(iota((rows, code.shape[1]), 0).astype(F32) == code, 1.0, 0.0).astype(BF16)


def pick_face(sides, face):
    out = None
    for f in range(6):
        part = jnp.where(face == float(f), sides[f * FR : (f + 1) * FR], 0.0)
        out = part if out is None else out + part
    return out


def spread_face(values, face):
    return jnp.concatenate([jnp.where(face == float(f), values, 0.0) for f in range(6)], axis=0)


def spread_split(values, face):
    high = values.astype(BF16).astype(F32)
    return spread_face(high, face).astype(BF16), spread_face(values - high, face).astype(BF16)


def by_subface(values, sub):
    return jnp.concatenate([jnp.where(sub == float(s), values, 0.0) for s in range(4)], axis=0).astype(BF16)


def column_sums(a, b):
    prod = a * b
    rows = jnp.sum(prod, axis=0, keepdims=True)
    return sum(rows[:, t * EB : (t + 1) * EB] for t in range(EA))


def kernel(
    n_gx,
    n_gy,
    b_hbm,
    stiff_hbm,
    metric_hbm,
    fine_hbm,
    face_hbm,
    owner_hbm,
    sub_hbm,
    coarse_hbm,
    cface_hbm,
    level_hbm,
    proj_hbm,
    pick_hbm,
    place_hbm,
    mix_hbm,
    q_ref,
    w_ref,
    coef_ref,
    b_ref,
    stiff_ref,
    metric_ref,
    ints_ref,
    proj_ref,
    pick_ref,
    place_ref,
    mix_ref,
    halo_x,
    halo_y,
    own_m,
    own_x,
    own_y,
    stiff_s,
    oh_self,
    oh_x,
    n_out,
    n_in,
    proj_s,
    proj_c,
    proj_t,
    red1,
    mine0,
    in_sem,
    sx_send,
    sx_recv,
    sy_send,
    sy_recv,
    ready_sem,
    s1_send,
    s1_recv,
):
    gx = lax.axis_index("gx")
    gy = lax.axis_index("gy")

    int_names = (fine_hbm, face_hbm, owner_hbm, sub_hbm, coarse_hbm, cface_hbm, level_hbm)
    loads = [(source, ints_ref.at[k]) for k, source in enumerate(int_names)]
    loads += [(b_hbm, b_ref), (pick_hbm, pick_ref), (proj_hbm, proj_ref), (mix_hbm, mix_ref)]
    loads += [(stiff_hbm, stiff_ref), (metric_hbm, metric_ref), (place_hbm, place_ref)]
    loads = [pltpu.make_async_copy(source, target, in_sem.at[k]) for k, (source, target) in enumerate(loads)]
    for load in loads:
        load.start()

    def there(d):
        dx, dy = DIRS[d]
        ok = (gx + dx >= 0) & (gx + dx < n_gx) & (gy + dy >= 0) & (gy + dy < n_gy)
        return ok, {"gx": gx + dx, "gy": gy + dy}

    def if_there(d, act):
        pl.when(there(d)[0])(act)

    size_x, size_y, size_z = n_gx // 2, n_gy // 4, 4
    chips = [(i, j, k) for i in range(size_x) for j in range(size_y) for k in range(size_z)][1:]
    chips.sort(key=lambda c: sum((v - 1) % n for v, n in zip(c, (size_x, size_y, size_z))))

    def chip(offset):
        y, z = gy // size_z, lax.rem(gy, size_z)
        return {
            "gx": lax.rem(gx + 2 * offset[0], n_gx),
            "gy": lax.rem(y + offset[1], size_y) * size_z + lax.rem(z + offset[2], size_z),
        }

    halo_x[...] = jnp.zeros_like(halo_x)
    halo_y[...] = jnp.zeros_like(halo_y)

    barrier = pltpu.get_barrier_semaphore()
    expected = jnp.int32(0)
    for d in DIRS:
        ok, where = there(d)

        @pl.when(ok)
        def _():
            pl.semaphore_signal(barrier, inc=1, device_id=where, device_id_type=MESH)

        expected = expected + ok.astype(jnp.int32)

    def x_copy(t, side, arriving):
        slot = side if arriving else 1 - side
        rows = pl.ds(0, FACES + 8 * (1 - t))
        return pltpu.make_async_remote_copy(
            src_ref=own_x.at[t, side, rows],
            dst_ref=halo_x.at[t, slot, rows],
            send_sem=sx_send.at[t, side],
            recv_sem=sx_recv.at[t, slot],
            device_id=there((1, 7)[side])[1],
            device_id_type=MESH,
        )

    def y_copy(t, index, arriving):
        d = EDGE_DIRS[index]
        slot = index if arriving else EDGE_DIRS.index(8 - d)
        rows = pl.ds(0, 8 + 8 * (1 - t))
        return pltpu.make_async_remote_copy(
            src_ref=own_y.at[t, index, rows],
            dst_ref=halo_y.at[t, slot, rows],
            send_sem=sy_send.at[t, index],
            recv_sem=sy_recv.at[t, slot],
            device_id=there(d)[1],
            device_id_type=MESH,
        )

    strides = [k for k in (1, 2, 4, 8, 16) if k < max(n_gx, n_gy)]

    def partners(k):
        by = strides[k]
        for dx in (-by, 0, by) if by < n_gx else (0,):
            for dy in (-by, 0, by) if by < n_gy else (0,):
                if dx or dy:
                    ok = (gx + dx >= 0) & (gx + dx < n_gx) & (gy + dy >= 0) & (gy + dy < n_gy)
                    yield ok, {"gx": gx + dx, "gy": gy + dy}

    def pass_on(k):
        for ok, where in partners(k):

            @pl.when(ok)
            def _():
                pl.semaphore_signal(ready_sem.at[k], inc=1, device_id=where, device_id_type=MESH)

    pending = list(range(len(strides)))

    def learn():
        if pending:
            k = pending.pop(0)
            pl.semaphore_wait(ready_sem.at[k], sum(ok.astype(jnp.int32) for ok, _ in partners(k)))
            if pending:
                pass_on(k + 1)

    def send(t):
        for index in (2, 3, 4, 5, 0, 1):
            if_there(EDGE_DIRS[index], lambda: y_copy(t, index, False).start())
        for side in range(2):
            if_there((1, 7)[side], lambda: x_copy(t, side, False).start())

    lane = iota((1, 128), 1)
    lane_face = lane >> 4
    lane_pair = lane & 15

    def stacked_table(value):
        high = value.astype(BF16)
        rest = value - high.astype(F32)
        return high, jnp.concatenate([high.astype(F32), rest], axis=0).astype(BF16)

    def by_table(table, value_h, value_l):
        high, both = table
        rows = high.shape[0]
        first = dot(both, value_h)
        return first[:rows] + first[rows:] + dot(high, value_l)

    def code(entry, active):
        return jnp.where(active > 0.0, entry, -1.0)

    for load in loads[:9]:
        load.wait()
    fine, face, owner, sub, coarse, cface, level = (ints_ref[k] for k in range(7))
    shift = n_gy.bit_length() - 1
    slot = ((owner >> shift) - gx + 1) * 3 + (owner & (n_gy - 1)) - gy + 1
    count = fine.shape[1]
    hits = jnp.where(iota((16, count), 0) == slot, 1.0, 0.0)
    parts = [hits[:, k : k + EB] for k in range(0, count, EB)]
    earlier = jnp.where(iota((EB, EB), 0) < iota((EB, EB), 1), 1.0, 0.0).astype(BF16)
    within = dot(jnp.concatenate(parts, axis=0).astype(BF16), earlier)
    offset, ranks = jnp.zeros((16, 1), F32), []
    for k, part in enumerate(parts):
        ranks.append(jnp.sum(part * (within[16 * k : 16 * k + 16] + offset), axis=0, keepdims=True))
        offset = offset + jnp.sum(part, axis=1, keepdims=True)
    position = jnp.concatenate(ranks, axis=1)
    row = iota((8, count), 0)
    facts = jnp.ones((8, count), jnp.int32)
    for index, entry in enumerate((fine >> 7, fine & 127, face, coarse >> 7, coarse & 127, cface, sub)):
        facts = jnp.where(row == index, entry, facts)
    facts = facts.astype(F32)
    stacked = jnp.concatenate([facts * hits[k : k + 1] for k in range(9)], axis=0).astype(BF16)
    packed = dot_nt(stacked, one_hot(EB, position))
    for k in range(9):
        own_m[k] = packed[8 * k : 8 * k + 8]
    for side in range(2):
        d = (1, 7)[side]
        own_x[0, side, FACES : FACES + 8, :] = packed[8 * d : 8 * d + 8]
    for index, d in enumerate(EDGE_DIRS):
        own_y[0, index, 8:16, :] = packed[8 * d : 8 * d + 8]
    scale = jnp.where(level == 0, 1.0, jnp.where(level == 1, 0.5, 0.25))

    def face_product(table, value):
        high, low = split(value)
        return dot(table, high) + dot(table, low)

    def edge_ends(faces):
        ends = faces[:, 0:EB]
        for a in range(1, EA):
            moved = pltpu.roll(faces[:, a * EB : (a + 1) * EB], 2 * a, 1)
            ends = jnp.where((lane == 2 * a) | (lane == 2 * a - 1), moved, ends)
        return ends

    def edge_values(ends):
        own = jnp.zeros((FR, 128), F32)
        for f in range(6):
            moved = pltpu.roll(ends[f * FR : (f + 1) * FR], 16 * f + 1, 1)
            own = jnp.where((lane_face == f) & (lane_pair < 8), moved, own)
        rows = own
        for pair, by in CORNER_SHIFT.items():
            own = jnp.where(lane_pair == pair, pltpu.roll(rows, by, 1), own)
        return own

    def lanes_of(start):
        return (lane >= start) & (lane < start + 8) & ((lane & 1) == start % 2)

    def pack(part, turn):
        result = jnp.zeros((8, 128), F32)
        for (f, g), start in PACK.items():
            result = jnp.where(lanes_of(start), pltpu.roll(part(f, g), (start + turn(f)) % 128, 1), result)
        return result

    def pack_pairs(values, first):
        return pack(lambda f, g: values[8 * g : 8 * g + 8], lambda f: -16 * f - first)

    def corner_lanes(c):
        return ((lane & 7) >> 1) == c

    def edge_across(t):
        corners = jnp.zeros((8, 128), F32)
        for c, a in enumerate(CORNER_ROWS):
            moved = pltpu.roll(halo_y[t, 2 + c, 0:8, :], 2 * (c - a) % 128, 1)
            corners = jnp.where(corner_lanes(c), moved, corners)
        groups = []
        for g in range(FR // 8):
            group = jnp.zeros((8, 128), F32)
            for packed_rows, first in ((halo_y[t, 0, 0:8, :], 1), (halo_y[t, 1, 0:8, :], 0), (corners, 8)):
                for f in range(6):
                    moved = pltpu.roll(packed_rows, (16 * f + first - PACK[f, g]) % 128, 1)
                    group = jnp.where(lanes_of(16 * f + first), moved, group)
            groups.append(group)
        return jnp.concatenate(groups, axis=0)

    def edge_spread(values):
        rows = jnp.where(lane_pair < 8, values, 0.0)
        for pair, by in CORNER_SHIFT.items():
            rows = rows + jnp.where(lane_pair == pair - by, pltpu.roll(values, 128 - by, 1), 0.0)
        ends = jnp.concatenate([pltpu.roll(rows, 127 - 16 * f, 1) for f in range(6)], axis=0)
        tiles = []
        for a in range(EA):
            moved = pltpu.roll(ends, 128 - 2 * a, 1) if a else ends
            tiles.append(jnp.where((lane == 0) | (lane == EB - 1), moved, 0.0))
        return tiles

    def publish(t, faces):
        own_x[t, 0, 0:FACES, :] = faces[:, 0:EB]
        own_x[t, 1, 0:FACES, :] = faces[:, (EA - 1) * EB :]
        ends = edge_ends(faces)

        def rows(f, g):
            return ends[f * FR + 8 * g : f * FR + 8 * g + 8]

        toward = (pack(rows, lambda f: 0), pack(rows, lambda f: 1))
        for index, d in enumerate(EDGE_DIRS):
            own_y[t, index, 0:8, :] = toward[0 if DIRS[d][1] < 0 else 1]
        return ends

    b = b_ref[...]
    faces = face_product(pick_ref[...], b)
    ends = publish(0, faces)

    pl.semaphore_wait(barrier, expected)
    send(0)
    pass_on(0)
    own = edge_values(ends)

    for load in loads[9:]:
        load.wait()
    for d in range(3):
        padded = jnp.concatenate([stiff_ref[d], jnp.zeros((SP - NODES, NODES), F32)], axis=0)
        high, low = split(padded)
        stiff_s[d * SP : (d + 1) * SP, :] = high
        stiff_s[(3 + d) * SP : (4 + d) * SP, :] = low
    proj_s[...] = jnp.zeros_like(proj_s)
    proj_c[...] = jnp.zeros_like(proj_c)
    for s in range(4):
        table = proj_ref[:, s, :]
        proj_s[s * FR : s * FR + SIDE, 0:SIDE] = table
        proj_c[0:SIDE, s * FR : s * FR + SIDE] = table
    proj_t[...] = proj_s[...].T[0:FR]
    table_s = stacked_table(proj_s[0 : 4 * FR, 0:FR])
    table_c = stacked_table(proj_c[:, 0 : 4 * FR])
    table_t = stacked_table(proj_t[:, 0 : 4 * FR])

    me = own_m[4]
    self_fine = code(me[0:1] * float(EB) + me[1:2], me[7:8])
    self_coarse = code(me[3:4] * float(EB) + me[4:5], me[7:8])
    oh_self[...] = one_hot(ELEMS, jnp.concatenate([self_fine, self_coarse], axis=1))

    wide = iota((32, 512), 1)
    repeat = jnp.where(iota((32, 512), 0) == (wide >> 7) * 8 + ((wide >> 4) & 7), 1.0, 0.0).astype(BF16)
    same_pair = (iota((128, 512), 0) & 15) == (iota((128, 512), 1) & 15)
    ones = jnp.ones((16, 6 * EB), BF16)

    def edge_counts(held):
        parts_f, parts_c = [], []
        for d, facts_d in zip(EDGE_DIRS, held):
            if d in (3, 5):
                pair = facts_d[0:1] * 2.0 + (1.0 if d == 3 else 0.0)
            else:
                pair = float(CORNERS[d])
            parts_f.append(code(facts_d[2:3] * 16.0 + pair, facts_d[7:8]))
            parts_c.append(code(facts_d[6:7] * 8.0 + facts_d[5:6], facts_d[7:8]))
        fine_hot = one_hot(128, jnp.concatenate(parts_f, axis=1))
        coarse_hot = one_hot(32, jnp.concatenate(parts_c, axis=1))
        joined = dot(dot_nt(fine_hot, coarse_hot).astype(BF16), repeat)
        return jnp.where(same_pair, joined, 0.0).astype(BF16), dot_nt(ones, fine_hot)[0:1]

    n_out[...], sum_out = edge_counts([own_m[d] for d in EDGE_DIRS])

    def mortar_jump(coarses, fines, subs):
        high = coarses.astype(BF16).astype(F32)
        return by_table(table_c, by_subface(high, subs), by_subface(coarses - high, subs)) - fines

    def mortar_back(jump, subs):
        high = jump.astype(BF16).astype(F32)
        return by_table(table_t, by_subface(high, subs), by_subface(jump - high, subs))

    def local_part(field, faces):
        f_h, f_l = split(faces)
        got = dot(f_h, oh_self[...]) + dot(f_l, oh_self[...])
        jump = mortar_jump(pick_face(got[:, EB:], me[5:6]), pick_face(got[:, 0:EB], me[2:3]), me[6:7])
        back = mortar_back(jump, me[6:7])
        terms = jnp.concatenate([-PENALTY * jump, PENALTY * back], axis=1)
        s_h, s_l = spread_split(terms, jnp.concatenate([me[2:3], me[5:6]], axis=1))
        gathered = dot_nt(s_h, oh_self[...]) + dot_nt(s_l, oh_self[...])

        blocks = []
        for a in range(EA):
            here = slice(a * EB, (a + 1) * EB)
            x_low, x_high = faces[0:FR, here], faces[FR : 2 * FR, here]
            y_low, y_high = faces[2 * FR : 3 * FR, here], faces[3 * FR : 4 * FR, here]
            left = x_low if a == 0 else x_low - faces[FR : 2 * FR, (a - 1) * EB : a * EB]
            right = x_high if a == EA - 1 else x_high - faces[0:FR, (a + 1) * EB : (a + 2) * EB]
            below = jnp.where(lane == 0, 0.0, pltpu.roll(y_high, 1, 1))
            above = jnp.where(lane == EB - 1, 0.0, pltpu.roll(y_low, EB - 1, 1))
            lateral = jnp.concatenate([left, right, y_low - below, y_high - above], axis=0)
            blocks.append(jnp.concatenate([PENALTY * lateral, jnp.zeros((2 * FR, EB), F32)], axis=0))
        gathered = gathered + jnp.concatenate(blocks, axis=1)

        field_h, field_l = split(field)
        both = dot(stiff_s[...], field_h)
        rest = dot(stiff_s[0 : 3 * SP, :], field_l)
        total = field
        for d in range(3):
            here = slice(d * SP, d * SP + NODES)
            again = slice((3 + d) * SP, (3 + d) * SP + NODES)
            total = total + metric_ref[d : d + 1, :] * (both[here] + both[again] + rest[here])
        return scale * total, gathered

    def side_jumps(faces):
        for side in range(2):
            d = (1, 7)[side]
            both = jnp.concatenate([own_m[d], halo_x[0, side, FACES : FACES + 8, :]], axis=1)
            oh_x[side] = one_hot(EB, code(both[1:2], both[7:8]))
        fines, coarses, subs = [], [], []
        for side in range(2):
            d = (1, 7)[side]
            theirs_m = halo_x[0, side, FACES : FACES + 8, :]
            here = slice(0, EB) if side == 0 else slice((EA - 1) * EB, EA * EB)
            pair = jnp.concatenate([faces[:, here], halo_x[0, side, 0:FACES, :]], axis=0)
            high, low = split(pair)
            got = dot(high, oh_x[side]) + dot(low, oh_x[side])
            ours, theirs = got[0:FACES], got[FACES:]
            fines += [pick_face(ours[:, 0:EB], own_m[d][2:3]), pick_face(theirs[:, EB:], theirs_m[2:3])]
            coarses += [pick_face(theirs[:, 0:EB], own_m[d][5:6]), pick_face(ours[:, EB:], theirs_m[5:6])]
            subs += [own_m[d][6:7], theirs_m[6:7]]
        jump = mortar_jump(*(jnp.concatenate(parts, axis=1) for parts in (coarses, fines, subs)))
        jump = [jump[:, k * EB : (k + 1) * EB] for k in range(4)]
        return jump, subs

    def side_adjoint(faces):
        fines, coarses, subs = [], [], []
        for side in range(2):
            d = (1, 7)[side]
            theirs_m = halo_x[0, side, FACES : FACES + 8, :]
            high, low = split(faces[:, 0:EB] if side == 0 else faces[:, (EA - 1) * EB :])
            got = dot(high, oh_x[side]) + dot(low, oh_x[side])
            fines.append(pick_face(got[:, 0:EB], own_m[d][2:3]))
            coarses.append(pick_face(got[:, EB:], theirs_m[5:6]))
            subs += [own_m[d][6:7], theirs_m[6:7]]
        fines = jnp.concatenate(fines, axis=1)
        images = mortar_jump(jnp.concatenate(coarses, axis=1), 0.0, jnp.concatenate([subs[1], subs[3]], axis=1))
        backs = mortar_back(fines, jnp.concatenate([subs[0], subs[2]], axis=1))
        against = []
        for side in range(2):
            d = (1, 7)[side]
            here = slice(side * EB, (side + 1) * EB)
            theirs_m = halo_x[0, side, FACES : FACES + 8, :]
            s_h, s_l = spread_split(
                jnp.concatenate([backs[:, here], images[:, here]], axis=1),
                jnp.concatenate([own_m[d][5:6], theirs_m[2:3]], axis=1),
            )
            against.append(dot_nt(s_h, oh_x[side]) + dot_nt(s_l, oh_x[side]))
        low_face, high_face = faces[0:FR, 0:EB], faces[FR : 2 * FR, (EA - 1) * EB :]
        against[0] = against[0] + jnp.concatenate([jnp.zeros((FR, EB), F32), low_face, jnp.zeros((4 * FR, EB), F32)], axis=0)
        against[1] = against[1] + jnp.concatenate([high_face, jnp.zeros((5 * FR, EB), F32)], axis=0)
        known = jnp.sum(fines * fines + images * images, axis=0, keepdims=True)
        return fines, images, subs, against, known[:, 0:EB] + known[:, EB:]

    def side_jumps_after(fines, images, subs):
        far_fines, far_coarses = [], []
        for side in range(2):
            d = (1, 7)[side]
            theirs_m = halo_x[0, side, FACES : FACES + 8, :]
            high, low = split(halo_x[1, side, 0:FACES, :])
            got = dot(high, oh_x[side]) + dot(low, oh_x[side])
            far_coarses.append(pick_face(got[:, 0:EB], own_m[d][5:6]))
            far_fines.append(pick_face(got[:, EB:], theirs_m[2:3]))
        out = mortar_jump(
            jnp.concatenate(far_coarses, axis=1), fines, jnp.concatenate([subs[0], subs[2]], axis=1)
        )
        into = images - jnp.concatenate(far_fines, axis=1)
        return [out[:, 0:EB], into[:, 0:EB], out[:, EB:], into[:, EB:]]

    def side_terms(t, jump, subs):
        back = mortar_back(jnp.concatenate([jump[1], jump[3]], axis=1), jnp.concatenate([subs[1], subs[3]], axis=1))
        result = []
        for side in range(2):
            d = (1, 7)[side]
            terms = jnp.concatenate(
                [-PENALTY * jump[2 * side], PENALTY * back[:, side * EB : (side + 1) * EB]], axis=1
            )
            theirs_m = halo_x[0, side, FACES : FACES + 8, :]
            s_h, s_l = spread_split(terms, jnp.concatenate([own_m[d][2:3], theirs_m[5:6]], axis=1))
            side_term = dot_nt(s_h, oh_x[side]) + dot_nt(s_l, oh_x[side])
            if side == 0:
                beside = [-PENALTY * halo_x[t, 0, FR : 2 * FR, :], jnp.zeros((5 * FR, EB), F32)]
            else:
                beside = [jnp.zeros((FR, EB), F32), -PENALTY * halo_x[t, 1, 0:FR, :], jnp.zeros((4 * FR, EB), F32)]
            result.append(side_term + jnp.concatenate(beside, axis=0))
        return result

    low_face = (lane_face == 2) & (lane_pair < 8) & ((lane_pair & 1) == 1)
    high_face = (lane_face == 3) & (lane_pair < 8) & ((lane_pair & 1) == 0)

    def edges_arrive(t):
        for index in range(6):
            if_there(EDGE_DIRS[index], lambda: y_copy(t, index, True).wait_recv())

    def sides_arrive(t):
        for side in range(2):
            if_there((1, 7)[side], lambda: x_copy(t, side, True).wait_recv())

    def edge_jumps(t, own, sum_in):
        across = edge_across(t)
        pairs = jnp.concatenate([own, across], axis=1)
        pairs_h, pairs_l = split(pairs)
        images = by_table(table_s, pairs_h, pairs_l)
        image_own = jnp.concatenate([images[s * FR : (s + 1) * FR, 0:128] for s in range(4)], axis=1)
        image_far = jnp.concatenate([images[s * FR : (s + 1) * FR, 128:] for s in range(4)], axis=1)
        far_h, far_l = split(image_far)
        on_fine = own * sum_out - dot_nt(far_h, n_out[...]) - dot_nt(far_l, n_out[...])
        jumps = image_own * sum_in - dot(pairs_h[:, 128:], n_in[...]) - dot(pairs_l[:, 128:], n_in[...])
        from_low = pltpu.roll(across, 128 - 16, 1)
        from_high = pltpu.roll(across, 16, 1)
        beside = jnp.where(low_face, from_low, jnp.where(high_face, from_high, 0.0))
        return PENALTY * (on_fine - beside), jumps

    def edge_adjoint(own, sum_in):
        own_h, own_l = split(own)
        images = by_table(table_s, own_h, own_l)
        images = jnp.concatenate([images[s * FR : (s + 1) * FR] for s in range(4)], axis=1)
        images_h, images_l = split(images)
        joined = dot(own_h, n_out[...]) + dot(own_l, n_out[...])
        joined_h, joined_l = split(jnp.concatenate([joined[:, s * 128 : (s + 1) * 128] for s in range(4)], axis=0))
        meets = by_table(table_t, joined_h, joined_l) + dot_nt(images_h, n_in[...]) + dot_nt(images_l, n_in[...])
        meets = meets + pltpu.roll(jnp.where(low_face, own, 0.0), 16, 1)
        meets = meets + pltpu.roll(jnp.where(high_face, own, 0.0), 128 - 16, 1)
        against = [pack_pairs(meets, 1), pack_pairs(meets, 0)]
        corners = pack_pairs(meets, 8)
        for c, a in enumerate(CORNER_ROWS):
            against.append(pltpu.roll(jnp.where(corner_lanes(c), corners, 0.0), 2 * (a - c) % 128, 1))
        known = jnp.sum(own * own * sum_out, axis=0, keepdims=True)
        both = jnp.sum(images * images * sum_in, axis=0, keepdims=True)
        return against, known + sum(both[:, s * 128 : (s + 1) * 128] for s in range(4))

    def edge_terms(direct, jumps):
        jumps = jnp.concatenate([jumps[:, s * 128 : (s + 1) * 128] for s in range(4)], axis=0)
        jumps_h, jumps_l = split(jumps)
        return edge_spread(direct + PENALTY * by_table(table_t, jumps_h, jumps_l))

    def placed(value):
        return face_product(place_ref[...], value)

    b = b_ref[...]
    total, gathered = local_part(b, faces)
    learn()
    total = total + placed(gathered)
    started = face_product(pick_ref[...], total)
    sides_arrive(0)
    edges_arrive(0)
    jump, subs = side_jumps(faces)
    sides = side_terms(0, jump, subs)
    n_in[...], _ = edge_counts([halo_y[0, index, 8:16, :] for index in range(6)])
    sum_in = dot(jnp.ones((16, 128), BF16), n_in[...])[0:1]
    direct, jumps = edge_jumps(0, own, sum_in)
    tiles = edge_terms(direct, jumps)
    tiles[0] = tiles[0] + sides[0]
    tiles[EA - 1] = tiles[EA - 1] + sides[1]
    remote = jnp.concatenate(tiles, axis=1)
    faces = started + face_product(mix_ref[...], remote)
    ends = publish(1, faces)
    send(1)
    learn()
    own = edge_values(ends)
    q = total + placed(remote)
    q_ref[...] = q

    total, gathered = local_part(q, faces)
    b = b_ref[...]
    q = q_ref[...]
    learn()
    early = [column_sums(b, b), column_sums(b, q), column_sums(q, q)]
    energy = column_sums(q, total) + column_sums(faces, gathered)
    fines, images, subs, side_against, known = side_adjoint(faces)
    energy = energy + PENALTY * known
    edge_against, known = edge_adjoint(own, sum_in)
    energy = energy + PENALTY * known
    sides_arrive(1)
    met = jnp.zeros((1, 128), F32)
    for side in range(2):
        met = met + jnp.sum(halo_x[1, side, 0:FACES, :] * side_against[side], axis=0, keepdims=True)
    energy = energy - PENALTY * met
    edges_arrive(1)
    met = sum(halo_y[1, index, 0:8, :] * edge_against[index] for index in range(6))
    energy = energy - PENALTY * jnp.sum(met, axis=0, keepdims=True)

    lanes = jnp.zeros((1, 128), F32)
    for index, sums in enumerate(early + [energy]):
        lanes = jnp.where(lane == index, jnp.sum(sums, axis=1, keepdims=True), lanes)
    mine0[...] = lanes
    while pending:
        learn()
    others = [(c, o) for o in [(0, 0, 0)] + chips for c in range(2) if c or o != (0, 0, 0)]
    others.sort(key=lambda t: sum((v - 1) % n for v, n in zip(t[1], (size_x, size_y, size_z))))
    for k, (flip, offset) in enumerate(others):
        where = chip(offset)
        if flip:
            core = lax.rem(gx, 2)
            where["gx"] = where["gx"] + 1 - 2 * core
        pltpu.make_async_remote_copy(
            src_ref=mine0,
            dst_ref=red1.at[pl.ds(k, 1)],
            send_sem=s1_send,
            recv_sem=s1_recv,
            device_id=where,
            device_id_type=MESH,
        ).start()

    sides = side_terms(1, side_jumps_after(fines, images, subs), subs)
    tiles = edge_terms(*edge_jumps(1, own, sum_in))
    tiles[0] = tiles[0] + sides[0]
    tiles[EA - 1] = tiles[EA - 1] + sides[1]
    w_ref[...] = total + placed(gathered + jnp.concatenate(tiles, axis=1))
    for t in range(2):
        for side in range(2):
            if_there((1, 7)[side], lambda: x_copy(t, side, False).wait_send())
        for index in range(6):
            if_there(EDGE_DIRS[index], lambda: y_copy(t, index, False).wait_send())

    pltpu.make_async_copy(red1, red1, s1_recv).wait()
    lanes = lanes + jnp.sum(red1[...], axis=0, keepdims=True)
    bb, bq, qq, qw = (lanes[:, i : i + 1] for i in range(4))
    alpha = bb / bq
    new = bb - 2.0 * alpha * bq + alpha * alpha * qq
    grow = 1.0 + new / bb
    alpha_next = new / (grow * grow * bq - 2.0 * grow * alpha * qq + alpha * alpha * qw)
    row = iota((8, 128), 0)
    coef_ref[...] = jnp.where(row == 0, alpha + alpha_next * grow, alpha * alpha_next)
    pltpu.make_async_copy(red1, red1, s1_send).wait()


def finish(coef_ref, b_ref, q_ref, w_ref, x_hbm, r_hbm, made, out_sem):
    first, second = coef_ref[0:1, 0:1], coef_ref[1:2, 0:1]
    stores = []
    for part, (start, size) in enumerate(((0, 40), (40, 56), (96, 56), (152, NODES - 152))):
        rows = pl.ds(start, size)
        b, q, w = b_ref[rows, :], q_ref[rows, :], w_ref[rows, :]
        made[0, rows, :] = first * b - second * q
        made[1, rows, :] = b - first * q + second * w
        for k, target in enumerate((x_hbm, r_hbm)):
            store = pltpu.make_async_copy(made.at[k, rows], target.at[rows], out_sem.at[part, k])
            store.start()
            stores.append(store)
    for store in stores:
        store.wait()


def body(
    n_gx,
    n_gy,
    right_side,
    stiffness,
    metric,
    levels,
    projection,
    mortar_fine,
    mortar_face,
    mortar_owner,
    mortar_subface,
    mortar_coarse,
    mortar_cface,
):
    pick, place, mix = (jnp.asarray(table, BF16) for table in constant_tables())
    field = jax.ShapeDtypeStruct(right_side.shape, F32)
    count = mortar_fine.shape[0]
    others = n_gx * n_gy - 1
    hbm = pl.BlockSpec(memory_space=pltpu.HBM)
    vmem = pl.BlockSpec(memory_space=pltpu.VMEM)
    dma = pltpu.SemaphoreType.DMA
    line = [
        entry.reshape(1, count)
        for entry in (
            mortar_fine,
            mortar_face,
            mortar_owner,
            mortar_subface,
            mortar_coarse,
            mortar_cface,
            levels,
        )
    ]
    q, w, coef = pl.pallas_call(
        functools.partial(kernel, n_gx, n_gy),
        out_shape=(field, field, jax.ShapeDtypeStruct((8, 128), F32)),
        in_specs=[hbm] * 14,
        out_specs=(vmem, vmem, vmem),
        scratch_shapes=[
            pltpu.VMEM((NODES, ELEMS), F32),
            pltpu.VMEM((3, NODES, NODES), F32),
            pltpu.VMEM((3, ELEMS), F32),
            pltpu.VMEM((7, 1, ELEMS), jnp.int32),
            pltpu.VMEM((SIDE, 4, SIDE), F32),
            pltpu.VMEM((FACES, NODES), BF16),
            pltpu.VMEM((NODES, FACES), BF16),
            pltpu.VMEM((FACES, FACES), BF16),
            pltpu.VMEM((2, 2, FACES + 8, EB), F32),
            pltpu.VMEM((2, 6, 16, 128), F32),
            pltpu.VMEM((9, 8, 128), F32),
            pltpu.VMEM((2, 2, FACES + 8, EB), F32),
            pltpu.VMEM((2, 6, 16, 128), F32),
            pltpu.VMEM((6 * SP, NODES), BF16),
            pltpu.VMEM((ELEMS, 2 * EB), BF16),
            pltpu.VMEM((2, EB, 2 * EB), BF16),
            pltpu.VMEM((128, 512), BF16),
            pltpu.VMEM((128, 512), BF16),
            pltpu.VMEM((256, 128), F32),
            pltpu.VMEM((FR, 256), F32),
            pltpu.VMEM((FR, 256), F32),
            pltpu.VMEM((others, 128), F32),
            pltpu.VMEM((1, 128), F32),
            dma((14,)),
            dma((2, 2)),
            dma((2, 2)),
            dma((2, 6)),
            dma((2, 6)),
            pltpu.SemaphoreType.REGULAR((8,)),
            dma,
            dma,
        ],
        compiler_params=pltpu.CompilerParams(
            collective_id=0, has_side_effects=True, vmem_limit_bytes=40 * 1024 * 1024
        ),
    )(
        *(
            pltpu.with_memory_space_constraint(operand, pltpu.HBM)
            for operand in (right_side, stiffness, metric, *line, projection.transpose(1, 0, 2), pick, place, mix)
        )
    )
    return pl.pallas_call(
        finish,
        out_shape=(field, field),
        in_specs=[vmem] * 4,
        out_specs=(hbm, hbm),
        scratch_shapes=[pltpu.VMEM((2, NODES, ELEMS), F32), dma((4, 2))],
        compiler_params=pltpu.CompilerParams(vmem_limit_bytes=40 * 1024 * 1024),
    )(coef, right_side, q, w)


def solution(mesh):
    columns = P(None, ("gx", "gy"))
    faces = P(("gx", "gy"))
    in_specs = (columns, P(), columns, faces, P(), faces, faces, P(("gx", "gy"), None), faces, faces, faces)
    run = functools.partial(body, mesh.shape["gx"], mesh.shape["gy"])
    return jax.shard_map(run, mesh=mesh, in_specs=in_specs, out_specs=(columns, columns), check_vma=False)
```
